32 devices in a mesh: slab: 2 (over y), vox: 8 (over z, x), ray: 2 (over core).
Axes of the slice: x: 2, y: 2, z: 4, core: 2. Of those that a mesh axis runs over, the one named last changes fastest.
Arguments:
- volume: float32 [256, 4, 128], P(('slab', 'vox', 'ray')), parts along dimension 0, may hold values from 0 to 1
- tiles: bfloat16 [16, 2, 48, 128, 128], P(('slab', 'vox'), 'ray'), parts along dimension 0, may hold values from 0 to 0.015625
- tile_row: int32 [16, 2, 48], P(('slab', 'vox'), 'ray'), parts along dimension 0, may hold values from 0 to 7
- tile_col: int32 [16, 2, 48], P(('slab', 'vox'), 'ray'), parts along dimension 0, may hold values from 0 to 15
- tile_count: int32 [16, 2], P(('slab', 'vox'), 'ray'), parts along dimension 0, may hold values from 12 to 48, as said below
- measured: float32 [2, 16, 4, 128], P('ray', ('slab', 'vox')), parts along dimension 1, may hold values from 0 to 48, as said below
Outputs:
- new_volume: float32 [256, 4, 128], P(('slab', 'vox', 'ray')), parts along dimension 0
- residual: bfloat16 [2, 16, 4, 128], P('ray', ('slab', 'vox')), parts along dimension 1
The draws below stay inside these ranges and needn't reach their ends.
There are 2 independent parts, one for each index of `slab`. The reference program is written for one: setup_inputs(seed, part) draws one part's arguments, and reference() takes and returns one part's arrays. A program takes and returns all parts, laid end to end along the dimension named above; each array names one. Nothing has to cross between parts.
Inputs may be any that keep to these rules, and one draw needn't show every extreme that they name: Each device uses its first tile_count slots; the most, 48, is reached by some device of every part. `measured`: recorded intensities are nonnegative.
All inputs are finite; a program needn't handle non-finite values.
Results may differ from the reference program's by a relative error of at most 0.0025.
Values may be sent and summed in bfloat16 or wider, within the bound.
No kernel may reach another device: no remote copies, remote signals or barrier semaphores. Data moves between devices by JAX's collectives and lax.ppermute only.
A program may use at most 64 MiB of HBM per device.

```python
import jax
import jax.numpy as jnp
from jax import lax

TILE = 128
INST = 4
VB = 16
RB_DEV = 1
NT = 48
RH = 8
NVB = 128
N_VOX = 8
N_RAY = 2


def draw_tile_count(key, part):
    key = jax.random.fold_in(key, 11)
    first, second = jax.random.split(key)
    counts = jax.random.randint(first, (N_VOX * N_RAY,), NT // 4, NT + 1)
    chosen = jax.random.randint(second, (), 0, N_VOX * N_RAY)
    counts = jnp.where(jnp.arange(N_VOX * N_RAY) == chosen, NT, counts)
    return counts.reshape(N_VOX, N_RAY).astype(jnp.int32)


def draw_measured(key, part):
    key = jax.random.fold_in(key, 23)
    first, second = jax.random.split(key, 2)
    scale = 0.3125 * NT / RB_DEV
    level = jax.random.uniform(first, (N_RAY, RH, INST, 1), jnp.float32, 0.0, 2.0)
    rough = jax.random.uniform(second, (N_RAY, RH, INST, TILE), jnp.float32, 0.7, 1.3)
    return (scale * level * rough).astype(jnp.float32)


def plant(drawn, rng, low, high):
    extent = drawn.shape
    place = [jax.random.randint(jax.random.fold_in(rng, axis), (), 0, extent[axis]) for axis in range(len(extent))]
    drawn = drawn.at[tuple(place)].set(low)
    longest = extent.index(max(extent))
    place[longest] = (place[longest] + 1) % extent[longest]
    return drawn.at[tuple(place)].set(high)


def block_levels(key, extent, cuts, least, top_value):
    def one(axis_at, shards_of):
        draws = jax.random.uniform(jax.random.fold_in(jax.random.fold_in(key, 6), axis_at), (shards_of,), jnp.float32, least / len(cuts), top_value / len(cuts))
        return jnp.repeat(jnp.exp(draws), extent[axis_at] // shards_of).reshape((-1,) + (1,) * (len(extent) - axis_at - 1))

    factor_of = one(*cuts[0])
    for cut in cuts[1:]:
        factor_of = factor_of * one(*cut)
    return factor_of


def setup_inputs(seed: int = 0, part: int = 0) -> dict:
    seeds = jax.random.split(jax.random.key(seed), 7)
    own_keys = jax.random.split(jax.random.fold_in(seeds[6], part), 7)
    return {
        "volume": jnp.clip(1.0 * jax.random.uniform(own_keys[0], (NVB, INST, TILE), jnp.float32) ** block_levels(own_keys[0], (NVB, INST, TILE), ((0, 16),), -0.2, 0.2), 0.0, 1.0),
        "tiles": jnp.clip(0.015625 * jax.random.uniform(own_keys[1], (N_VOX, N_RAY, NT, TILE, TILE), jnp.float32) ** block_levels(own_keys[1], (N_VOX, N_RAY, NT, TILE, TILE), ((0, 8), (1, 2)), -0.2, 0.2), 0.0, 0.015625).astype(jnp.bfloat16),
        "tile_row": plant(jax.random.randint(own_keys[2], (N_VOX, N_RAY, NT), 0, RH), jax.random.fold_in(own_keys[2], 1), 0, RH - 1).astype(jnp.int32),
        "tile_col": plant(jax.random.randint(own_keys[3], (N_VOX, N_RAY, NT), 0, VB), jax.random.fold_in(own_keys[3], 1), 0, VB - 1).astype(jnp.int32),
        "tile_count": draw_tile_count(jax.random.fold_in(jax.random.fold_in(seeds[6], part), 71), part),
        "measured": draw_measured(jax.random.fold_in(jax.random.fold_in(seeds[6], part), 71), part),
    }


def reference(volume, tiles, tile_row, tile_col, tile_count, measured):
    chans = INST + 1
    panel = volume.astype(jnp.bfloat16).astype(jnp.float32).reshape(N_VOX, VB, INST, TILE)
    panel = jnp.concatenate([panel, jnp.ones((N_VOX, VB, 1, TILE), jnp.float32)], axis=2)
    slots = jnp.arange(NT, dtype=jnp.int32)
    valid = (slots[None, None, :] < tile_count[:, :, None]).astype(jnp.float32)
    ray_ids = jnp.arange(RH, dtype=jnp.int32)
    vox_ids = jnp.arange(VB, dtype=jnp.int32)
    highest = lax.Precision.HIGHEST

    def forward(carry, index):
        block = tiles[index].astype(jnp.float32)
        picked = panel[index][tile_col[index]]
        prod = jnp.einsum('anrv,ancv->ancr', block, picked, precision=highest)
        onehot = (tile_row[index][:, :, None] == ray_ids).astype(jnp.float32) * valid[index][:, :, None]
        return carry + jnp.einsum('anb,ancr->abcr', onehot, prod, precision=highest), None

    sums, _ = lax.scan(forward, jnp.zeros((N_RAY, RH, chans, TILE), jnp.float32), jnp.arange(N_VOX, dtype=jnp.int32))
    residual = ((measured - sums[:, :, :INST]) / (sums[:, :, INST:] + 1.0)).astype(jnp.bfloat16)
    resid = jnp.concatenate([residual.astype(jnp.float32), jnp.ones((N_RAY, RH, 1, TILE), jnp.float32)], axis=2)

    def backward(index):
        block = tiles[index].astype(jnp.float32)
        picked = jax.vmap(lambda table, rows: table[rows])(resid, tile_row[index])
        back = jnp.einsum('anrv,ancr->ancv', block, picked, precision=highest)
        onehot = (tile_col[index][:, :, None] == vox_ids).astype(jnp.float32) * valid[index][:, :, None]
        return jnp.einsum('anb,ancv->bcv', onehot, back, precision=highest)

    bsum = lax.map(backward, jnp.arange(N_VOX, dtype=jnp.int32)).reshape(NVB, chans, TILE)
    new_volume = jnp.maximum(volume + bsum[:, :INST] / (bsum[:, INST:] + 1.0), 0.0)
    return new_volume, residual
```

```python
import jax
import jax.numpy as jnp
from jax import lax
from jax.sharding import PartitionSpec as P


def exchange(value, axis, mask):
    size = lax.axis_size(axis)
    return lax.ppermute(value, axis, [(i, i ^ mask) for i in range(size)])


def radices_of(size, most):
    out = []
    while size > 1:
        radix = min(size, most)
        out.append(radix)
        size //= radix
    return out


def all_sum(value, axis, most):
    stride = 1
    for radix in radices_of(lax.axis_size(axis), most):
        terms = [value] + [exchange(value, axis, stride * k) for k in range(1, radix)]
        while len(terms) > 1:
            terms = [a + b for a, b in zip(terms[::2], terms[1::2])]
        value = terms[0]
        stride *= radix
    return value


def on_device(volume, tiles, tile_row, tile_col, tile_count, measured):
    block = tiles[0, 0]
    rows = tile_row[0, 0]
    cols = tile_col[0, 0]
    used = tile_count[0, 0]
    inst = volume.shape[1]
    width = volume.shape[2]
    half = volume.shape[0]
    slots = block.shape[0]
    highest = lax.Precision.HIGHEST
    ray = lax.axis_index("ray")
    vox = lax.axis_index("vox")
    valid = jnp.arange(slots, dtype=jnp.int32) < used
    ones = jnp.ones((slots, 1, width), jnp.bfloat16)

    own = volume.astype(jnp.bfloat16)
    other = exchange(own, "ray", 1)
    place = jnp.where(ray == 0, cols, lax.rem(cols + half, 2 * half))
    panel = jnp.concatenate([own, other], axis=0)
    picked = jnp.concatenate([panel[place], ones], axis=1)
    prod = jnp.einsum("nrv,ncv->ncr", block, picked, preferred_element_type=jnp.float32)
    blocks = jnp.arange(lax.axis_size("vox"), dtype=jnp.int32)
    onehot = ((rows[:, None] == blocks[None, :]) & valid[:, None]).astype(jnp.float32)
    sums = jnp.einsum("nb,ncr->bcr", onehot, prod, precision=highest)
    mine = (blocks == vox)[:, None, None]
    part = jnp.concatenate([jnp.where(mine, measured[0], 0.0) - sums[:, :inst], sums[:, inst:]], axis=1)
    total = all_sum(part, "vox", 8)
    residual = (total[:, :inst] / (total[:, inst:] + 1.0)).astype(jnp.bfloat16)
    own_res = lax.dynamic_slice_in_dim(residual, vox, 1, 0)
    gathered = jnp.concatenate([residual[rows], ones], axis=1)
    back = jnp.einsum("nrv,ncr->ncv", block, gathered, preferred_element_type=jnp.float32)
    blocks = jnp.arange(2 * half, dtype=jnp.int32)
    onehot = ((place[:, None] == blocks[None, :]) & valid[:, None]).astype(jnp.float32)
    bsum = jnp.einsum("nb,ncv->bcv", onehot, back, precision=highest)
    there = exchange(bsum[half:].astype(jnp.bfloat16), "ray", 1)
    bsum = bsum[:half] + there.astype(jnp.float32)
    new_volume = jnp.maximum(volume + bsum[:, :inst] / (bsum[:, inst:] + 1.0), 0.0)
    return (new_volume, own_res[None])


def solution(mesh):
    in_specs = (
        P(("slab", "vox", "ray"), None, None),
        P(("slab", "vox"), "ray", None, None, None),
        P(("slab", "vox"), "ray", None),
        P(("slab", "vox"), "ray", None),
        P(("slab", "vox"), "ray"),
        P("ray", ("slab", "vox"), None, None),
    )
    out_specs = (P(("slab", "vox", "ray"), None, None), P("ray", ("slab", "vox"), None, None))
    return jax.shard_map(
        on_device, mesh=mesh, in_specs=in_specs, out_specs=out_specs, check_vma=False
    )
```

```python
import jax
import jax.numpy as jnp
from jax import lax
from jax.sharding import PartitionSpec as P


def exchange(value, axis, mask):
    size = lax.axis_size(axis)
    return lax.ppermute(value, axis, [(i, i ^ mask) for i in range(size)])


def on_device(volume, tiles, tile_row, tile_col, tile_count, measured):
    block = tiles[0, 0]
    rows = tile_row[0, 0]
    cols = tile_col[0, 0]
    used = tile_count[0, 0]
    inst = volume.shape[1]
    width = volume.shape[2]
    half = volume.shape[0]
    slots = block.shape[0]
    highest = lax.Precision.HIGHEST
    ray = lax.axis_index("ray")
    valid = jnp.arange(slots, dtype=jnp.int32) < used
    ones = jnp.ones((slots, 1, width), jnp.bfloat16)

    own = volume.astype(jnp.bfloat16)
    other = exchange(own, "ray", 1)
    place = jnp.where(ray == 0, cols, lax.rem(cols + half, 2 * half))
    panel = jnp.concatenate([own, other], axis=0)
    picked = jnp.concatenate([panel[place], ones], axis=1)
    prod = jnp.einsum("nrv,ncv->ncr", block, picked, preferred_element_type=jnp.float32)
    blocks = jnp.arange(lax.axis_size("vox"), dtype=jnp.int32)
    onehot = ((rows[:, None] == blocks[None, :]) & valid[:, None]).astype(jnp.float32)
    sums = jnp.einsum("nb,ncr->bcr", onehot, prod, precision=highest)
    sums = jnp.sum(lax.all_to_all(sums, "vox", 0, 0, tiled=True), axis=0, keepdims=True)
    own_res = ((measured[0] - sums[:, :inst]) / (sums[:, inst:] + 1.0)).astype(jnp.bfloat16)
    copies = jnp.broadcast_to(own_res, (blocks.shape[0],) + own_res.shape[1:])
    residual = lax.all_to_all(copies, "vox", 0, 0, tiled=True)
    gathered = jnp.concatenate([residual[rows], ones], axis=1)
    back = jnp.einsum("nrv,ncr->ncv", block, gathered, preferred_element_type=jnp.float32)
    blocks = jnp.arange(2 * half, dtype=jnp.int32)
    onehot = ((place[:, None] == blocks[None, :]) & valid[:, None]).astype(jnp.float32)
    bsum = jnp.einsum("nb,ncv->bcv", onehot, back, precision=highest)
    there = exchange(bsum[half:].astype(jnp.bfloat16), "ray", 1)
    bsum = bsum[:half] + there.astype(jnp.float32)
    new_volume = jnp.maximum(volume + bsum[:, :inst] / (bsum[:, inst:] + 1.0), 0.0)
    return (new_volume, own_res[None])


def solution(mesh):
    in_specs = (
        P(("slab", "vox", "ray"), None, None),
        P(("slab", "vox"), "ray", None, None, None),
        P(("slab", "vox"), "ray", None),
        P(("slab", "vox"), "ray", None),
        P(("slab", "vox"), "ray"),
        P("ray", ("slab", "vox"), None, None),
    )
    out_specs = (P(("slab", "vox", "ray"), None, None), P("ray", ("slab", "vox"), None, None))
    return jax.shard_map(
        on_device, mesh=mesh, in_specs=in_specs, out_specs=out_specs, check_vma=False
    )
```

```python
import jax
import jax.numpy as jnp
from jax import lax
from jax.sharding import PartitionSpec as P


def exchange(value, axis, mask):
    size = lax.axis_size(axis)
    return lax.ppermute(value, axis, [(i, i ^ mask) for i in range(size)])


def radices_of(size, most):
    out = []
    while size > 1:
        radix = min(size, most)
        out.append(radix)
        size //= radix
    return out


def all_sum(value, axis, most):
    stride = 1
    for radix in radices_of(lax.axis_size(axis), most):
        terms = [value] + [exchange(value, axis, stride * k) for k in range(1, radix)]
        while len(terms) > 1:
            terms = [a + b for a, b in zip(terms[::2], terms[1::2])]
        value = terms[0]
        stride *= radix
    return value


def on_device(volume, tiles, tile_row, tile_col, tile_count, measured):
    block = tiles[0, 0]
    rows = tile_row[0, 0]
    cols = tile_col[0, 0]
    used = tile_count[0, 0]
    inst = volume.shape[1]
    width = volume.shape[2]
    half = volume.shape[0]
    slots = block.shape[0]
    highest = lax.Precision.HIGHEST
    ray = lax.axis_index("ray")
    vox = lax.axis_index("vox")
    valid = jnp.arange(slots, dtype=jnp.int32) < used
    ones = jnp.ones((slots, 1, width), jnp.bfloat16)

    own = volume.astype(jnp.bfloat16)
    other = exchange(own, "ray", 1)
    place = jnp.where(ray == 0, cols, lax.rem(cols + half, 2 * half))
    panel = jnp.concatenate([own, other], axis=0)
    picked = jnp.concatenate([panel[place], ones], axis=1)
    prod = jnp.einsum("nrv,ncv->ncr", block, picked, preferred_element_type=jnp.float32)
    blocks = jnp.arange(lax.axis_size("vox"), dtype=jnp.int32)
    onehot = ((rows[:, None] == blocks[None, :]) & valid[:, None]).astype(jnp.float32)
    sums = jnp.einsum("nb,ncr->bcr", onehot, prod, precision=highest)
    mine = (blocks == vox)[:, None, None]
    part = jnp.concatenate([jnp.where(mine, measured[0], 0.0) - sums[:, :inst], sums[:, inst:]], axis=1)
    total = all_sum(part, "vox", 2)
    residual = (total[:, :inst] / (total[:, inst:] + 1.0)).astype(jnp.bfloat16)
    own_res = lax.dynamic_slice_in_dim(residual, vox, 1, 0)
    gathered = jnp.concatenate([residual[rows], ones], axis=1)
    back = jnp.einsum("nrv,ncr->ncv", block, gathered, preferred_element_type=jnp.float32)
    blocks = jnp.arange(2 * half, dtype=jnp.int32)
    onehot = ((place[:, None] == blocks[None, :]) & valid[:, None]).astype(jnp.float32)
    bsum = jnp.einsum("nb,ncv->bcv", onehot, back, precision=highest)
    there = exchange(bsum[half:].astype(jnp.bfloat16), "ray", 1)
    bsum = bsum[:half] + there.astype(jnp.float32)
    new_volume = jnp.maximum(volume + bsum[:, :inst] / (bsum[:, inst:] + 1.0), 0.0)
    return (new_volume, own_res[None])


def solution(mesh):
    in_specs = (
        P(("slab", "vox", "ray"), None, None),
        P(("slab", "vox"), "ray", None, None, None),
        P(("slab", "vox"), "ray", None),
        P(("slab", "vox"), "ray", None),
        P(("slab", "vox"), "ray"),
        P("ray", ("slab", "vox"), None, None),
    )
    out_specs = (P(("slab", "vox", "ray"), None, None), P("ray", ("slab", "vox"), None, None))
    return jax.shard_map(
        on_device, mesh=mesh, in_specs=in_specs, out_specs=out_specs, check_vma=False
    )
```

```python
import jax
import jax.numpy as jnp
from jax import lax
from jax.sharding import PartitionSpec as P


def exchange(value, axis, mask):
    size = lax.axis_size(axis)
    return lax.ppermute(value, axis, [(i, i ^ mask) for i in range(size)])


def radices_of(size, first):
    out = []
    while size > 1:
        radix = min(size, 4 if out else first)
        out.append(radix)
        size //= radix
    return out


def all_sum(value, axis, first):
    stride = 1
    for radix in radices_of(lax.axis_size(axis), first):
        terms = [value] + [exchange(value, axis, stride * k) for k in range(1, radix)]
        while len(terms) > 1:
            terms = [a + b for a, b in zip(terms[::2], terms[1::2])]
        value = terms[0]
        stride *= radix
    return value


def on_device(volume, tiles, tile_row, tile_col, tile_count, measured):
    block = tiles[0, 0]
    rows = tile_row[0, 0]
    cols = tile_col[0, 0]
    used = tile_count[0, 0]
    inst = volume.shape[1]
    width = volume.shape[2]
    half = volume.shape[0]
    slots = block.shape[0]
    highest = lax.Precision.HIGHEST
    ray = lax.axis_index("ray")
    vox = lax.axis_index("vox")
    valid = jnp.arange(slots, dtype=jnp.int32) < used
    ones = jnp.ones((slots, 1, width), jnp.bfloat16)

    own = volume.astype(jnp.bfloat16)
    other = exchange(own, "ray", 1)
    place = jnp.where(ray == 0, cols, lax.rem(cols + half, 2 * half))
    panel = jnp.concatenate([own, other], axis=0)
    picked = jnp.concatenate([panel[place], ones], axis=1)
    prod = jnp.einsum("nrv,ncv->ncr", block, picked, preferred_element_type=jnp.float32)
    blocks = jnp.arange(lax.axis_size("vox"), dtype=jnp.int32)
    onehot = ((rows[:, None] == blocks[None, :]) & valid[:, None]).astype(jnp.float32)
    sums = jnp.einsum("nb,ncr->bcr", onehot, prod, precision=highest)
    mine = (blocks == vox)[:, None, None]
    part = jnp.concatenate([jnp.where(mine, measured[0], 0.0) - sums[:, :inst], sums[:, inst:]], axis=1)
    total = all_sum(part, "vox", 2)
    residual = (total[:, :inst] / (total[:, inst:] + 1.0)).astype(jnp.bfloat16)
    own_res = lax.dynamic_slice_in_dim(residual, vox, 1, 0)
    gathered = jnp.concatenate([residual[rows], ones], axis=1)
    back = jnp.einsum("nrv,ncr->ncv", block, gathered, preferred_element_type=jnp.float32)
    blocks = jnp.arange(2 * half, dtype=jnp.int32)
    onehot = ((place[:, None] == blocks[None, :]) & valid[:, None]).astype(jnp.float32)
    bsum = jnp.einsum("nb,ncv->bcv", onehot, back, precision=highest)
    there = exchange(bsum[half:].astype(jnp.bfloat16), "ray", 1)
    bsum = bsum[:half] + there.astype(jnp.float32)
    new_volume = jnp.maximum(volume + bsum[:, :inst] / (bsum[:, inst:] + 1.0), 0.0)
    return (new_volume, own_res[None])


def solution(mesh):
    in_specs = (
        P(("slab", "vox", "ray"), None, None),
        P(("slab", "vox"), "ray", None, None, None),
        P(("slab", "vox"), "ray", None),
        P(("slab", "vox"), "ray", None),
        P(("slab", "vox"), "ray"),
        P("ray", ("slab", "vox"), None, None),
    )
    out_specs = (P(("slab", "vox", "ray"), None, None), P("ray", ("slab", "vox"), None, None))
    return jax.shard_map(
        on_device, mesh=mesh, in_specs=in_specs, out_specs=out_specs, check_vma=False
    )
```

```python
import jax
import jax.numpy as jnp
from jax import lax
from jax.experimental import pallas as pl
from jax.experimental.pallas import tpu as pltpu
from jax.sharding import PartitionSpec as P

SUB = 8
BANKS = 4


def exchange(value, axis, mask):
    size = lax.axis_size(axis)
    return lax.ppermute(value, axis, [(i, i ^ mask) for i in range(size)])


def all_sum(value, axis):
    stride = 1
    while stride < lax.axis_size(axis):
        value = value + exchange(value, axis, stride)
        stride *= 2
    return value


def rows_of(index):
    return pl.ds(pl.multiple_of(index * SUB, SUB), SUB)


def apply_tiles(tiles, take, put, count, table, banks, contract):
    used = count[0, 0]
    for n in range(tiles.shape[2]):
        left = jnp.where(n < used, table[rows_of(take[0, 0, n]), :], 0.0).astype(jnp.bfloat16)
        prod = lax.dot_general(
            left, tiles[0, 0, n], (((1,), (contract,)), ((), ())), preferred_element_type=jnp.float32
        )
        banks[n % BANKS, rows_of(put[0, 0, n]), :] += prod


def front_kernel(tiles, rows, cols, count, own, other, measured, part, table, banks):
    half, inst, width = own.shape
    blocks = part.shape[1]
    ray = lax.axis_index("ray")
    vox = lax.axis_index("vox")
    filler = (lax.broadcasted_iota(jnp.int32, (SUB, width), 0) == inst).astype(jnp.float32)
    banks[...] = jnp.zeros_like(banks)
    for b in range(half):
        for ref, first in ((own, ray * half), (other, (1 - ray) * half)):
            table[rows_of(first + b), :] = filler
            table[pl.ds(pl.multiple_of((first + b) * SUB, SUB), inst), :] = ref[b]
    banks[0, pl.ds(pl.multiple_of(vox * SUB, SUB), inst), :] = -measured[0, 0]
    apply_tiles(tiles, cols, rows, count, table, banks, 1)
    for c in range(inst + 1):
        total = banks[0, pl.ds(c, blocks, stride=SUB), :]
        for k in range(1, BANKS):
            total = total + banks[k, pl.ds(c, blocks, stride=SUB), :]
        part[c] = total if c == inst else -total


def back_kernel(tiles, rows, cols, count, total, own, send, residual, table, banks):
    inst = total.shape[0] - 1
    blocks, width = total.shape[1:]
    half = own.shape[0] // SUB
    ray = lax.axis_index("ray")
    vox = lax.axis_index("vox")
    banks[...] = jnp.zeros_like(banks)
    weight = total[inst] + 1.0
    for c in range(SUB):
        if c < inst:
            row = (total[c] / weight).astype(jnp.bfloat16).astype(jnp.float32)
        else:
            row = jnp.full((blocks, width), 1.0 if c == inst else 0.0, jnp.float32)
        table[pl.ds(c, blocks, stride=SUB), :] = row
    residual[...] = table[rows_of(vox), :]
    apply_tiles(tiles, rows, cols, count, table, banks, 0)
    mine = pl.ds(pl.multiple_of(ray * half * SUB, SUB), half * SUB)
    theirs = pl.ds(pl.multiple_of((1 - ray) * half * SUB, SUB), half * SUB)
    own[...] = sum(banks[k, mine, :] for k in range(BANKS))
    send[...] = sum(banks[k, theirs, :] for k in range(BANKS)).astype(jnp.bfloat16)


def end_kernel(volume, own, there, residual, new_volume, own_residual):
    half, inst, _ = volume.shape
    sums = own[...] + there[...].astype(jnp.float32)
    for b in range(half):
        both = sums[b * SUB : (b + 1) * SUB]
        step = both[:inst] / (both[inst : inst + 1] + 1.0)
        new_volume[b] = jnp.maximum(volume[b] + step, 0.0)
    own_residual[0, 0] = residual[:inst, :].astype(jnp.bfloat16)


def on_device(volume, tiles, tile_row, tile_col, tile_count, measured):
    half, inst, width = volume.shape
    blocks = measured.shape[1] * lax.axis_size("vox")
    vmem = pl.BlockSpec(memory_space=pltpu.VMEM)
    smem = pl.BlockSpec(memory_space=pltpu.SMEM)
    slots = [vmem, smem, smem, smem]

    other = exchange(volume, "ray", 1)
    part = pl.pallas_call(
        front_kernel,
        out_shape=jax.ShapeDtypeStruct((inst + 1, blocks, width), jnp.float32),
        in_specs=slots + [vmem] * 3,
        out_specs=vmem,
        scratch_shapes=[
            pltpu.VMEM((2 * half * SUB, width), jnp.float32),
            pltpu.VMEM((BANKS, blocks * SUB, width), jnp.float32),
        ],
        name="project",
    )(tiles, tile_row, tile_col, tile_count, volume, other, measured)
    total = all_sum(part, "vox")
    own, send, residual = pl.pallas_call(
        back_kernel,
        out_shape=[
            jax.ShapeDtypeStruct((half * SUB, width), jnp.float32),
            jax.ShapeDtypeStruct((half * SUB, width), jnp.bfloat16),
            jax.ShapeDtypeStruct((SUB, width), jnp.float32),
        ],
        in_specs=slots + [vmem],
        out_specs=[vmem] * 3,
        scratch_shapes=[
            pltpu.VMEM((blocks * SUB, width), jnp.float32),
            pltpu.VMEM((BANKS, 2 * half * SUB, width), jnp.float32),
        ],
        name="backproject",
    )(tiles, tile_row, tile_col, tile_count, total)
    there = exchange(send, "ray", 1)
    return tuple(
        pl.pallas_call(
            end_kernel,
            out_shape=[
                jax.ShapeDtypeStruct(volume.shape, jnp.float32),
                jax.ShapeDtypeStruct(measured.shape, jnp.bfloat16),
            ],
            in_specs=[vmem] * 4,
            out_specs=[vmem] * 2,
            name="update",
        )(volume, own, there, residual)
    )


def solution(mesh):
    in_specs = (
        P(("slab", "vox", "ray"), None, None),
        P(("slab", "vox"), "ray", None, None, None),
        P(("slab", "vox"), "ray", None),
        P(("slab", "vox"), "ray", None),
        P(("slab", "vox"), "ray"),
        P("ray", ("slab", "vox"), None, None),
    )
    out_specs = (P(("slab", "vox", "ray"), None, None), P("ray", ("slab", "vox"), None, None))
    return jax.shard_map(
        on_device, mesh=mesh, in_specs=in_specs, out_specs=out_specs, check_vma=False
    )
```

```python
import jax
import jax.numpy as jnp
from jax import lax
from jax.experimental import pallas as pl
from jax.experimental.pallas import tpu as pltpu
from jax.sharding import PartitionSpec as P

SUB = 8
VMEM_BYTES = 16 << 20
BANKS = 4


def exchange(value, axis, mask):
    size = lax.axis_size(axis)
    return lax.ppermute(value, axis, [(i, i ^ mask) for i in range(size)])


def all_sum(value, axis):
    stride = 1
    while stride < lax.axis_size(axis):
        value = value + exchange(value, axis, stride)
        stride *= 2
    return value


def rows_of(index):
    return pl.ds(pl.multiple_of(index * SUB, SUB), SUB)


def apply_tiles(tiles, take, put, count, table, banks, contract):
    used = count[0, 0]
    for n in range(tiles.shape[2]):
        left = jnp.where(n < used, table[rows_of(take[0, 0, n]), :], 0.0).astype(jnp.bfloat16)
        prod = lax.dot_general(
            left, tiles[0, 0, n], (((1,), (contract,)), ((), ())), preferred_element_type=jnp.float32
        )
        banks[n % BANKS, rows_of(put[0, 0, n]), :] += prod


def front_kernel(tiles, rows, cols, count, own, other, measured, part, table, banks):
    half, inst, width = own.shape
    blocks = part.shape[1]
    ray = lax.axis_index("ray")
    vox = lax.axis_index("vox")
    filler = (lax.broadcasted_iota(jnp.int32, (SUB, width), 0) == inst).astype(jnp.float32)
    banks[...] = jnp.zeros_like(banks)
    for b in range(half):
        for ref, first in ((own, ray * half), (other, (1 - ray) * half)):
            table[rows_of(first + b), :] = filler
            table[pl.ds(pl.multiple_of((first + b) * SUB, SUB), inst), :] = ref[b]
    banks[0, pl.ds(pl.multiple_of(vox * SUB, SUB), inst), :] = -measured[0, 0]
    apply_tiles(tiles, cols, rows, count, table, banks, 1)
    for c in range(inst + 1):
        total = banks[0, pl.ds(c, blocks, stride=SUB), :]
        for k in range(1, BANKS):
            total = total + banks[k, pl.ds(c, blocks, stride=SUB), :]
        part[c] = total if c == inst else -total


def back_kernel(tiles, rows, cols, count, total, own, send, residual, table, banks):
    inst = total.shape[0] - 1
    blocks, width = total.shape[1:]
    half = own.shape[0] // SUB
    ray = lax.axis_index("ray")
    vox = lax.axis_index("vox")
    banks[...] = jnp.zeros_like(banks)
    weight = total[inst] + 1.0
    for c in range(SUB):
        if c < inst:
            row = (total[c] / weight).astype(jnp.bfloat16).astype(jnp.float32)
        else:
            row = jnp.full((blocks, width), 1.0 if c == inst else 0.0, jnp.float32)
        table[pl.ds(c, blocks, stride=SUB), :] = row
    residual[...] = table[rows_of(vox), :]
    apply_tiles(tiles, rows, cols, count, table, banks, 0)
    mine = pl.ds(pl.multiple_of(ray * half * SUB, SUB), half * SUB)
    theirs = pl.ds(pl.multiple_of((1 - ray) * half * SUB, SUB), half * SUB)
    own[...] = sum(banks[k, mine, :] for k in range(BANKS))
    send[...] = sum(banks[k, theirs, :] for k in range(BANKS)).astype(jnp.bfloat16)


def end_kernel(volume, own, there, residual, new_volume, own_residual):
    half, inst, _ = volume.shape
    sums = own[...] + there[...].astype(jnp.float32)
    for b in range(half):
        both = sums[b * SUB : (b + 1) * SUB]
        step = both[:inst] / (both[inst : inst + 1] + 1.0)
        new_volume[b] = jnp.maximum(volume[b] + step, 0.0)
    own_residual[0, 0] = residual[:inst, :].astype(jnp.bfloat16)


def on_device(volume, tiles, tile_row, tile_col, tile_count, measured):
    half, inst, width = volume.shape
    blocks = measured.shape[1] * lax.axis_size("vox")
    vmem = pl.BlockSpec(memory_space=pltpu.VMEM)
    smem = pl.BlockSpec(memory_space=pltpu.SMEM)
    slots = [vmem, smem, smem, smem]

    other = exchange(volume, "ray", 1)
    part = pl.pallas_call(
        front_kernel,
        out_shape=jax.ShapeDtypeStruct((inst + 1, blocks, width), jnp.float32),
        in_specs=slots + [vmem] * 3,
        out_specs=vmem,
        scratch_shapes=[
            pltpu.VMEM((2 * half * SUB, width), jnp.float32),
            pltpu.VMEM((BANKS, blocks * SUB, width), jnp.float32),
        ],
        compiler_params=pltpu.CompilerParams(vmem_limit_bytes=VMEM_BYTES),
        name="project",
    )(tiles, tile_row, tile_col, tile_count, volume, other, measured)
    total = all_sum(part, "vox")
    own, send, residual = pl.pallas_call(
        back_kernel,
        out_shape=[
            jax.ShapeDtypeStruct((half * SUB, width), jnp.float32),
            jax.ShapeDtypeStruct((half * SUB, width), jnp.bfloat16),
            jax.ShapeDtypeStruct((SUB, width), jnp.float32),
        ],
        in_specs=slots + [vmem],
        out_specs=[vmem] * 3,
        scratch_shapes=[
            pltpu.VMEM((blocks * SUB, width), jnp.float32),
            pltpu.VMEM((BANKS, 2 * half * SUB, width), jnp.float32),
        ],
        compiler_params=pltpu.CompilerParams(vmem_limit_bytes=VMEM_BYTES),
        name="backproject",
    )(tiles, tile_row, tile_col, tile_count, total)
    there = exchange(send, "ray", 1)
    return tuple(
        pl.pallas_call(
            end_kernel,
            out_shape=[
                jax.ShapeDtypeStruct(volume.shape, jnp.float32),
                jax.ShapeDtypeStruct(measured.shape, jnp.bfloat16),
            ],
            in_specs=[vmem] * 4,
            out_specs=[vmem] * 2,
            compiler_params=pltpu.CompilerParams(vmem_limit_bytes=VMEM_BYTES),
            name="update",
        )(volume, own, there, residual)
    )


def solution(mesh):
    in_specs = (
        P(("slab", "vox", "ray"), None, None),
        P(("slab", "vox"), "ray", None, None, None),
        P(("slab", "vox"), "ray", None),
        P(("slab", "vox"), "ray", None),
        P(("slab", "vox"), "ray"),
        P("ray", ("slab", "vox"), None, None),
    )
    out_specs = (P(("slab", "vox", "ray"), None, None), P("ray", ("slab", "vox"), None, None))
    return jax.shard_map(
        on_device, mesh=mesh, in_specs=in_specs, out_specs=out_specs, check_vma=False
    )
```

```python
import jax
import jax.numpy as jnp
from jax import lax
from jax.sharding import PartitionSpec as P

SUB = 8


def exchange(value, axis, mask):
    size = lax.axis_size(axis)
    return lax.ppermute(value, axis, [(i, i ^ mask) for i in range(size)])


def all_sum(value, axis):
    stride = 1
    while stride < lax.axis_size(axis):
        value = value + exchange(value, axis, stride)
        stride *= 2
    return value


def picker(place, valid, blocks):
    row = place[:, None] * SUB + jnp.arange(SUB, dtype=jnp.int32)[None, :]
    row = jnp.where(valid[:, None], row, -1).reshape(-1)
    return (row[:, None] == jnp.arange(blocks * SUB, dtype=jnp.int32)[None, :]).astype(jnp.bfloat16)


def pick(matrix, table):
    blocks, inst, width = table.shape
    ones = jnp.ones((blocks, 1, width), jnp.bfloat16)
    zeros = jnp.zeros((blocks, SUB - inst - 1, width), jnp.bfloat16)
    table = jnp.concatenate([table, ones, zeros], axis=1).reshape(blocks * SUB, width)
    rows = jnp.dot(matrix, table, preferred_element_type=jnp.float32).astype(jnp.bfloat16)
    return rows.reshape(-1, SUB, width)[:, : inst + 1]


def block_sums(place, blocks, prod):
    onehot = (place[:, None] == jnp.arange(blocks, dtype=jnp.int32)[None, :]).astype(jnp.float32)
    return jnp.einsum("nb,ncr->bcr", onehot, prod, precision=lax.Precision.HIGHEST)


def on_device(volume, tiles, tile_row, tile_col, tile_count, measured):
    block = tiles[0, 0]
    rows = tile_row[0, 0]
    cols = tile_col[0, 0]
    used = tile_count[0, 0]
    half, inst, width = volume.shape
    ray_blocks = lax.axis_size("vox") * measured.shape[1]
    ray = lax.axis_index("ray")
    vox = lax.axis_index("vox")

    other = exchange(volume, "ray", 1)
    valid = jnp.arange(block.shape[0], dtype=jnp.int32) < used
    place = lax.rem(cols + ray * half, 2 * half)
    panel = jnp.concatenate([volume, other], axis=0).astype(jnp.bfloat16)
    picked = pick(picker(place, valid, 2 * half), panel)
    prod = jnp.einsum("nrv,ncv->ncr", block, picked, preferred_element_type=jnp.float32)
    sums = block_sums(rows, ray_blocks, prod)
    mine = (jnp.arange(ray_blocks, dtype=jnp.int32) == vox)[:, None, None]
    part = jnp.concatenate([jnp.where(mine, measured[0], 0.0) - sums[:, :inst], sums[:, inst:]], axis=1)
    total = all_sum(part, "vox")
    residual = (total[:, :inst] / (total[:, inst:] + 1.0)).astype(jnp.bfloat16)
    own_res = lax.dynamic_slice_in_dim(residual, vox, 1, 0)
    gathered = pick(picker(rows, valid, ray_blocks), residual)
    back = jnp.einsum("nrv,ncr->ncv", block, gathered, preferred_element_type=jnp.float32)
    bsum = block_sums(place, 2 * half, back)
    there = exchange(bsum[half:].astype(jnp.bfloat16), "ray", 1)
    bsum = bsum[:half] + there.astype(jnp.float32)
    new_volume = jnp.maximum(volume + bsum[:, :inst] / (bsum[:, inst:] + 1.0), 0.0)
    return (new_volume, own_res[None])


def solution(mesh):
    in_specs = (
        P(("slab", "vox", "ray"), None, None),
        P(("slab", "vox"), "ray", None, None, None),
        P(("slab", "vox"), "ray", None),
        P(("slab", "vox"), "ray", None),
        P(("slab", "vox"), "ray"),
        P("ray", ("slab", "vox"), None, None),
    )
    out_specs = (P(("slab", "vox", "ray"), None, None), P("ray", ("slab", "vox"), None, None))
    return jax.shard_map(
        on_device, mesh=mesh, in_specs=in_specs, out_specs=out_specs, check_vma=False
    )
```

```python
import jax
import jax.numpy as jnp
from jax import lax
from jax.sharding import PartitionSpec as P

SUB = 8


def exchange(value, axis, mask):
    size = lax.axis_size(axis)
    return lax.ppermute(value, axis, [(i, i ^ mask) for i in range(size)])


def all_sum(value, axis):
    stride = 1
    while stride < lax.axis_size(axis):
        value = value + exchange(value, axis, stride)
        stride *= 2
    return value


def picker(place, valid, blocks):
    row = place[:, None] * SUB + jnp.arange(SUB, dtype=jnp.int32)[None, :]
    row = jnp.where(valid[:, None], row, -1).reshape(-1)
    return (row[:, None] == jnp.arange(blocks * SUB, dtype=jnp.int32)[None, :]).astype(jnp.bfloat16)


def pick(matrix, table):
    blocks, inst, width = table.shape
    ones = jnp.ones((blocks, 1, width), jnp.bfloat16)
    zeros = jnp.zeros((blocks, SUB - inst - 1, width), jnp.bfloat16)
    table = jnp.concatenate([table, ones, zeros], axis=1).reshape(blocks * SUB, width)
    rows = jnp.dot(matrix, table, preferred_element_type=jnp.float32).astype(jnp.bfloat16)
    return rows.reshape(-1, SUB, width)[:, : inst + 1]


def block_sums(place, blocks, prod):
    onehot = (place[:, None] == jnp.arange(blocks, dtype=jnp.int32)[None, :]).astype(jnp.float32)
    return jnp.einsum("nb,ncr->bcr", onehot, prod, precision=lax.Precision.HIGHEST)


def on_device(volume, tiles, tile_row, tile_col, tile_count, measured):
    block = tiles[0, 0]
    rows = tile_row[0, 0]
    cols = tile_col[0, 0]
    used = tile_count[0, 0]
    half, inst, width = volume.shape
    ray_blocks = lax.axis_size("vox") * measured.shape[1]
    ray = lax.axis_index("ray")
    vox = lax.axis_index("vox")

    other = lax.optimization_barrier(exchange(volume, "ray", 1))
    valid = jnp.arange(block.shape[0], dtype=jnp.int32) < used
    place = lax.rem(cols + ray * half, 2 * half)
    panel = jnp.concatenate([volume, other], axis=0).astype(jnp.bfloat16)
    picked = pick(picker(place, valid, 2 * half), panel)
    prod = jnp.einsum("nrv,ncv->ncr", block, picked, preferred_element_type=jnp.float32)
    sums = block_sums(rows, ray_blocks, prod)
    mine = (jnp.arange(ray_blocks, dtype=jnp.int32) == vox)[:, None, None]
    part = jnp.concatenate([jnp.where(mine, measured[0], 0.0) - sums[:, :inst], sums[:, inst:]], axis=1)
    total = all_sum(part, "vox")
    residual = (total[:, :inst] / (total[:, inst:] + 1.0)).astype(jnp.bfloat16)
    own_res = lax.dynamic_slice_in_dim(residual, vox, 1, 0)
    gathered = pick(picker(rows, valid, ray_blocks), residual)
    back = jnp.einsum("nrv,ncr->ncv", block, gathered, preferred_element_type=jnp.float32)
    bsum = block_sums(place, 2 * half, back)
    there = exchange(bsum[half:].astype(jnp.bfloat16), "ray", 1)
    bsum = bsum[:half] + there.astype(jnp.float32)
    new_volume = jnp.maximum(volume + bsum[:, :inst] / (bsum[:, inst:] + 1.0), 0.0)
    return (new_volume, own_res[None])


def solution(mesh):
    in_specs = (
        P(("slab", "vox", "ray"), None, None),
        P(("slab", "vox"), "ray", None, None, None),
        P(("slab", "vox"), "ray", None),
        P(("slab", "vox"), "ray", None),
        P(("slab", "vox"), "ray"),
        P("ray", ("slab", "vox"), None, None),
    )
    out_specs = (P(("slab", "vox", "ray"), None, None), P("ray", ("slab", "vox"), None, None))
    return jax.shard_map(
        on_device, mesh=mesh, in_specs=in_specs, out_specs=out_specs, check_vma=False
    )
```

```python
import jax
import jax.numpy as jnp
from jax import lax
from jax.sharding import PartitionSpec as P

SUB = 8


def exchange(value, axis, mask):
    size = lax.axis_size(axis)
    return lax.ppermute(value, axis, [(i, i ^ mask) for i in range(size)])


def all_sum(value, axis):
    size = lax.axis_size(axis)
    stride = 1
    while stride < size:
        if 2 * stride < size:
            across = exchange(value, axis, stride)
            both = exchange(value, axis, 3 * stride)
            along = exchange(value, axis, 2 * stride)
            value = (value + across) + (along + both)
        else:
            value = value + exchange(value, axis, stride)
        stride *= 4
    return value


def picker(place, valid, blocks):
    row = place[:, None] * SUB + jnp.arange(SUB, dtype=jnp.int32)[None, :]
    row = jnp.where(valid[:, None], row, -1).reshape(-1)
    return (row[:, None] == jnp.arange(blocks * SUB, dtype=jnp.int32)[None, :]).astype(jnp.bfloat16)


def pick(matrix, table):
    blocks, inst, width = table.shape
    ones = jnp.ones((blocks, 1, width), jnp.bfloat16)
    zeros = jnp.zeros((blocks, SUB - inst - 1, width), jnp.bfloat16)
    table = jnp.concatenate([table, ones, zeros], axis=1).reshape(blocks * SUB, width)
    rows = jnp.dot(matrix, table, preferred_element_type=jnp.float32).astype(jnp.bfloat16)
    return rows.reshape(-1, SUB, width)[:, : inst + 1]


def block_sums(place, blocks, prod):
    onehot = (place[:, None] == jnp.arange(blocks, dtype=jnp.int32)[None, :]).astype(jnp.float32)
    return jnp.einsum("nb,ncr->bcr", onehot, prod, precision=lax.Precision.HIGHEST)


def on_device(volume, tiles, tile_row, tile_col, tile_count, measured):
    block = tiles[0, 0]
    rows = tile_row[0, 0]
    cols = tile_col[0, 0]
    used = tile_count[0, 0]
    half, inst, width = volume.shape
    ray_blocks = lax.axis_size("vox") * measured.shape[1]
    ray = lax.axis_index("ray")
    vox = lax.axis_index("vox")

    other = exchange(volume, "ray", 1)
    valid = jnp.arange(block.shape[0], dtype=jnp.int32) < used
    place = lax.rem(cols + ray * half, 2 * half)
    panel = jnp.concatenate([volume, other], axis=0).astype(jnp.bfloat16)
    picked = pick(picker(place, valid, 2 * half), panel)
    prod = jnp.einsum("nrv,ncv->ncr", block, picked, preferred_element_type=jnp.float32)
    sums = block_sums(rows, ray_blocks, prod)
    mine = (jnp.arange(ray_blocks, dtype=jnp.int32) == vox)[:, None, None]
    part = jnp.concatenate([jnp.where(mine, measured[0], 0.0) - sums[:, :inst], sums[:, inst:]], axis=1)
    total = all_sum(part, "vox")
    residual = (total[:, :inst] / (total[:, inst:] + 1.0)).astype(jnp.bfloat16)
    own_res = lax.dynamic_slice_in_dim(residual, vox, 1, 0)
    gathered = pick(picker(rows, valid, ray_blocks), residual)
    back = jnp.einsum("nrv,ncr->ncv", block, gathered, preferred_element_type=jnp.float32)
    bsum = block_sums(place, 2 * half, back)
    there = exchange(bsum[half:].astype(jnp.bfloat16), "ray", 1)
    bsum = bsum[:half] + there.astype(jnp.float32)
    new_volume = jnp.maximum(volume + bsum[:, :inst] / (bsum[:, inst:] + 1.0), 0.0)
    return (new_volume, own_res[None])


def solution(mesh):
    in_specs = (
        P(("slab", "vox", "ray"), None, None),
        P(("slab", "vox"), "ray", None, None, None),
        P(("slab", "vox"), "ray", None),
        P(("slab", "vox"), "ray", None),
        P(("slab", "vox"), "ray"),
        P("ray", ("slab", "vox"), None, None),
    )
    out_specs = (P(("slab", "vox", "ray"), None, None), P("ray", ("slab", "vox"), None, None))
    return jax.shard_map(
        on_device, mesh=mesh, in_specs=in_specs, out_specs=out_specs, check_vma=False
    )
```

```python
import jax
import jax.numpy as jnp
from jax import lax
from jax.experimental import pallas as pl
from jax.experimental.pallas import tpu as pltpu
from jax.sharding import PartitionSpec as P

SUB = 8
VMEM_BYTES = 16 << 20


def exchange(value, axis, mask):
    size = lax.axis_size(axis)
    return lax.ppermute(value, axis, [(i, i ^ mask) for i in range(size)])


def all_sum(value, axis):
    size = lax.axis_size(axis)
    stride = 1
    while stride < size:
        if 2 * stride < size:
            across = exchange(value, axis, stride)
            both = exchange(value, axis, 3 * stride)
            along = exchange(value, axis, 2 * stride)
            value = (value + across) + (along + both)
        else:
            value = value + exchange(value, axis, stride)
        stride *= 4
    return value


def pick_rows(key, blocks):
    shape = (SUB, blocks * SUB)
    lane = lax.broadcasted_iota(jnp.int32, shape, 1)
    same = lane % SUB == lax.broadcasted_iota(jnp.int32, shape, 0)
    block = jnp.where(same, lane // SUB, -2)
    hits = [(block == key[:, n : n + 1]).astype(jnp.float32) for n in range(key.shape[1])]
    return jnp.concatenate(hits, axis=0).astype(jnp.bfloat16)


def blocks_of(values):
    inst, width = values[0].shape
    row = lax.broadcasted_iota(jnp.int32, (SUB - inst, width), 0)
    rest = (row == 0).astype(jnp.float32)
    return jnp.concatenate([x for value in values for x in (value, rest)], axis=0).astype(jnp.bfloat16)


def load_kernel(tiles, volume, measured, rows, cols, count, *refs):
    tiles_out, volume_out, measured_out, table, pick, pick_back, add, add_back = refs[:8]
    rows_in, cols_in, sems = refs[8:]
    pairs = (
        (rows, rows_in),
        (cols, cols_in),
        (volume, volume_out),
        (measured, measured_out),
        (tiles, tiles_out),
    )
    copies = [pltpu.make_async_copy(a, b, sems.at[i]) for i, (a, b) in enumerate(pairs)]
    for copy in copies:
        copy.start()
    for copy in copies[:3]:
        copy.wait()
    half = volume.shape[0]
    slots = rows.shape[2]
    valid = lax.broadcasted_iota(jnp.int32, (1, slots), 1) < count[0, 0]
    place = cols_in[0] + lax.axis_index("ray") * half
    place = jnp.where(place < 2 * half, place, place - 2 * half)
    place = jnp.where(valid, place, -1)
    row = jnp.where(valid, rows_in[0], -1)
    for out, key in ((add, row), (add_back, place)):
        out[...] = (lax.broadcasted_iota(jnp.int32, out.shape, 0) == key).astype(jnp.float32)
    pick[...] = pick_rows(place, 2 * half)
    pick_back[...] = pick_rows(row, add.shape[0])
    table[...] = blocks_of([volume_out[b] for b in range(half)])
    for copy in copies[3:]:
        copy.wait()


def apply_tiles(picked, tiles, contract, add, prods):
    slots = tiles.shape[2]
    width = picked.shape[1]
    for n in range(slots):
        prods[pl.ds(n, SUB, stride=slots), :] = lax.dot_general(
            picked[n * SUB : (n + 1) * SUB].astype(jnp.bfloat16),
            tiles[0, 0, n],
            (((1,), (contract,)), ((), ())),
            preferred_element_type=jnp.float32,
        )
    kinds = prods.shape[0] // slots
    left = jnp.concatenate([prods[c * slots : (c + 1) * slots, :] for c in range(kinds)], axis=1)
    sums = None
    for _ in range(3):
        piece = left.astype(jnp.bfloat16)
        left = left - piece.astype(jnp.float32)
        term = jnp.dot(add[...].astype(jnp.bfloat16), piece, preferred_element_type=jnp.float32)
        sums = term if sums is None else sums + term
    return [sums[:, c * width : (c + 1) * width] for c in range(kinds)]


def project_kernel(tiles, table, pick, add, measured, other, part, prods):
    half, inst, _ = other.shape
    blocks = add.shape[0]
    panel = jnp.concatenate([table[...], blocks_of([other[b] for b in range(half)])], axis=0)
    picked = jnp.dot(pick[...], panel, preferred_element_type=jnp.float32)
    sums = apply_tiles(picked, tiles, 1, add, prods)
    mine = lax.broadcasted_iota(jnp.int32, sums[0].shape, 0) == lax.axis_index("vox")
    for c in range(inst):
        row = jnp.broadcast_to(measured[0, 0, c : c + 1, :], sums[c].shape)
        part[c * blocks : (c + 1) * blocks, :] = jnp.where(mine, row, 0.0) - sums[c]
    part[inst * blocks : (inst + 1) * blocks, :] = sums[inst]


def backproject_kernel(tiles, pick, add, total, own, send, residual, table, prods, mixed):
    blocks = pick.shape[1] // SUB
    inst = total.shape[0] // blocks - 1
    half = add.shape[0] // 2
    weight = total[inst * blocks : (inst + 1) * blocks, :] + 1.0
    for c in range(SUB):
        if c < inst:
            row = (total[c * blocks : (c + 1) * blocks, :] / weight).astype(jnp.bfloat16).astype(jnp.float32)
        else:
            row = jnp.full(weight.shape, 1.0 if c == inst else 0.0, jnp.float32)
        table[pl.ds(c, blocks, stride=SUB), :] = row
    residual[...] = table[pl.ds(pl.multiple_of(lax.axis_index("vox") * SUB, SUB), SUB), :]
    picked = jnp.dot(pick[...], table[...].astype(jnp.bfloat16), preferred_element_type=jnp.float32)
    sums = apply_tiles(picked, tiles, 0, add, prods)
    for c in range(SUB):
        own[pl.ds(c, half, stride=SUB), :] = sums[c][:half]
        mixed[pl.ds(c, half, stride=SUB), :] = sums[c][half:]
    send[...] = mixed[...].astype(jnp.bfloat16)


def update_kernel(volume, own, there, residual, new_volume, own_residual):
    half, inst, _ = volume.shape
    sums = own[...] + there[...].astype(jnp.float32)
    for b in range(half):
        both = sums[b * SUB : (b + 1) * SUB]
        step = both[:inst] / (both[inst : inst + 1] + 1.0)
        new_volume[b] = jnp.maximum(volume[b] + step, 0.0)
    own_residual[0, 0] = residual[:inst, :].astype(jnp.bfloat16)


def on_device(volume, tiles, tile_row, tile_col, tile_count, measured):
    half, inst, width = volume.shape
    slots = tiles.shape[2]
    blocks = lax.axis_size("vox") * measured.shape[1]
    f32, bf16 = jnp.float32, jnp.bfloat16
    vmem = pl.BlockSpec(memory_space=pltpu.VMEM)
    load_specs = [pl.BlockSpec(memory_space=pltpu.HBM)] * 5 + [pl.BlockSpec(memory_space=pltpu.SMEM)]
    params = pltpu.CompilerParams(vmem_limit_bytes=VMEM_BYTES)

    def call(kernel, name, outs, scratch, args, specs=None, cost=None):
        return pl.pallas_call(
            kernel,
            out_shape=[jax.ShapeDtypeStruct(shape, dtype) for shape, dtype in outs],
            in_specs=specs or [vmem] * len(args),
            out_specs=[vmem] * len(outs),
            scratch_shapes=scratch,
            compiler_params=params,
            cost_estimate=cost,
            name=name,
        )(*args)

    other = exchange(volume, "ray", 1)
    args = [pltpu.with_memory_space_constraint(x, pltpu.HBM) for x in (tiles, volume, measured, tile_row, tile_col)]
    ints = [pltpu.VMEM(x.shape, x.dtype) for x in (tile_row, tile_col)]
    tiles, volume, measured, table, pick, pick_back, add, add_back = call(
        load_kernel,
        "load",
        [
            (tiles.shape, bf16),
            (volume.shape, f32),
            (measured.shape, f32),
            ((half * SUB, width), bf16),
            ((slots * SUB, 2 * half * SUB), bf16),
            ((slots * SUB, blocks * SUB), bf16),
            ((blocks, slots), f32),
            ((2 * half, slots), f32),
        ],
        ints + [pltpu.SemaphoreType.DMA((len(args),))],
        args + [tile_count],
        specs=load_specs,
        cost=pl.CostEstimate(flops=0, bytes_accessed=4 * tiles.size, transcendentals=0),
    )
    prods = pltpu.VMEM((slots * SUB, width), f32)
    (part,) = call(
        project_kernel,
        "project",
        [(((inst + 1) * blocks, width), f32)],
        [prods],
        [tiles, table, pick, add, measured, other],
    )
    total = all_sum(part, "vox")
    flat = (half * SUB, width)
    own, send, residual = call(
        backproject_kernel,
        "backproject",
        [(flat, f32), (flat, bf16), ((SUB, width), f32)],
        [pltpu.VMEM((blocks * SUB, width), f32), prods, pltpu.VMEM(flat, f32)],
        [tiles, pick_back, add_back, total],
    )
    there = exchange(send, "ray", 1)
    return tuple(
        call(
            update_kernel,
            "update",
            [(volume.shape, f32), ((1, 1, inst, width), bf16)],
            [],
            [volume, own, there, residual],
        )
    )


def solution(mesh):
    in_specs = (
        P(("slab", "vox", "ray"), None, None),
        P(("slab", "vox"), "ray", None, None, None),
        P(("slab", "vox"), "ray", None),
        P(("slab", "vox"), "ray", None),
        P(("slab", "vox"), "ray"),
        P("ray", ("slab", "vox"), None, None),
    )
    out_specs = (P(("slab", "vox", "ray"), None, None), P("ray", ("slab", "vox"), None, None))
    return jax.shard_map(
        on_device, mesh=mesh, in_specs=in_specs, out_specs=out_specs, check_vma=False
    )
```

```python
import jax
import jax.numpy as jnp
from jax import lax
from jax.experimental import pallas as pl
from jax.experimental.pallas import tpu as pltpu
from jax.sharding import PartitionSpec as P

SUB = 8
VMEM_BYTES = 16 << 20


def exchange(value, axis, mask):
    size = lax.axis_size(axis)
    return lax.ppermute(value, axis, [(i, i ^ mask) for i in range(size)])


def all_sum(value, axis):
    size = lax.axis_size(axis)
    stride = 1
    while stride < size:
        if 2 * stride < size:
            across = exchange(value, axis, stride)
            both = exchange(value, axis, 3 * stride)
            along = exchange(value, axis, 2 * stride)
            value = (value + across) + (along + both)
        else:
            value = value + exchange(value, axis, stride)
        stride *= 4
    return value


def load_kernel(tiles, volume, measured, rows, cols, count, *refs):
    tiles_out, volume_out, measured_out, add, add_back, rows_in, cols_in, sems = refs
    pairs = (
        (rows, rows_in),
        (cols, cols_in),
        (tiles, tiles_out),
        (volume, volume_out),
        (measured, measured_out),
    )
    copies = [pltpu.make_async_copy(a, b, sems.at[i]) for i, (a, b) in enumerate(pairs)]
    for copy in copies:
        copy.start()
    for copy in copies[:2]:
        copy.wait()
    blocks = add_back.shape[0]
    valid = lax.broadcasted_iota(jnp.int32, (1, rows.shape[2]), 1) < count[0, 0]
    place = cols_in[0] + lax.axis_index("ray") * (blocks // 2)
    place = jnp.where(place < blocks, place, place - blocks)
    for out, key in ((add, rows_in[0]), (add_back, place)):
        hit = (lax.broadcasted_iota(jnp.int32, out.shape, 0) == key) & valid
        out[...] = hit.astype(jnp.float32)
    for copy in copies[2:]:
        copy.wait()


def slot_rows(which, table, picked):
    slots, width = which.shape[1], table[0].shape[1]
    rows = lax.dot_general(
        which[...].astype(jnp.bfloat16),
        jnp.concatenate(table, axis=1).astype(jnp.bfloat16),
        (((0,), (0,)), ((), ())),
        preferred_element_type=jnp.float32,
    )
    for c in range(len(table)):
        picked[pl.ds(c, slots, stride=SUB), :] = rows[:, c * width : (c + 1) * width]
    picked[pl.ds(len(table), slots, stride=SUB), :] = jnp.ones((slots, width), jnp.float32)


def apply_tiles(picked, tiles, contract, add, prods, kinds):
    slots = tiles.shape[2]
    width = picked.shape[1]
    for n in range(slots):
        prods[pl.ds(n, SUB, stride=slots), :] = lax.dot_general(
            picked[n * SUB : (n + 1) * SUB, :].astype(jnp.bfloat16),
            tiles[0, 0, n],
            (((1,), (contract,)), ((), ())),
            preferred_element_type=jnp.float32,
        )
    left = jnp.concatenate([prods[c * slots : (c + 1) * slots, :] for c in range(kinds)], axis=1)
    onehot = add[...].astype(jnp.bfloat16)
    sums = None
    for _ in range(3):
        piece = left.astype(jnp.bfloat16)
        left = left - piece.astype(jnp.float32)
        term = jnp.dot(onehot, piece, preferred_element_type=jnp.float32)
        sums = term if sums is None else sums + term
    return [sums[:, c * width : (c + 1) * width] for c in range(kinds)]


def project_kernel(tiles, add, add_back, volume, other, measured, part, picked, prods):
    blocks = add.shape[0]
    half = add_back.shape[0] // 2
    inst = measured.shape[2]
    rows = [pl.ds(c, half, stride=inst) for c in range(inst)]
    table = [jnp.concatenate([volume[row, :], other[row, :]], axis=0) for row in rows]
    slot_rows(add_back, table, picked)
    sums = apply_tiles(picked, tiles, 1, add, prods, inst + 1)
    mine = lax.broadcasted_iota(jnp.int32, sums[0].shape, 0) == lax.axis_index("vox")
    for c in range(inst):
        row = jnp.broadcast_to(measured[0, 0, c : c + 1, :], sums[c].shape)
        part[c * blocks : (c + 1) * blocks, :] = jnp.where(mine, row, 0.0) - sums[c]
    part[inst * blocks : (inst + 1) * blocks, :] = sums[inst]


def backproject_kernel(tiles, add, add_back, total, own, send, residual, picked, prods):
    blocks = add.shape[0]
    half = add_back.shape[0] // 2
    inst = residual.shape[0]
    rows = [total[c * blocks : (c + 1) * blocks, :] for c in range(inst + 1)]
    weight = rows[inst] + 1.0
    table = [(row / weight).astype(jnp.bfloat16).astype(jnp.float32) for row in rows[:inst]]
    mine = lax.broadcasted_iota(jnp.int32, weight.shape, 0) == lax.axis_index("vox")
    for c in range(inst):
        residual[c : c + 1, :] = jnp.sum(jnp.where(mine, table[c], 0.0), axis=0, keepdims=True)
    slot_rows(add, table, picked)
    sums = apply_tiles(picked, tiles, 0, add_back, prods, inst + 1)
    filler = [jnp.zeros((half, weight.shape[1]), jnp.float32)] * (SUB - inst - 1)
    own[...] = jnp.concatenate([x[:half] for x in sums], axis=0)
    send[...] = jnp.concatenate([x[half:] for x in sums] + filler, axis=0).astype(jnp.bfloat16)


def update_kernel(volume, own, there, residual, new_volume, own_residual):
    inst = residual.shape[0]
    half = volume.shape[0] // inst
    both = own[...] + there[...].astype(jnp.float32)[: own.shape[0]]
    weight = both[inst * half :] + 1.0
    for c in range(inst):
        row = pl.ds(c, half, stride=inst)
        new_volume[row, :] = jnp.maximum(volume[row, :] + both[c * half : (c + 1) * half] / weight, 0.0)
    own_residual[0, 0] = residual[...].astype(jnp.bfloat16)


def on_device(volume, tiles, tile_row, tile_col, tile_count, measured):
    half, inst, width = volume.shape
    slots = tiles.shape[2]
    blocks = lax.axis_size("vox") * measured.shape[1]
    f32, bf16 = jnp.float32, jnp.bfloat16
    vmem = pl.BlockSpec(memory_space=pltpu.VMEM)
    load_specs = [pl.BlockSpec(memory_space=pltpu.HBM)] * 5 + [pl.BlockSpec(memory_space=pltpu.SMEM)]
    params = pltpu.CompilerParams(vmem_limit_bytes=VMEM_BYTES)

    def call(kernel, name, outs, scratch, args, specs=None, cost=None):
        return pl.pallas_call(
            kernel,
            out_shape=[jax.ShapeDtypeStruct(shape, dtype) for shape, dtype in outs],
            in_specs=specs or [vmem] * len(args),
            out_specs=[vmem] * len(outs),
            scratch_shapes=scratch,
            compiler_params=params,
            cost_estimate=cost,
            name=name,
        )(*args)

    volume = volume.reshape(half * inst, width)
    other = exchange(volume, "ray", 1)
    args = [pltpu.with_memory_space_constraint(x, pltpu.HBM) for x in (tiles, volume, measured, tile_row, tile_col)]
    ints = [pltpu.VMEM(x.shape, x.dtype) for x in (tile_row, tile_col)]
    tiles, volume, measured, add, add_back = call(
        load_kernel,
        "load",
        [
            (tiles.shape, bf16),
            (volume.shape, f32),
            (measured.shape, f32),
            ((blocks, slots), f32),
            ((2 * half, slots), f32),
        ],
        ints + [pltpu.SemaphoreType.DMA((len(args),))],
        args + [tile_count],
        specs=load_specs,
        cost=pl.CostEstimate(flops=0, bytes_accessed=4 * tiles.size, transcendentals=0),
    )
    scratch = [pltpu.VMEM((slots * SUB, width), f32)] * 2
    (part,) = call(
        project_kernel,
        "project",
        [(((inst + 1) * blocks, width), f32)],
        scratch,
        [tiles, add, add_back, volume, other, measured],
    )
    total = all_sum(part, "vox")
    own, send, residual = call(
        backproject_kernel,
        "backproject",
        [(((inst + 1) * half, width), f32), ((SUB * half, width), bf16), ((inst, width), f32)],
        scratch,
        [tiles, add, add_back, total],
    )
    there = exchange(send, "ray", 1)
    new_volume, own_residual = call(
        update_kernel,
        "update",
        [(volume.shape, f32), ((1, 1, inst, width), bf16)],
        [],
        [volume, own, there, residual],
    )
    return new_volume.reshape(half, inst, width), own_residual


def solution(mesh):
    in_specs = (
        P(("slab", "vox", "ray"), None, None),
        P(("slab", "vox"), "ray", None, None, None),
        P(("slab", "vox"), "ray", None),
        P(("slab", "vox"), "ray", None),
        P(("slab", "vox"), "ray"),
        P("ray", ("slab", "vox"), None, None),
    )
    out_specs = (P(("slab", "vox", "ray"), None, None), P("ray", ("slab", "vox"), None, None))
    return jax.shard_map(
        on_device, mesh=mesh, in_specs=in_specs, out_specs=out_specs, check_vma=False
    )
```

```python
import jax
import jax.numpy as jnp
from jax import lax
from jax.experimental import pallas as pl
from jax.experimental.pallas import tpu as pltpu
from jax.sharding import PartitionSpec as P

SUB = 8
TILE_COPIES = 6
VMEM_BYTES = 16 << 20


def exchange(value, axis, mask):
    size = lax.axis_size(axis)
    return lax.ppermute(value, axis, [(i, i ^ mask) for i in range(size)])


def all_sum(value, axis):
    size = lax.axis_size(axis)
    stride = 1
    while stride < size:
        if 2 * stride < size:
            across = exchange(value, axis, stride)
            both = exchange(value, axis, 3 * stride)
            along = exchange(value, axis, 2 * stride)
            value = (value + across) + (along + both)
        else:
            value = value + exchange(value, axis, stride)
        stride *= 4
    return value


def load_kernel(tiles, volume, measured, rows, cols, count, *refs):
    tiles_out, volume_out, measured_out, add, add_back, rows_in, cols_in, sems = refs
    step = tiles.shape[2] // TILE_COPIES
    parts = [pl.ds(i * step, step) for i in range(TILE_COPIES)]
    pairs = [(rows, rows_in), (cols, cols_in), (volume, volume_out), (measured, measured_out)]
    pairs += [(tiles.at[0, 0, part], tiles_out.at[0, 0, part]) for part in parts]
    copies = [pltpu.make_async_copy(a, b, sems.at[i]) for i, (a, b) in enumerate(pairs)]
    for copy in copies:
        copy.start()
    for copy in copies[:2]:
        copy.wait()
    blocks = add_back.shape[0]
    valid = lax.broadcasted_iota(jnp.int32, (1, rows.shape[2]), 1) < count[0, 0]
    place = cols_in[0] + lax.axis_index("ray") * (blocks // 2)
    place = jnp.where(place < blocks, place, place - blocks)
    for out, key in ((add, rows_in[0]), (add_back, place)):
        hit = (lax.broadcasted_iota(jnp.int32, out.shape, 0) == key) & valid
        out[...] = hit.astype(jnp.float32)
    for copy in copies[2:]:
        copy.wait()


def slot_rows(which, table, picked):
    slots, width = which.shape[1], table[0].shape[1]
    rows = lax.dot_general(
        which[...].astype(jnp.bfloat16),
        jnp.concatenate(table, axis=1).astype(jnp.bfloat16),
        (((0,), (0,)), ((), ())),
        preferred_element_type=jnp.float32,
    )
    for c in range(len(table)):
        picked[pl.ds(c, slots, stride=SUB), :] = rows[:, c * width : (c + 1) * width]
    picked[pl.ds(len(table), slots, stride=SUB), :] = jnp.ones((slots, width), jnp.float32)


def apply_tiles(picked, tiles, contract, add, prods, kinds):
    slots = tiles.shape[2]
    width = picked.shape[1]
    for n in range(slots):
        prods[pl.ds(n, SUB, stride=slots), :] = lax.dot_general(
            picked[n * SUB : (n + 1) * SUB, :].astype(jnp.bfloat16),
            tiles[0, 0, n],
            (((1,), (contract,)), ((), ())),
            preferred_element_type=jnp.float32,
        )
    left = jnp.concatenate([prods[c * slots : (c + 1) * slots, :] for c in range(kinds)], axis=1)
    onehot = add[...].astype(jnp.bfloat16)
    sums = None
    for _ in range(3):
        piece = left.astype(jnp.bfloat16)
        left = left - piece.astype(jnp.float32)
        term = jnp.dot(onehot, piece, preferred_element_type=jnp.float32)
        sums = term if sums is None else sums + term
    return [sums[:, c * width : (c + 1) * width] for c in range(kinds)]


def project_kernel(tiles, add, add_back, volume, other, measured, part, picked, prods):
    blocks = add.shape[0]
    half = add_back.shape[0] // 2
    inst = measured.shape[2]
    rows = [pl.ds(c, half, stride=inst) for c in range(inst)]
    table = [jnp.concatenate([volume[row, :], other[row, :]], axis=0) for row in rows]
    slot_rows(add_back, table, picked)
    sums = apply_tiles(picked, tiles, 1, add, prods, inst + 1)
    mine = lax.broadcasted_iota(jnp.int32, sums[0].shape, 0) == lax.axis_index("vox")
    for c in range(inst):
        row = jnp.broadcast_to(measured[0, 0, c : c + 1, :], sums[c].shape)
        part[c * blocks : (c + 1) * blocks, :] = jnp.where(mine, row, 0.0) - sums[c]
    part[inst * blocks : (inst + 1) * blocks, :] = sums[inst]


def backproject_kernel(tiles, add, add_back, total, own, send, residual, picked, prods):
    blocks = add.shape[0]
    half = add_back.shape[0] // 2
    inst = residual.shape[0]
    rows = [total[c * blocks : (c + 1) * blocks, :] for c in range(inst + 1)]
    weight = rows[inst] + 1.0
    table = [(row / weight).astype(jnp.bfloat16).astype(jnp.float32) for row in rows[:inst]]
    mine = lax.broadcasted_iota(jnp.int32, weight.shape, 0) == lax.axis_index("vox")
    for c in range(inst):
        residual[c : c + 1, :] = jnp.sum(jnp.where(mine, table[c], 0.0), axis=0, keepdims=True)
    slot_rows(add, table, picked)
    sums = apply_tiles(picked, tiles, 0, add_back, prods, inst + 1)
    filler = [jnp.zeros((half, weight.shape[1]), jnp.float32)] * (SUB - inst - 1)
    own[...] = jnp.concatenate([x[:half] for x in sums], axis=0)
    send[...] = jnp.concatenate([x[half:] for x in sums] + filler, axis=0).astype(jnp.bfloat16)


def update_kernel(volume, own, there, residual, new_volume, own_residual):
    inst = residual.shape[0]
    half = volume.shape[0] // inst
    both = own[...] + there[...].astype(jnp.float32)[: own.shape[0]]
    weight = both[inst * half :] + 1.0
    for c in range(inst):
        row = pl.ds(c, half, stride=inst)
        new_volume[row, :] = jnp.maximum(volume[row, :] + both[c * half : (c + 1) * half] / weight, 0.0)
    own_residual[0, 0] = residual[...].astype(jnp.bfloat16)


def on_device(volume, tiles, tile_row, tile_col, tile_count, measured):
    half, inst, width = volume.shape
    slots = tiles.shape[2]
    blocks = lax.axis_size("vox") * measured.shape[1]
    f32, bf16 = jnp.float32, jnp.bfloat16
    vmem = pl.BlockSpec(memory_space=pltpu.VMEM)
    load_specs = [pl.BlockSpec(memory_space=pltpu.HBM)] * 5 + [pl.BlockSpec(memory_space=pltpu.SMEM)]
    params = pltpu.CompilerParams(vmem_limit_bytes=VMEM_BYTES)

    def call(kernel, name, outs, scratch, args, specs=None, cost=None):
        return pl.pallas_call(
            kernel,
            out_shape=[jax.ShapeDtypeStruct(shape, dtype) for shape, dtype in outs],
            in_specs=specs or [vmem] * len(args),
            out_specs=[vmem] * len(outs),
            scratch_shapes=scratch,
            compiler_params=params,
            cost_estimate=cost,
            name=name,
        )(*args)

    volume = volume.reshape(half * inst, width)
    other = exchange(volume, "ray", 1)
    args = [pltpu.with_memory_space_constraint(x, pltpu.HBM) for x in (tiles, volume, measured, tile_row, tile_col)]
    ints = [pltpu.VMEM(x.shape, x.dtype) for x in (tile_row, tile_col)]
    tiles, volume, measured, add, add_back = call(
        load_kernel,
        "load",
        [
            (tiles.shape, bf16),
            (volume.shape, f32),
            (measured.shape, f32),
            ((blocks, slots), f32),
            ((2 * half, slots), f32),
        ],
        ints + [pltpu.SemaphoreType.DMA((len(args) - 1 + TILE_COPIES,))],
        args + [tile_count],
        specs=load_specs,
        cost=pl.CostEstimate(flops=0, bytes_accessed=4 * tiles.size, transcendentals=0),
    )
    scratch = [pltpu.VMEM((slots * SUB, width), f32)] * 2
    (part,) = call(
        project_kernel,
        "project",
        [(((inst + 1) * blocks, width), f32)],
        scratch,
        [tiles, add, add_back, volume, other, measured],
    )
    total = all_sum(part, "vox")
    own, send, residual = call(
        backproject_kernel,
        "backproject",
        [(((inst + 1) * half, width), f32), ((SUB * half, width), bf16), ((inst, width), f32)],
        scratch,
        [tiles, add, add_back, total],
    )
    there = exchange(send, "ray", 1)
    new_volume, own_residual = call(
        update_kernel,
        "update",
        [(volume.shape, f32), ((1, 1, inst, width), bf16)],
        [],
        [volume, own, there, residual],
    )
    return new_volume.reshape(half, inst, width), own_residual


def solution(mesh):
    in_specs = (
        P(("slab", "vox", "ray"), None, None),
        P(("slab", "vox"), "ray", None, None, None),
        P(("slab", "vox"), "ray", None),
        P(("slab", "vox"), "ray", None),
        P(("slab", "vox"), "ray"),
        P("ray", ("slab", "vox"), None, None),
    )
    out_specs = (P(("slab", "vox", "ray"), None, None), P("ray", ("slab", "vox"), None, None))
    return jax.shard_map(
        on_device, mesh=mesh, in_specs=in_specs, out_specs=out_specs, check_vma=False
    )
```

```python
import jax
import jax.numpy as jnp
from jax import lax
from jax.experimental import pallas as pl
from jax.experimental.pallas import tpu as pltpu
from jax.sharding import PartitionSpec as P

SUB = 8
LOAD_FLOPS = 20_000_000_000
VMEM_BYTES = 16 << 20


def exchange(value, axis, mask):
    size = lax.axis_size(axis)
    return lax.ppermute(value, axis, [(i, i ^ mask) for i in range(size)])


def all_sum(value, axis):
    size = lax.axis_size(axis)
    stride = 1
    while stride < size:
        if 2 * stride < size:
            across = exchange(value, axis, stride)
            both = exchange(value, axis, 3 * stride)
            along = exchange(value, axis, 2 * stride)
            value = (value + across) + (along + both)
        else:
            value = value + exchange(value, axis, stride)
        stride *= 4
    return value


def load_kernel(volume, measured, rows, cols, *refs):
    volume_out, measured_out, add, add_back, rows_in, cols_in, sems = refs
    pairs = (
        (rows, rows_in),
        (cols, cols_in),
        (volume, volume_out),
        (measured, measured_out),
    )
    copies = [pltpu.make_async_copy(a, b, sems.at[i]) for i, (a, b) in enumerate(pairs)]
    for copy in copies:
        copy.start()
    for copy in copies[:2]:
        copy.wait()
    blocks = add_back.shape[0]
    place = cols_in[0] + lax.axis_index("ray") * (blocks // 2)
    place = jnp.where(place < blocks, place, place - blocks)
    for out, key in ((add, rows_in[0]), (add_back, place)):
        out[...] = (lax.broadcasted_iota(jnp.int32, out.shape, 0) == key).astype(jnp.float32)
    for copy in copies[2:]:
        copy.wait()


def slot_rows(which, table, picked):
    slots, width = which.shape[1], table[0].shape[1]
    rows = lax.dot_general(
        which[...].astype(jnp.bfloat16),
        jnp.concatenate(table, axis=1).astype(jnp.bfloat16),
        (((0,), (0,)), ((), ())),
        preferred_element_type=jnp.float32,
    )
    for c in range(len(table)):
        picked[pl.ds(c, slots, stride=SUB), :] = rows[:, c * width : (c + 1) * width]
    picked[pl.ds(len(table), slots, stride=SUB), :] = jnp.ones((slots, width), jnp.float32)


def apply_tiles(picked, tiles, contract, add, count, prods, kinds):
    slots = tiles.shape[2]
    width = picked.shape[1]
    for n in range(slots):
        prods[pl.ds(n, SUB, stride=slots), :] = lax.dot_general(
            picked[n * SUB : (n + 1) * SUB, :].astype(jnp.bfloat16),
            tiles[0, 0, n],
            (((1,), (contract,)), ((), ())),
            preferred_element_type=jnp.float32,
        )
    left = jnp.concatenate([prods[c * slots : (c + 1) * slots, :] for c in range(kinds)], axis=1)
    used = lax.broadcasted_iota(jnp.int32, add.shape, 1) < count[0, 0]
    onehot = jnp.where(used, add[...], 0.0).astype(jnp.bfloat16)
    sums = None
    for _ in range(3):
        piece = left.astype(jnp.bfloat16)
        left = left - piece.astype(jnp.float32)
        term = jnp.dot(onehot, piece, preferred_element_type=jnp.float32)
        sums = term if sums is None else sums + term
    return [sums[:, c * width : (c + 1) * width] for c in range(kinds)]


def project_kernel(count, tiles, add, add_back, volume, other, measured, part, picked, prods):
    blocks = add.shape[0]
    half = add_back.shape[0] // 2
    inst = measured.shape[2]
    rows = [pl.ds(c, half, stride=inst) for c in range(inst)]
    table = [jnp.concatenate([volume[row, :], other[row, :]], axis=0) for row in rows]
    slot_rows(add_back, table, picked)
    sums = apply_tiles(picked, tiles, 1, add, count, prods, inst + 1)
    mine = lax.broadcasted_iota(jnp.int32, sums[0].shape, 0) == lax.axis_index("vox")
    for c in range(inst):
        row = jnp.broadcast_to(measured[0, 0, c : c + 1, :], sums[c].shape)
        part[c * blocks : (c + 1) * blocks, :] = jnp.where(mine, row, 0.0) - sums[c]
    part[inst * blocks : (inst + 1) * blocks, :] = sums[inst]


def backproject_kernel(count, tiles, add, add_back, total, own, send, residual, picked, prods):
    blocks = add.shape[0]
    half = add_back.shape[0] // 2
    inst = residual.shape[0]
    rows = [total[c * blocks : (c + 1) * blocks, :] for c in range(inst + 1)]
    weight = rows[inst] + 1.0
    table = [(row / weight).astype(jnp.bfloat16).astype(jnp.float32) for row in rows[:inst]]
    mine = lax.broadcasted_iota(jnp.int32, weight.shape, 0) == lax.axis_index("vox")
    for c in range(inst):
        residual[c : c + 1, :] = jnp.sum(jnp.where(mine, table[c], 0.0), axis=0, keepdims=True)
    slot_rows(add, table, picked)
    sums = apply_tiles(picked, tiles, 0, add_back, count, prods, inst + 1)
    filler = [jnp.zeros((half, weight.shape[1]), jnp.float32)] * (SUB - inst - 1)
    own[...] = jnp.concatenate([x[:half] for x in sums], axis=0)
    send[...] = jnp.concatenate([x[half:] for x in sums] + filler, axis=0).astype(jnp.bfloat16)


def update_kernel(volume, own, there, residual, new_volume, own_residual):
    inst = residual.shape[0]
    half = volume.shape[0] // inst
    both = own[...] + there[...].astype(jnp.float32)[: own.shape[0]]
    weight = both[inst * half :] + 1.0
    for c in range(inst):
        row = pl.ds(c, half, stride=inst)
        new_volume[row, :] = jnp.maximum(volume[row, :] + both[c * half : (c + 1) * half] / weight, 0.0)
    own_residual[0, 0] = residual[...].astype(jnp.bfloat16)


def on_device(volume, tiles, tile_row, tile_col, tile_count, measured):
    half, inst, width = volume.shape
    slots = tiles.shape[2]
    blocks = lax.axis_size("vox") * measured.shape[1]
    f32, bf16 = jnp.float32, jnp.bfloat16
    vmem = pl.BlockSpec(memory_space=pltpu.VMEM)
    hbm = pl.BlockSpec(memory_space=pltpu.HBM)
    smem = pl.BlockSpec(memory_space=pltpu.SMEM)
    params = pltpu.CompilerParams(vmem_limit_bytes=VMEM_BYTES)

    def call(kernel, name, outs, scratch, args, specs=None, cost=None):
        return pl.pallas_call(
            kernel,
            out_shape=[jax.ShapeDtypeStruct(shape, dtype) for shape, dtype in outs],
            in_specs=specs or [vmem] * len(args),
            out_specs=[vmem] * len(outs),
            scratch_shapes=scratch,
            compiler_params=params,
            cost_estimate=cost,
            name=name,
        )(*args)

    volume = volume.reshape(half * inst, width)
    other = exchange(volume, "ray", 1)
    args = [pltpu.with_memory_space_constraint(x, pltpu.HBM) for x in (volume, measured, tile_row, tile_col)]
    ints = [pltpu.VMEM(x.shape, x.dtype) for x in (tile_row, tile_col)]
    volume, measured, add, add_back = call(
        load_kernel,
        "load",
        [
            (volume.shape, f32),
            (measured.shape, f32),
            ((blocks, slots), f32),
            ((2 * half, slots), f32),
        ],
        ints + [pltpu.SemaphoreType.DMA((len(args),))],
        args,
        specs=[hbm] * len(args),
        cost=pl.CostEstimate(flops=LOAD_FLOPS, bytes_accessed=0, transcendentals=0),
    )
    scratch = [pltpu.VMEM((slots * SUB, width), f32)] * 2
    (part,) = call(
        project_kernel,
        "project",
        [(((inst + 1) * blocks, width), f32)],
        scratch,
        [tile_count, tiles, add, add_back, volume, other, measured],
        specs=[smem] + [vmem] * 6,
    )
    total = all_sum(part, "vox")
    own, send, residual = call(
        backproject_kernel,
        "backproject",
        [(((inst + 1) * half, width), f32), ((SUB * half, width), bf16), ((inst, width), f32)],
        scratch,
        [tile_count, tiles, add, add_back, total],
        specs=[smem] + [vmem] * 4,
    )
    there = exchange(send, "ray", 1)
    new_volume, own_residual = call(
        update_kernel,
        "update",
        [(volume.shape, f32), ((1, 1, inst, width), bf16)],
        [],
        [volume, own, there, residual],
    )
    return new_volume.reshape(half, inst, width), own_residual


def solution(mesh):
    in_specs = (
        P(("slab", "vox", "ray"), None, None),
        P(("slab", "vox"), "ray", None, None, None),
        P(("slab", "vox"), "ray", None),
        P(("slab", "vox"), "ray", None),
        P(("slab", "vox"), "ray"),
        P("ray", ("slab", "vox"), None, None),
    )
    out_specs = (P(("slab", "vox", "ray"), None, None), P("ray", ("slab", "vox"), None, None))
    return jax.shard_map(
        on_device, mesh=mesh, in_specs=in_specs, out_specs=out_specs, check_vma=False
    )
```

```python
import functools

import jax
import jax.numpy as jnp
from jax import lax
from jax.experimental import pallas as pl
from jax.experimental.pallas import tpu as pltpu
from jax.sharding import PartitionSpec as P

SUB = 8
ROWS_FLOPS = 20_000_000_000
VMEM_BYTES = 16 << 20


def exchange(value, axis, mask):
    size = lax.axis_size(axis)
    return lax.ppermute(value, axis, [(i, i ^ mask) for i in range(size)])


def all_sum(value, axis):
    size = lax.axis_size(axis)
    stride = 1
    while stride < size:
        if 2 * stride < size:
            across = exchange(value, axis, stride)
            both = exchange(value, axis, 3 * stride)
            along = exchange(value, axis, 2 * stride)
            value = (value + across) + (along + both)
        else:
            value = value + exchange(value, axis, stride)
        stride *= 4
    return value


def rows_kernel(inst, picked):
    kind = lax.broadcasted_iota(jnp.int32, picked.shape, 0) % SUB
    picked[...] = (kind == inst).astype(jnp.float32)


def one_hot(key, blocks):
    return (lax.broadcasted_iota(jnp.int32, (blocks, key.shape[1]), 0) == key).astype(jnp.float32)


def places(cols, half):
    place = cols + lax.axis_index("ray") * half
    return jnp.where(place < 2 * half, place, place - 2 * half)


def slot_rows(which, table, picked):
    slots, width = which.shape[1], table[0].shape[1]
    rows = lax.dot_general(
        which.astype(jnp.bfloat16),
        jnp.concatenate(table, axis=1).astype(jnp.bfloat16),
        (((0,), (0,)), ((), ())),
        preferred_element_type=jnp.float32,
    )
    for c in range(len(table)):
        picked[pl.ds(c, slots, stride=SUB), :] = rows[:, c * width : (c + 1) * width]


def apply_tiles(picked, tiles, contract, add, count, prods, kinds):
    slots, rays, width = tiles.shape[2:]
    for n in range(0, slots, 2):
        pair = tiles[0, 0, n : n + 2]
        if contract:
            pair = pair.reshape(2 * rays, width)
        else:
            pair = jnp.concatenate([pair[0], pair[1]], axis=1)
        both = lax.dot_general(
            picked[n * SUB : (n + 2) * SUB, :].astype(jnp.bfloat16),
            pair,
            (((1,), (contract,)), ((), ())),
            preferred_element_type=jnp.float32,
        )
        prods[pl.ds(n, SUB, stride=slots), :] = both[:SUB, :width]
        prods[pl.ds(n + 1, SUB, stride=slots), :] = both[SUB:, width:]
    left = jnp.concatenate([prods[c * slots : (c + 1) * slots, :] for c in range(kinds)], axis=1)
    used = lax.broadcasted_iota(jnp.int32, add.shape, 1) < count[0, 0]
    onehot = jnp.where(used, add, 0.0).astype(jnp.bfloat16)
    sums = None
    for _ in range(3):
        piece = left.astype(jnp.bfloat16)
        left = left - piece.astype(jnp.float32)
        term = jnp.dot(onehot, piece, preferred_element_type=jnp.float32)
        sums = term if sums is None else sums + term
    return [sums[:, c * width : (c + 1) * width] for c in range(kinds)]


def project_kernel(count, tiles, rows, cols, volume, other, measured, _, part, picked, prods):
    inst = measured.shape[2]
    blocks = part.shape[0] // (inst + 1)
    half = volume.shape[0] // inst
    strides = [pl.ds(c, half, stride=inst) for c in range(inst)]
    table = [jnp.concatenate([volume[row, :], other[row, :]], axis=0) for row in strides]
    slot_rows(one_hot(places(cols[0], half), 2 * half), table, picked)
    sums = apply_tiles(picked, tiles, 1, one_hot(rows[0], blocks), count, prods, inst + 1)
    mine = lax.broadcasted_iota(jnp.int32, sums[0].shape, 0) == lax.axis_index("vox")
    for c in range(inst):
        row = jnp.broadcast_to(measured[0, 0, c : c + 1, :], sums[c].shape)
        part[c * blocks : (c + 1) * blocks, :] = jnp.where(mine, row, 0.0) - sums[c]
    part[inst * blocks : (inst + 1) * blocks, :] = sums[inst]


def backproject_kernel(count, tiles, rows, cols, total, _, own, send, residual, picked, prods):
    inst = residual.shape[0]
    blocks = total.shape[0] // (inst + 1)
    half = own.shape[0] // (inst + 1)
    kinds = [total[c * blocks : (c + 1) * blocks, :] for c in range(inst + 1)]
    weight = kinds[inst] + 1.0
    table = [(kind / weight).astype(jnp.bfloat16).astype(jnp.float32) for kind in kinds[:inst]]
    mine = lax.broadcasted_iota(jnp.int32, weight.shape, 0) == lax.axis_index("vox")
    for c in range(inst):
        residual[c : c + 1, :] = jnp.sum(jnp.where(mine, table[c], 0.0), axis=0, keepdims=True)
    slot_rows(one_hot(rows[0], blocks), table, picked)
    sums = apply_tiles(picked, tiles, 0, one_hot(places(cols[0], half), 2 * half), count, prods, inst + 1)
    filler = [jnp.zeros((half, weight.shape[1]), jnp.float32)] * (SUB - inst - 1)
    own[...] = jnp.concatenate([x[:half] for x in sums], axis=0)
    send[...] = jnp.concatenate([x[half:] for x in sums] + filler, axis=0).astype(jnp.bfloat16)


def update_kernel(volume, own, there, residual, new_volume, own_residual):
    inst = residual.shape[0]
    half = volume.shape[0] // inst
    both = own[...] + there[...].astype(jnp.float32)[: own.shape[0]]
    weight = both[inst * half :] + 1.0
    for c in range(inst):
        row = pl.ds(c, half, stride=inst)
        new_volume[row, :] = jnp.maximum(volume[row, :] + both[c * half : (c + 1) * half] / weight, 0.0)
    own_residual[0, 0] = residual[...].astype(jnp.bfloat16)


def on_device(volume, tiles, tile_row, tile_col, tile_count, measured):
    half, inst, width = volume.shape
    slots = tiles.shape[2]
    blocks = lax.axis_size("vox") * measured.shape[1]
    f32, bf16 = jnp.float32, jnp.bfloat16
    vmem = pl.BlockSpec(memory_space=pltpu.VMEM)
    smem = pl.BlockSpec(memory_space=pltpu.SMEM)
    params = pltpu.CompilerParams(vmem_limit_bytes=VMEM_BYTES)

    def call(kernel, name, outs, scratch, args, scalars=0, cost=None, aliases={}):
        return pl.pallas_call(
            kernel,
            out_shape=[jax.ShapeDtypeStruct(shape, dtype) for shape, dtype in outs],
            in_specs=[smem] * scalars + [vmem] * (len(args) - scalars),
            out_specs=[vmem] * len(outs),
            scratch_shapes=scratch,
            input_output_aliases=aliases,
            compiler_params=params,
            cost_estimate=cost,
            name=name,
        )(*args)

    volume = volume.reshape(half * inst, width)
    other = exchange(volume, "ray", 1)
    slot_shape = ((slots * SUB, width), f32)
    prods = pltpu.VMEM(*slot_shape)
    (picked,) = call(
        functools.partial(rows_kernel, inst),
        "rows",
        [slot_shape],
        [],
        [],
        cost=pl.CostEstimate(flops=ROWS_FLOPS, bytes_accessed=0, transcendentals=0),
    )
    part, picked = call(
        project_kernel,
        "project",
        [(((inst + 1) * blocks, width), f32), slot_shape],
        [prods],
        [tile_count, tiles, tile_row, tile_col, volume, other, measured, picked],
        scalars=1,
        aliases={7: 1},
    )
    total = all_sum(part, "vox")
    own, send, residual, _ = call(
        backproject_kernel,
        "backproject",
        [(((inst + 1) * half, width), f32), ((SUB * half, width), bf16), ((inst, width), f32), slot_shape],
        [prods],
        [tile_count, tiles, tile_row, tile_col, total, picked],
        scalars=1,
        aliases={5: 3},
    )
    there = exchange(send, "ray", 1)
    new_volume, own_residual = call(
        update_kernel,
        "update",
        [(volume.shape, f32), ((1, 1, inst, width), bf16)],
        [],
        [volume, own, there, residual],
    )
    return new_volume.reshape(half, inst, width), own_residual


def solution(mesh):
    in_specs = (
        P(("slab", "vox", "ray"), None, None),
        P(("slab", "vox"), "ray", None, None, None),
        P(("slab", "vox"), "ray", None),
        P(("slab", "vox"), "ray", None),
        P(("slab", "vox"), "ray"),
        P("ray", ("slab", "vox"), None, None),
    )
    out_specs = (P(("slab", "vox", "ray"), None, None), P("ray", ("slab", "vox"), None, None))
    return jax.shard_map(
        on_device, mesh=mesh, in_specs=in_specs, out_specs=out_specs, check_vma=False
    )
```

```python
import functools

import jax
import jax.numpy as jnp
from jax import lax
from jax.experimental import pallas as pl
from jax.experimental.pallas import tpu as pltpu
from jax.sharding import PartitionSpec as P

SUB = 8
HINT_FLOPS = 20_000_000_000
VMEM_BYTES = 16 << 20


def exchange(value, axis, mask, senders=None):
    size = lax.axis_size(axis)
    return lax.ppermute(value, axis, [(i, i ^ mask) for i in range(size) if senders is None or senders(i)])


def odd(i):
    return (i // 2) % 2 == 1


def even(i):
    return not odd(i)


def all_sum(value, axis, stride):
    size = lax.axis_size(axis)
    while stride < size:
        if 2 * stride < size:
            across = exchange(value, axis, stride)
            both = exchange(value, axis, 3 * stride)
            along = exchange(value, axis, 2 * stride)
            value = (value + across) + (along + both)
        else:
            value = value + exchange(value, axis, stride)
        stride *= 4
    return value


def rows_kernel(inst, picked):
    kind = lax.broadcasted_iota(jnp.int32, picked.shape, 0) % SUB
    picked[...] = (kind == inst).astype(jnp.float32)


def one_hot(key, blocks):
    return (lax.broadcasted_iota(jnp.int32, (blocks, key.shape[1]), 0) == key).astype(jnp.float32)


def places(cols, half):
    place = cols + lax.axis_index("ray") * half
    return jnp.where(place < 2 * half, place, place - 2 * half)


def slot_rows(which, table, picked):
    slots, width = which.shape[1], table[0].shape[1]
    rows = lax.dot_general(
        which.astype(jnp.bfloat16),
        jnp.concatenate(table, axis=1).astype(jnp.bfloat16),
        (((0,), (0,)), ((), ())),
        preferred_element_type=jnp.float32,
    )
    for c in range(len(table)):
        picked[pl.ds(c, slots, stride=SUB), :] = rows[:, c * width : (c + 1) * width]


def apply_tiles(picked, tiles, contract, add, count, prods, kinds):
    slots, rays, width = tiles.shape[2:]
    for n in range(0, slots, 2):
        pair = tiles[0, 0, n : n + 2]
        if contract:
            pair = pair.reshape(2 * rays, width)
        else:
            pair = jnp.concatenate([pair[0], pair[1]], axis=1)
        both = lax.dot_general(
            picked[n * SUB : (n + 2) * SUB, :].astype(jnp.bfloat16),
            pair,
            (((1,), (contract,)), ((), ())),
            preferred_element_type=jnp.float32,
        )
        prods[pl.ds(n, SUB, stride=slots), :] = both[:SUB, :width]
        prods[pl.ds(n + 1, SUB, stride=slots), :] = both[SUB:, width:]
    left = jnp.concatenate([prods[c * slots : (c + 1) * slots, :] for c in range(kinds)], axis=1)
    used = lax.broadcasted_iota(jnp.int32, add.shape, 1) < count[0, 0]
    onehot = jnp.where(used, add, 0.0).astype(jnp.bfloat16)
    sums = None
    for _ in range(3):
        piece = left.astype(jnp.bfloat16)
        left = left - piece.astype(jnp.float32)
        term = jnp.dot(onehot, piece, preferred_element_type=jnp.float32)
        sums = term if sums is None else sums + term
    return [sums[:, c * width : (c + 1) * width] for c in range(kinds)]


def project(count, tiles, rows, cols, volume, other, measured, part, picked, prods):
    inst = measured.shape[2]
    blocks = part.shape[0] // (inst + 1)
    half = volume.shape[0] // inst
    strides = [pl.ds(c, half, stride=inst) for c in range(inst)]
    table = [jnp.concatenate([volume[row, :], other[row, :]], axis=0) for row in strides]
    slot_rows(one_hot(places(cols[0], half), 2 * half), table, picked)
    sums = apply_tiles(picked, tiles, 1, one_hot(rows[0], blocks), count, prods, inst + 1)
    mine = lax.broadcasted_iota(jnp.int32, sums[0].shape, 0) == lax.axis_index("vox")
    for c in range(inst):
        row = jnp.broadcast_to(measured[0, 0, c : c + 1, :], sums[c].shape)
        part[c * blocks : (c + 1) * blocks, :] = jnp.where(mine, row, 0.0) - sums[c]
    part[inst * blocks : (inst + 1) * blocks, :] = sums[inst]


def project_odd_kernel(*refs):
    inputs, (_, part, picked, prods) = refs[:7], refs[7:]

    @pl.when(odd(lax.axis_index("vox")))
    def _():
        project(*inputs, part, picked, prods)


def project_even_kernel(*refs):
    inputs, (_, odd_part, part, picked, prods) = refs[:7], refs[7:]
    is_odd = odd(lax.axis_index("vox"))

    @pl.when(is_odd)
    def _():
        part[...] = odd_part[...]

    @pl.when(jnp.logical_not(is_odd))
    def _():
        project(*inputs, part, picked, prods)


def copy_kernel(value, out):
    out[...] = value[...]


def add_kernel(*refs):
    *values, kept, total, out = refs
    total[...] = sum(value[...] for value in values)
    out[...] = kept[...]


def backproject_kernel(count, tiles, rows, cols, total, _, own, send, residual, picked, prods):
    inst = residual.shape[0]
    blocks = total.shape[0] // (inst + 1)
    half = own.shape[0] // (inst + 1)
    kinds = [total[c * blocks : (c + 1) * blocks, :] for c in range(inst + 1)]
    weight = kinds[inst] + 1.0
    table = [(kind / weight).astype(jnp.bfloat16).astype(jnp.float32) for kind in kinds[:inst]]
    mine = lax.broadcasted_iota(jnp.int32, weight.shape, 0) == lax.axis_index("vox")
    for c in range(inst):
        residual[c : c + 1, :] = jnp.sum(jnp.where(mine, table[c], 0.0), axis=0, keepdims=True)
    slot_rows(one_hot(rows[0], blocks), table, picked)
    sums = apply_tiles(picked, tiles, 0, one_hot(places(cols[0], half), 2 * half), count, prods, inst + 1)
    filler = [jnp.zeros((half, weight.shape[1]), jnp.float32)] * (SUB - inst - 1)
    own[...] = jnp.concatenate([x[:half] for x in sums], axis=0)
    send[...] = jnp.concatenate([x[half:] for x in sums] + filler, axis=0).astype(jnp.bfloat16)


def update_kernel(volume, own, there, residual, new_volume, own_residual):
    inst = residual.shape[0]
    half = volume.shape[0] // inst
    both = own[...] + there[...].astype(jnp.float32)[: own.shape[0]]
    weight = both[inst * half :] + 1.0
    for c in range(inst):
        row = pl.ds(c, half, stride=inst)
        new_volume[row, :] = jnp.maximum(volume[row, :] + both[c * half : (c + 1) * half] / weight, 0.0)
    own_residual[0, 0] = residual[...].astype(jnp.bfloat16)


def on_device(volume, tiles, tile_row, tile_col, tile_count, measured):
    half, inst, width = volume.shape
    slots = tiles.shape[2]
    blocks = lax.axis_size("vox") * measured.shape[1]
    f32, bf16 = jnp.float32, jnp.bfloat16
    vmem = pl.BlockSpec(memory_space=pltpu.VMEM)
    smem = pl.BlockSpec(memory_space=pltpu.SMEM)
    params = pltpu.CompilerParams(vmem_limit_bytes=VMEM_BYTES)

    def call(kernel, name, outs, scratch, args, scalars=0, cost=None, aliases={}):
        return pl.pallas_call(
            kernel,
            out_shape=[jax.ShapeDtypeStruct(shape, dtype) for shape, dtype in outs],
            in_specs=[smem] * scalars + [vmem] * (len(args) - scalars),
            out_specs=[vmem] * len(outs),
            scratch_shapes=scratch,
            input_output_aliases=aliases,
            compiler_params=params,
            cost_estimate=cost,
            name=name,
        )(*args)

    hint = pl.CostEstimate(flops=HINT_FLOPS, bytes_accessed=0, transcendentals=0)
    volume = volume.reshape(half * inst, width)
    other = exchange(volume, "ray", 1)
    slot_shape = ((slots * SUB, width), f32)
    prods = pltpu.VMEM(*slot_shape)
    (picked,) = call(
        functools.partial(rows_kernel, inst),
        "rows",
        [slot_shape],
        [],
        [],
        cost=hint,
    )
    part_shape = (((inst + 1) * blocks, width), f32)
    inputs = [tile_count, tiles, tile_row, tile_col, volume, other, measured]

    def later(value):
        return call(copy_kernel, "later", [part_shape], [], [value])[0]

    odd_part, picked = call(
        project_odd_kernel,
        "project_odd",
        [part_shape, slot_shape],
        [prods],
        inputs + [picked],
        scalars=1,
        aliases={7: 1},
    )
    z_up = exchange(odd_part, "vox", 2, odd)
    xz_up = exchange(odd_part, "vox", 3, odd)
    part, picked = call(
        project_even_kernel,
        "project_even",
        [part_shape, slot_shape],
        [prods],
        inputs + [picked, odd_part],
        scalars=1,
        cost=hint,
        aliases={7: 1},
    )
    x_even = exchange(part, "vox", 1, even)
    step = later(part)
    z_down = exchange(step, "vox", 2, even)
    step = later(step)
    xz_down = exchange(step, "vox", 3, even)
    step = later(step)
    x_odd = exchange(step, "vox", 1, odd)

    def add(*values):
        return call(add_kernel, "add", [part_shape] * 2, [], values)

    along, own = add(z_up, xz_up, part)
    across, along = add(own, x_even, along)
    along, across = add(along, z_down, across)
    along, across = add(along, xz_down, across)
    total = (across + x_odd) + along
    total = all_sum(total, "vox", 4)
    own, send, residual, _ = call(
        backproject_kernel,
        "backproject",
        [(((inst + 1) * half, width), f32), ((SUB * half, width), bf16), ((inst, width), f32), slot_shape],
        [prods],
        [tile_count, tiles, tile_row, tile_col, total, picked],
        scalars=1,
        aliases={5: 3},
    )
    there = exchange(send, "ray", 1)
    new_volume, own_residual = call(
        update_kernel,
        "update",
        [(volume.shape, f32), ((1, 1, inst, width), bf16)],
        [],
        [volume, own, there, residual],
    )
    return new_volume.reshape(half, inst, width), own_residual


def solution(mesh):
    in_specs = (
        P(("slab", "vox", "ray"), None, None),
        P(("slab", "vox"), "ray", None, None, None),
        P(("slab", "vox"), "ray", None),
        P(("slab", "vox"), "ray", None),
        P(("slab", "vox"), "ray"),
        P("ray", ("slab", "vox"), None, None),
    )
    out_specs = (P(("slab", "vox", "ray"), None, None), P("ray", ("slab", "vox"), None, None))
    return jax.shard_map(
        on_device, mesh=mesh, in_specs=in_specs, out_specs=out_specs, check_vma=False
    )
```

```python
import functools

import jax
import jax.numpy as jnp
from jax import lax
from jax.experimental import pallas as pl
from jax.experimental.pallas import tpu as pltpu
from jax.sharding import PartitionSpec as P

SUB = 8
ROWS_FLOPS = 20_000_000_000
VMEM_BYTES = 16 << 20


def exchange(value, axis, mask):
    size = lax.axis_size(axis)
    return lax.ppermute(value, axis, [(i, i ^ mask) for i in range(size)])


def all_sum(value, axis):
    size = lax.axis_size(axis)
    stride = 1
    while stride < size:
        if 2 * stride < size:
            firsts = [i for i in range(size) if (i // stride) % 4 == 0]
            groups = [[i + k * stride for k in range(4)] for i in firsts]
            copies = jnp.concatenate([value] * 4, axis=0)
            got = lax.all_to_all(copies, axis, 0, 0, axis_index_groups=groups, tiled=True)
            got = got.reshape((4,) + value.shape)
            value = (got[0] + got[1]) + (got[2] + got[3])
        else:
            value = value + exchange(value, axis, stride)
        stride *= 4
    return value


def rows_kernel(inst, picked):
    kind = lax.broadcasted_iota(jnp.int32, picked.shape, 0) % SUB
    picked[...] = (kind == inst).astype(jnp.float32)


def one_hot(key, blocks):
    return (lax.broadcasted_iota(jnp.int32, (blocks, key.shape[1]), 0) == key).astype(jnp.float32)


def places(cols, half):
    place = cols + lax.axis_index("ray") * half
    return jnp.where(place < 2 * half, place, place - 2 * half)


def slot_rows(which, table, picked):
    slots, width = which.shape[1], table[0].shape[1]
    rows = lax.dot_general(
        which.astype(jnp.bfloat16),
        jnp.concatenate(table, axis=1).astype(jnp.bfloat16),
        (((0,), (0,)), ((), ())),
        preferred_element_type=jnp.float32,
    )
    for c in range(len(table)):
        picked[pl.ds(c, slots, stride=SUB), :] = rows[:, c * width : (c + 1) * width]


def apply_tiles(picked, tiles, contract, add, count, prods, kinds):
    slots, rays, width = tiles.shape[2:]
    for n in range(0, slots, 2):
        pair = tiles[0, 0, n : n + 2]
        if contract:
            pair = pair.reshape(2 * rays, width)
        else:
            pair = jnp.concatenate([pair[0], pair[1]], axis=1)
        both = lax.dot_general(
            picked[n * SUB : (n + 2) * SUB, :].astype(jnp.bfloat16),
            pair,
            (((1,), (contract,)), ((), ())),
            preferred_element_type=jnp.float32,
        )
        prods[pl.ds(n, SUB, stride=slots), :] = both[:SUB, :width]
        prods[pl.ds(n + 1, SUB, stride=slots), :] = both[SUB:, width:]
    left = jnp.concatenate([prods[c * slots : (c + 1) * slots, :] for c in range(kinds)], axis=1)
    used = lax.broadcasted_iota(jnp.int32, add.shape, 1) < count[0, 0]
    onehot = jnp.where(used, add, 0.0).astype(jnp.bfloat16)
    sums = None
    for _ in range(3):
        piece = left.astype(jnp.bfloat16)
        left = left - piece.astype(jnp.float32)
        term = jnp.dot(onehot, piece, preferred_element_type=jnp.float32)
        sums = term if sums is None else sums + term
    return [sums[:, c * width : (c + 1) * width] for c in range(kinds)]


def project_kernel(count, tiles, rows, cols, volume, other, measured, _, part, picked, prods):
    inst = measured.shape[2]
    blocks = part.shape[0] // (inst + 1)
    half = volume.shape[0] // inst
    strides = [pl.ds(c, half, stride=inst) for c in range(inst)]
    table = [jnp.concatenate([volume[row, :], other[row, :]], axis=0) for row in strides]
    slot_rows(one_hot(places(cols[0], half), 2 * half), table, picked)
    sums = apply_tiles(picked, tiles, 1, one_hot(rows[0], blocks), count, prods, inst + 1)
    mine = lax.broadcasted_iota(jnp.int32, sums[0].shape, 0) == lax.axis_index("vox")
    for c in range(inst):
        row = jnp.broadcast_to(measured[0, 0, c : c + 1, :], sums[c].shape)
        part[c * blocks : (c + 1) * blocks, :] = jnp.where(mine, row, 0.0) - sums[c]
    part[inst * blocks : (inst + 1) * blocks, :] = sums[inst]


def backproject_kernel(count, tiles, rows, cols, total, _, own, send, residual, picked, prods):
    inst = residual.shape[0]
    blocks = total.shape[0] // (inst + 1)
    half = own.shape[0] // (inst + 1)
    kinds = [total[c * blocks : (c + 1) * blocks, :] for c in range(inst + 1)]
    weight = kinds[inst] + 1.0
    table = [(kind / weight).astype(jnp.bfloat16).astype(jnp.float32) for kind in kinds[:inst]]
    mine = lax.broadcasted_iota(jnp.int32, weight.shape, 0) == lax.axis_index("vox")
    for c in range(inst):
        residual[c : c + 1, :] = jnp.sum(jnp.where(mine, table[c], 0.0), axis=0, keepdims=True)
    slot_rows(one_hot(rows[0], blocks), table, picked)
    sums = apply_tiles(picked, tiles, 0, one_hot(places(cols[0], half), 2 * half), count, prods, inst + 1)
    filler = [jnp.zeros((half, weight.shape[1]), jnp.float32)] * (SUB - inst - 1)
    own[...] = jnp.concatenate([x[:half] for x in sums], axis=0)
    send[...] = jnp.concatenate([x[half:] for x in sums] + filler, axis=0).astype(jnp.bfloat16)


def update_kernel(volume, own, there, residual, new_volume, own_residual):
    inst = residual.shape[0]
    half = volume.shape[0] // inst
    both = own[...] + there[...].astype(jnp.float32)[: own.shape[0]]
    weight = both[inst * half :] + 1.0
    for c in range(inst):
        row = pl.ds(c, half, stride=inst)
        new_volume[row, :] = jnp.maximum(volume[row, :] + both[c * half : (c + 1) * half] / weight, 0.0)
    own_residual[0, 0] = residual[...].astype(jnp.bfloat16)


def on_device(volume, tiles, tile_row, tile_col, tile_count, measured):
    half, inst, width = volume.shape
    slots = tiles.shape[2]
    blocks = lax.axis_size("vox") * measured.shape[1]
    f32, bf16 = jnp.float32, jnp.bfloat16
    vmem = pl.BlockSpec(memory_space=pltpu.VMEM)
    smem = pl.BlockSpec(memory_space=pltpu.SMEM)
    params = pltpu.CompilerParams(vmem_limit_bytes=VMEM_BYTES)

    def call(kernel, name, outs, scratch, args, scalars=0, cost=None, aliases={}):
        return pl.pallas_call(
            kernel,
            out_shape=[jax.ShapeDtypeStruct(shape, dtype) for shape, dtype in outs],
            in_specs=[smem] * scalars + [vmem] * (len(args) - scalars),
            out_specs=[vmem] * len(outs),
            scratch_shapes=scratch,
            input_output_aliases=aliases,
            compiler_params=params,
            cost_estimate=cost,
            name=name,
        )(*args)

    volume = volume.reshape(half * inst, width)
    other = exchange(volume, "ray", 1)
    slot_shape = ((slots * SUB, width), f32)
    prods = pltpu.VMEM(*slot_shape)
    (picked,) = call(
        functools.partial(rows_kernel, inst),
        "rows",
        [slot_shape],
        [],
        [],
        cost=pl.CostEstimate(flops=ROWS_FLOPS, bytes_accessed=0, transcendentals=0),
    )
    part, picked = call(
        project_kernel,
        "project",
        [(((inst + 1) * blocks, width), f32), slot_shape],
        [prods],
        [tile_count, tiles, tile_row, tile_col, volume, other, measured, picked],
        scalars=1,
        aliases={7: 1},
    )
    total = all_sum(part, "vox")
    own, send, residual, _ = call(
        backproject_kernel,
        "backproject",
        [(((inst + 1) * half, width), f32), ((SUB * half, width), bf16), ((inst, width), f32), slot_shape],
        [prods],
        [tile_count, tiles, tile_row, tile_col, total, picked],
        scalars=1,
        aliases={5: 3},
    )
    there = exchange(send, "ray", 1)
    new_volume, own_residual = call(
        update_kernel,
        "update",
        [(volume.shape, f32), ((1, 1, inst, width), bf16)],
        [],
        [volume, own, there, residual],
    )
    return new_volume.reshape(half, inst, width), own_residual


def solution(mesh):
    in_specs = (
        P(("slab", "vox", "ray"), None, None),
        P(("slab", "vox"), "ray", None, None, None),
        P(("slab", "vox"), "ray", None),
        P(("slab", "vox"), "ray", None),
        P(("slab", "vox"), "ray"),
        P("ray", ("slab", "vox"), None, None),
    )
    out_specs = (P(("slab", "vox", "ray"), None, None), P("ray", ("slab", "vox"), None, None))
    return jax.shard_map(
        on_device, mesh=mesh, in_specs=in_specs, out_specs=out_specs, check_vma=False
    )
```

```python
import functools

import jax
import jax.numpy as jnp
from jax import lax
from jax.experimental import pallas as pl
from jax.experimental.pallas import tpu as pltpu
from jax.sharding import PartitionSpec as P

SUB = 8
HINT_FLOPS = 20_000_000_000
VMEM_BYTES = 16 << 20


def exchange(value, axis, mask):
    size = lax.axis_size(axis)
    return lax.ppermute(value, axis, [(i, i ^ mask) for i in range(size)])


def all_sum(value, axis, add):
    size = lax.axis_size(axis)
    stride = 1
    while stride < size:
        if 2 * stride < size:
            across = exchange(value, axis, stride)
            both = exchange(value, axis, 3 * stride)
            along = exchange(value, axis, 2 * stride)
            value = (value + across) + add(along, both)
        else:
            value = value + exchange(value, axis, stride)
        stride *= 4
    return value


def spread_kernel(spread):
    slot = lax.broadcasted_iota(jnp.int32, spread.shape, 0)
    column = lax.broadcasted_iota(jnp.int32, spread.shape, 1)
    spread[...] = (column // SUB == slot).astype(jnp.float32)


def pick_matrix(key, blocks, kinds):
    shape = (SUB, kinds * blocks)
    lane = lax.broadcasted_iota(jnp.int32, shape, 1)
    same = lane // blocks == lax.broadcasted_iota(jnp.int32, shape, 0)
    block = jnp.where(same, lane % blocks, -2)
    hits = [(block == key[:, n : n + 1]).astype(jnp.float32) for n in range(key.shape[1])]
    return jnp.concatenate(hits, axis=0).astype(jnp.bfloat16)


def add_matrix(key, first, blocks, kinds, spread):
    hit = lax.broadcasted_iota(jnp.int32, (blocks, key.shape[1]), 0) + first == key
    hit = jnp.dot(
        hit.astype(jnp.float32).astype(jnp.bfloat16),
        spread[...].astype(jnp.bfloat16),
        preferred_element_type=jnp.float32,
    )
    kind = lax.broadcasted_iota(jnp.int32, hit.shape, 1) % SUB
    return jnp.concatenate([jnp.where(kind == c, hit, 0.0) for c in range(kinds)], axis=0)


def prepare_kernel(kinds, count, rows, cols, spread, pick, pick_back, add, add_back):
    blocks = add.shape[0] // kinds
    half = add_back.shape[0] // (2 * kinds)
    valid = lax.broadcasted_iota(jnp.int32, rows.shape[1:], 1) < count[0, 0]
    row = jnp.where(valid, rows[0], -1)
    place = cols[0] + lax.axis_index("ray") * half
    place = jnp.where(place < 2 * half, place, place - 2 * half)
    place = jnp.where(valid, place, -1)
    pick[...] = pick_matrix(place, 2 * half, kinds)
    pick_back[...] = pick_matrix(row, blocks, kinds)
    add[...] = add_matrix(row, 0, blocks, kinds, spread).astype(jnp.bfloat16)
    own = add_matrix(place, 0, half, kinds, spread)
    theirs = add_matrix(place, half, half, kinds, spread)
    add_back[...] = jnp.concatenate([own, theirs], axis=0).astype(jnp.bfloat16)


def add_kernel(left, right, out):
    out[...] = left[...] + right[...]


def apply_tiles(pick, table, tiles, contract, add):
    slots, rays, width = tiles.shape[2:]
    picked = jnp.dot(pick[...], table.astype(jnp.bfloat16), preferred_element_type=jnp.float32)
    prods = []
    for n in range(0, slots, 2):
        pair = tiles[0, 0, n : n + 2]
        if contract:
            pair = pair.reshape(2 * rays, width)
        else:
            pair = jnp.concatenate([pair[0], pair[1]], axis=1)
        both = lax.dot_general(
            picked[n * SUB : (n + 2) * SUB].astype(jnp.bfloat16),
            pair,
            (((1,), (contract,)), ((), ())),
            preferred_element_type=jnp.float32,
        )
        prods += [both[:SUB, :width], both[SUB:, width:]]
    left = jnp.concatenate(prods, axis=0)
    sums = None
    for _ in range(3):
        piece = left.astype(jnp.bfloat16)
        left = left - piece.astype(jnp.float32)
        term = jnp.dot(add[...], piece, preferred_element_type=jnp.float32)
        sums = term if sums is None else sums + term
    return sums


def project_kernel(tiles, pick, add, volume, other, measured, part):
    inst = measured.shape[2]
    blocks = part.shape[0] // (inst + 1)
    half = volume.shape[0] // inst
    table = []
    for c in range(inst):
        row = pl.ds(c, half, stride=inst)
        table += [volume[row, :], other[row, :]]
    table.append(jnp.ones((2 * half, part.shape[1]), jnp.float32))
    sums = apply_tiles(pick, jnp.concatenate(table, axis=0), tiles, 1, add)
    mine = lax.broadcasted_iota(jnp.int32, (blocks, part.shape[1]), 0) == lax.axis_index("vox")
    for c in range(inst):
        row = jnp.broadcast_to(measured[0, 0, c : c + 1, :], mine.shape)
        part[c * blocks : (c + 1) * blocks, :] = jnp.where(mine, row, 0.0) - sums[c * blocks : (c + 1) * blocks]
    part[inst * blocks : (inst + 1) * blocks, :] = sums[inst * blocks :]


def backproject_kernel(tiles, pick, add, total, own, send, residual):
    inst = residual.shape[0]
    blocks = total.shape[0] // (inst + 1)
    kinds = [total[c * blocks : (c + 1) * blocks, :] for c in range(inst + 1)]
    weight = kinds[inst] + 1.0
    table = [(kind / weight).astype(jnp.bfloat16).astype(jnp.float32) for kind in kinds[:inst]]
    mine = lax.broadcasted_iota(jnp.int32, weight.shape, 0) == lax.axis_index("vox")
    for c in range(inst):
        residual[c : c + 1, :] = jnp.sum(jnp.where(mine, table[c], 0.0), axis=0, keepdims=True)
    table = jnp.concatenate(table + [jnp.ones_like(weight)], axis=0)
    sums = apply_tiles(pick, table, tiles, 0, add)
    rows = own.shape[0]
    own[...] = sums[:rows]
    filler = jnp.zeros((send.shape[0] - rows, weight.shape[1]), jnp.float32)
    send[...] = jnp.concatenate([sums[rows:], filler], axis=0).astype(jnp.bfloat16)


def update_kernel(volume, own, there, residual, new_volume, own_residual):
    inst = residual.shape[0]
    half = volume.shape[0] // inst
    both = own[...] + there[...].astype(jnp.float32)[: own.shape[0]]
    weight = both[inst * half :] + 1.0
    for c in range(inst):
        row = pl.ds(c, half, stride=inst)
        new_volume[row, :] = jnp.maximum(volume[row, :] + both[c * half : (c + 1) * half] / weight, 0.0)
    own_residual[0, 0] = residual[...].astype(jnp.bfloat16)


def on_device(volume, tiles, tile_row, tile_col, tile_count, measured):
    half, inst, width = volume.shape
    slots = tiles.shape[2]
    blocks = lax.axis_size("vox") * measured.shape[1]
    f32, bf16 = jnp.float32, jnp.bfloat16
    vmem = pl.BlockSpec(memory_space=pltpu.VMEM)
    smem = pl.BlockSpec(memory_space=pltpu.SMEM)
    params = pltpu.CompilerParams(vmem_limit_bytes=VMEM_BYTES)

    def call(kernel, name, outs, scratch, args, scalars=0, cost=None):
        return pl.pallas_call(
            kernel,
            out_shape=[jax.ShapeDtypeStruct(shape, dtype) for shape, dtype in outs],
            in_specs=[smem] * scalars + [vmem] * (len(args) - scalars),
            out_specs=[vmem] * len(outs),
            scratch_shapes=scratch,
            compiler_params=params,
            cost_estimate=cost,
            name=name,
        )(*args)

    volume = volume.reshape(half * inst, width)
    other = exchange(volume, "ray", 1)
    kinds = inst + 1
    (spread,) = call(
        spread_kernel,
        "spread",
        [((slots, slots * SUB), f32)],
        [],
        [],
        cost=pl.CostEstimate(flops=HINT_FLOPS, bytes_accessed=0, transcendentals=0),
    )
    pick, pick_back, add, add_back = call(
        functools.partial(prepare_kernel, kinds),
        "prepare",
        [
            ((slots * SUB, 2 * half * kinds), bf16),
            ((slots * SUB, blocks * kinds), bf16),
            ((blocks * kinds, slots * SUB), bf16),
            ((2 * half * kinds, slots * SUB), bf16),
        ],
        [],
        [tile_count, tile_row, tile_col, spread],
        scalars=1,
    )
    (part,) = call(
        project_kernel,
        "project",
        [((kinds * blocks, width), f32)],
        [],
        [tiles, pick, add, volume, other, measured],
    )

    def add_parts(left, right):
        return call(add_kernel, "add", [((kinds * blocks, width), f32)], [], [left, right])[0]

    total = all_sum(part, "vox", add_parts)
    padded = -(-kinds * half // 16) * 16
    own, send, residual = call(
        backproject_kernel,
        "backproject",
        [((kinds * half, width), f32), ((padded, width), bf16), ((inst, width), f32)],
        [],
        [tiles, pick_back, add_back, total],
    )
    there = exchange(send, "ray", 1)
    new_volume, own_residual = call(
        update_kernel,
        "update",
        [(volume.shape, f32), ((1, 1, inst, width), bf16)],
        [],
        [volume, own, there, residual],
    )
    return new_volume.reshape(half, inst, width), own_residual


def solution(mesh):
    in_specs = (
        P(("slab", "vox", "ray"), None, None),
        P(("slab", "vox"), "ray", None, None, None),
        P(("slab", "vox"), "ray", None),
        P(("slab", "vox"), "ray", None),
        P(("slab", "vox"), "ray"),
        P("ray", ("slab", "vox"), None, None),
    )
    out_specs = (P(("slab", "vox", "ray"), None, None), P("ray", ("slab", "vox"), None, None))
    return jax.shard_map(
        on_device, mesh=mesh, in_specs=in_specs, out_specs=out_specs, check_vma=False
    )
```

```python
import functools

import jax
import jax.numpy as jnp
from jax import lax
from jax.experimental import pallas as pl
from jax.experimental.pallas import tpu as pltpu
from jax.sharding import PartitionSpec as P

SUB = 8
ROWS_FLOPS = 20_000_000_000
VMEM_BYTES = 16 << 20


def exchange(value, axis, mask):
    return permute(value, axis, lambda i: i ^ mask)


def permute(value, axis, target):
    return lax.ppermute(value, axis, [(i, target(i)) for i in range(lax.axis_size(axis))])


QUAD = ((1, 0, 2, 3), (2, 3, 1, 0), (3, 2, 0, 1), (0, 1, 3, 2))


def copy_kernel(value, out):
    out[...] = value[...]


def add_kernel(kept, left, right, kept_out, out):
    kept_out[...] = kept[...]
    out[...] = left[...] + right[...]


def all_sum(value, axis, call):
    size = lax.axis_size(axis)
    shape = (value.shape, value.dtype)
    stride = 1
    while stride < size:
        if 2 * stride < size:
            place = [(i // stride) % 4 for i in range(size)]
            first, right, left, last = (
                permute(value, axis, lambda i: i + (to[place[i]] - place[i]) * stride) for to in QUAD
            )
            (first,) = call(copy_kernel, "kept", [shape], [], [first])
            first, both = call(add_kernel, "add", [shape] * 2, [], [first, left, right])
            low = (lax.axis_index(axis) // stride) % 4 < 2
            value = (value + jnp.where(low, first, last)) + both
        else:
            value = value + exchange(value, axis, stride)
        stride *= 4
    return value


def rows_kernel(inst, picked):
    kind = lax.broadcasted_iota(jnp.int32, picked.shape, 0) % SUB
    picked[...] = (kind == inst).astype(jnp.float32)


def one_hot(key, blocks):
    return (lax.broadcasted_iota(jnp.int32, (blocks, key.shape[1]), 0) == key).astype(jnp.float32)


def places(cols, half):
    place = cols + lax.axis_index("ray") * half
    return jnp.where(place < 2 * half, place, place - 2 * half)


def slot_rows(which, table, picked):
    slots, width = which.shape[1], table[0].shape[1]
    rows = lax.dot_general(
        which.astype(jnp.bfloat16),
        jnp.concatenate(table, axis=1).astype(jnp.bfloat16),
        (((0,), (0,)), ((), ())),
        preferred_element_type=jnp.float32,
    )
    for c in range(len(table)):
        picked[pl.ds(c, slots, stride=SUB), :] = rows[:, c * width : (c + 1) * width]


def apply_tiles(picked, tiles, contract, add, count, prods, kinds):
    slots, rays, width = tiles.shape[2:]
    for n in range(0, slots, 2):
        pair = tiles[0, 0, n : n + 2]
        if contract:
            pair = pair.reshape(2 * rays, width)
        else:
            pair = jnp.concatenate([pair[0], pair[1]], axis=1)
        both = lax.dot_general(
            picked[n * SUB : (n + 2) * SUB, :].astype(jnp.bfloat16),
            pair,
            (((1,), (contract,)), ((), ())),
            preferred_element_type=jnp.float32,
        )
        prods[pl.ds(n, SUB, stride=slots), :] = both[:SUB, :width]
        prods[pl.ds(n + 1, SUB, stride=slots), :] = both[SUB:, width:]
    left = jnp.concatenate([prods[c * slots : (c + 1) * slots, :] for c in range(kinds)], axis=1)
    used = lax.broadcasted_iota(jnp.int32, add.shape, 1) < count[0, 0]
    onehot = jnp.where(used, add, 0.0).astype(jnp.bfloat16)
    sums = None
    for _ in range(3):
        piece = left.astype(jnp.bfloat16)
        left = left - piece.astype(jnp.float32)
        term = jnp.dot(onehot, piece, preferred_element_type=jnp.float32)
        sums = term if sums is None else sums + term
    return [sums[:, c * width : (c + 1) * width] for c in range(kinds)]


def project_kernel(count, tiles, rows, cols, volume, other, measured, _, part, picked, prods):
    inst = measured.shape[2]
    blocks = part.shape[0] // (inst + 1)
    half = volume.shape[0] // inst
    strides = [pl.ds(c, half, stride=inst) for c in range(inst)]
    table = [jnp.concatenate([volume[row, :], other[row, :]], axis=0) for row in strides]
    slot_rows(one_hot(places(cols[0], half), 2 * half), table, picked)
    sums = apply_tiles(picked, tiles, 1, one_hot(rows[0], blocks), count, prods, inst + 1)
    mine = lax.broadcasted_iota(jnp.int32, sums[0].shape, 0) == lax.axis_index("vox")
    for c in range(inst):
        row = jnp.broadcast_to(measured[0, 0, c : c + 1, :], sums[c].shape)
        part[c * blocks : (c + 1) * blocks, :] = jnp.where(mine, row, 0.0) - sums[c]
    part[inst * blocks : (inst + 1) * blocks, :] = sums[inst]


def backproject_kernel(count, tiles, rows, cols, total, _, own, send, residual, picked, prods):
    inst = residual.shape[0]
    blocks = total.shape[0] // (inst + 1)
    half = own.shape[0] // (inst + 1)
    kinds = [total[c * blocks : (c + 1) * blocks, :] for c in range(inst + 1)]
    weight = kinds[inst] + 1.0
    table = [(kind / weight).astype(jnp.bfloat16).astype(jnp.float32) for kind in kinds[:inst]]
    mine = lax.broadcasted_iota(jnp.int32, weight.shape, 0) == lax.axis_index("vox")
    for c in range(inst):
        residual[c : c + 1, :] = jnp.sum(jnp.where(mine, table[c], 0.0), axis=0, keepdims=True)
    slot_rows(one_hot(rows[0], blocks), table, picked)
    sums = apply_tiles(picked, tiles, 0, one_hot(places(cols[0], half), 2 * half), count, prods, inst + 1)
    filler = [jnp.zeros((half, weight.shape[1]), jnp.float32)] * (SUB - inst - 1)
    own[...] = jnp.concatenate([x[:half] for x in sums], axis=0)
    send[...] = jnp.concatenate([x[half:] for x in sums] + filler, axis=0).astype(jnp.bfloat16)


def update_kernel(volume, own, there, residual, new_volume, own_residual):
    inst = residual.shape[0]
    half = volume.shape[0] // inst
    both = own[...] + there[...].astype(jnp.float32)[: own.shape[0]]
    weight = both[inst * half :] + 1.0
    for c in range(inst):
        row = pl.ds(c, half, stride=inst)
        new_volume[row, :] = jnp.maximum(volume[row, :] + both[c * half : (c + 1) * half] / weight, 0.0)
    own_residual[0, 0] = residual[...].astype(jnp.bfloat16)


def on_device(volume, tiles, tile_row, tile_col, tile_count, measured):
    half, inst, width = volume.shape
    slots = tiles.shape[2]
    blocks = lax.axis_size("vox") * measured.shape[1]
    f32, bf16 = jnp.float32, jnp.bfloat16
    vmem = pl.BlockSpec(memory_space=pltpu.VMEM)
    smem = pl.BlockSpec(memory_space=pltpu.SMEM)
    params = pltpu.CompilerParams(vmem_limit_bytes=VMEM_BYTES)

    def call(kernel, name, outs, scratch, args, scalars=0, cost=None, aliases={}):
        return pl.pallas_call(
            kernel,
            out_shape=[jax.ShapeDtypeStruct(shape, dtype) for shape, dtype in outs],
            in_specs=[smem] * scalars + [vmem] * (len(args) - scalars),
            out_specs=[vmem] * len(outs),
            scratch_shapes=scratch,
            input_output_aliases=aliases,
            compiler_params=params,
            cost_estimate=cost,
            name=name,
        )(*args)

    volume = volume.reshape(half * inst, width)
    other = exchange(volume, "ray", 1)
    slot_shape = ((slots * SUB, width), f32)
    prods = pltpu.VMEM(*slot_shape)
    (picked,) = call(
        functools.partial(rows_kernel, inst),
        "rows",
        [slot_shape],
        [],
        [],
        cost=pl.CostEstimate(flops=ROWS_FLOPS, bytes_accessed=0, transcendentals=0),
    )
    part, picked = call(
        project_kernel,
        "project",
        [(((inst + 1) * blocks, width), f32), slot_shape],
        [prods],
        [tile_count, tiles, tile_row, tile_col, volume, other, measured, picked],
        scalars=1,
        aliases={7: 1},
    )
    total = all_sum(part, "vox", call)
    own, send, residual, _ = call(
        backproject_kernel,
        "backproject",
        [(((inst + 1) * half, width), f32), ((SUB * half, width), bf16), ((inst, width), f32), slot_shape],
        [prods],
        [tile_count, tiles, tile_row, tile_col, total, picked],
        scalars=1,
        aliases={5: 3},
    )
    there = exchange(send, "ray", 1)
    new_volume, own_residual = call(
        update_kernel,
        "update",
        [(volume.shape, f32), ((1, 1, inst, width), bf16)],
        [],
        [volume, own, there, residual],
    )
    return new_volume.reshape(half, inst, width), own_residual


def solution(mesh):
    in_specs = (
        P(("slab", "vox", "ray"), None, None),
        P(("slab", "vox"), "ray", None, None, None),
        P(("slab", "vox"), "ray", None),
        P(("slab", "vox"), "ray", None),
        P(("slab", "vox"), "ray"),
        P("ray", ("slab", "vox"), None, None),
    )
    out_specs = (P(("slab", "vox", "ray"), None, None), P("ray", ("slab", "vox"), None, None))
    return jax.shard_map(
        on_device, mesh=mesh, in_specs=in_specs, out_specs=out_specs, check_vma=False
    )
```

```python
import functools

import jax
import jax.numpy as jnp
from jax import lax
from jax.experimental import pallas as pl
from jax.experimental.pallas import tpu as pltpu
from jax.sharding import PartitionSpec as P

SUB = 8
ROWS_FLOPS = 20_000_000_000
VMEM_BYTES = 16 << 20


def exchange(value, axis, mask):
    size = lax.axis_size(axis)
    return lax.ppermute(value, axis, [(i, i ^ mask) for i in range(size)])


def all_sum(value, axis):
    size = lax.axis_size(axis)
    stride = 1
    while stride < size:
        if 2 * stride < size:
            across = exchange(value, axis, stride)
            both = exchange(value, axis, 3 * stride)
            along = exchange(value, axis, 2 * stride)
            value = (value + across) + (along + both)
        else:
            value = value + exchange(value, axis, stride)
        stride *= 4
    return value


def rows_kernel(inst, picked):
    kind = lax.broadcasted_iota(jnp.int32, picked.shape, 0) % SUB
    picked[...] = (kind == inst).astype(jnp.float32)


def one_hot(key, blocks):
    return (lax.broadcasted_iota(jnp.int32, (blocks, key.shape[1]), 0) == key).astype(jnp.float32)


def places(cols, half):
    place = cols + lax.axis_index("ray") * half
    return jnp.where(place < 2 * half, place, place - 2 * half)


def slot_rows(which, table, picked):
    slots, width = which.shape[1], table[0].shape[1]
    rows = lax.dot_general(
        which.astype(jnp.bfloat16),
        jnp.concatenate(table, axis=1).astype(jnp.bfloat16),
        (((0,), (0,)), ((), ())),
        preferred_element_type=jnp.float32,
    )
    for c in range(len(table)):
        picked[pl.ds(c, slots, stride=SUB), :] = rows[:, c * width : (c + 1) * width]


def apply_tiles(picked, tiles, contract, add, count, prods, kinds):
    slots, _, width = tiles.shape[2:]
    zeros = jnp.zeros((SUB, width), jnp.float32)
    for n in range(0, slots, 4):
        rows = [picked[k * SUB : (k + 1) * SUB, :] for k in range(n, n + 4)]
        first = jnp.concatenate([rows[0], zeros, rows[2], zeros], axis=0)
        second = jnp.concatenate([zeros, rows[1], zeros, rows[3]], axis=0)
        four = [tiles[0, 0, k] for k in range(n, n + 4)]
        order = (0, 1, 2, 3) if contract else (0, 2, 1, 3)
        upper = jnp.concatenate([four[order[0]], four[order[1]]], axis=1)
        lower = jnp.concatenate([four[order[2]], four[order[3]]], axis=1)
        both = lax.dot_general(
            jnp.concatenate([first, second], axis=1).astype(jnp.bfloat16),
            jnp.concatenate([upper, lower], axis=0),
            (((1,), (contract,)), ((), ())),
            preferred_element_type=jnp.float32,
        )
        for k in range(4):
            columns = slice(0, width) if k < 2 else slice(width, 2 * width)
            prods[pl.ds(n + k, SUB, stride=slots), :] = both[k * SUB : (k + 1) * SUB, columns]
    left = jnp.concatenate([prods[c * slots : (c + 1) * slots, :] for c in range(kinds)], axis=1)
    used = lax.broadcasted_iota(jnp.int32, add.shape, 1) < count[0, 0]
    onehot = jnp.where(used, add, 0.0).astype(jnp.bfloat16)
    sums = None
    for _ in range(3):
        piece = left.astype(jnp.bfloat16)
        left = left - piece.astype(jnp.float32)
        term = jnp.dot(onehot, piece, preferred_element_type=jnp.float32)
        sums = term if sums is None else sums + term
    return [sums[:, c * width : (c + 1) * width] for c in range(kinds)]


def project_kernel(count, tiles, rows, cols, volume, other, measured, _, part, picked, prods):
    inst = measured.shape[2]
    blocks = part.shape[0] // (inst + 1)
    half = volume.shape[0] // inst
    strides = [pl.ds(c, half, stride=inst) for c in range(inst)]
    table = [jnp.concatenate([volume[row, :], other[row, :]], axis=0) for row in strides]
    slot_rows(one_hot(places(cols[0], half), 2 * half), table, picked)
    sums = apply_tiles(picked, tiles, 1, one_hot(rows[0], blocks), count, prods, inst + 1)
    mine = lax.broadcasted_iota(jnp.int32, sums[0].shape, 0) == lax.axis_index("vox")
    for c in range(inst):
        row = jnp.broadcast_to(measured[0, 0, c : c + 1, :], sums[c].shape)
        part[c * blocks : (c + 1) * blocks, :] = jnp.where(mine, row, 0.0) - sums[c]
    part[inst * blocks : (inst + 1) * blocks, :] = sums[inst]


def backproject_kernel(count, tiles, rows, cols, total, _, own, send, residual, picked, prods):
    inst = residual.shape[0]
    blocks = total.shape[0] // (inst + 1)
    half = own.shape[0] // (inst + 1)
    kinds = [total[c * blocks : (c + 1) * blocks, :] for c in range(inst + 1)]
    weight = kinds[inst] + 1.0
    table = [(kind / weight).astype(jnp.bfloat16).astype(jnp.float32) for kind in kinds[:inst]]
    mine = lax.broadcasted_iota(jnp.int32, weight.shape, 0) == lax.axis_index("vox")
    for c in range(inst):
        residual[c : c + 1, :] = jnp.sum(jnp.where(mine, table[c], 0.0), axis=0, keepdims=True)
    slot_rows(one_hot(rows[0], blocks), table, picked)
    sums = apply_tiles(picked, tiles, 0, one_hot(places(cols[0], half), 2 * half), count, prods, inst + 1)
    filler = [jnp.zeros((half, weight.shape[1]), jnp.float32)] * (SUB - inst - 1)
    own[...] = jnp.concatenate([x[:half] for x in sums], axis=0)
    send[...] = jnp.concatenate([x[half:] for x in sums] + filler, axis=0).astype(jnp.bfloat16)


def update_kernel(volume, own, there, residual, new_volume, own_residual):
    inst = residual.shape[0]
    half = volume.shape[0] // inst
    both = own[...] + there[...].astype(jnp.float32)[: own.shape[0]]
    weight = both[inst * half :] + 1.0
    for c in range(inst):
        row = pl.ds(c, half, stride=inst)
        new_volume[row, :] = jnp.maximum(volume[row, :] + both[c * half : (c + 1) * half] / weight, 0.0)
    own_residual[0, 0] = residual[...].astype(jnp.bfloat16)


def on_device(volume, tiles, tile_row, tile_col, tile_count, measured):
    half, inst, width = volume.shape
    slots = tiles.shape[2]
    blocks = lax.axis_size("vox") * measured.shape[1]
    f32, bf16 = jnp.float32, jnp.bfloat16
    vmem = pl.BlockSpec(memory_space=pltpu.VMEM)
    smem = pl.BlockSpec(memory_space=pltpu.SMEM)
    params = pltpu.CompilerParams(vmem_limit_bytes=VMEM_BYTES)

    def call(kernel, name, outs, scratch, args, scalars=0, cost=None, aliases={}):
        return pl.pallas_call(
            kernel,
            out_shape=[jax.ShapeDtypeStruct(shape, dtype) for shape, dtype in outs],
            in_specs=[smem] * scalars + [vmem] * (len(args) - scalars),
            out_specs=[vmem] * len(outs),
            scratch_shapes=scratch,
            input_output_aliases=aliases,
            compiler_params=params,
            cost_estimate=cost,
            name=name,
        )(*args)

    volume = volume.reshape(half * inst, width)
    other = exchange(volume, "ray", 1)
    slot_shape = ((slots * SUB, width), f32)
    prods = pltpu.VMEM(*slot_shape)
    (picked,) = call(
        functools.partial(rows_kernel, inst),
        "rows",
        [slot_shape],
        [],
        [],
        cost=pl.CostEstimate(flops=ROWS_FLOPS, bytes_accessed=0, transcendentals=0),
    )
    part, picked = call(
        project_kernel,
        "project",
        [(((inst + 1) * blocks, width), f32), slot_shape],
        [prods],
        [tile_count, tiles, tile_row, tile_col, volume, other, measured, picked],
        scalars=1,
        aliases={7: 1},
    )
    total = all_sum(part, "vox")
    own, send, residual, _ = call(
        backproject_kernel,
        "backproject",
        [(((inst + 1) * half, width), f32), ((SUB * half, width), bf16), ((inst, width), f32), slot_shape],
        [prods],
        [tile_count, tiles, tile_row, tile_col, total, picked],
        scalars=1,
        aliases={5: 3},
    )
    there = exchange(send, "ray", 1)
    new_volume, own_residual = call(
        update_kernel,
        "update",
        [(volume.shape, f32), ((1, 1, inst, width), bf16)],
        [],
        [volume, own, there, residual],
    )
    return new_volume.reshape(half, inst, width), own_residual


def solution(mesh):
    in_specs = (
        P(("slab", "vox", "ray"), None, None),
        P(("slab", "vox"), "ray", None, None, None),
        P(("slab", "vox"), "ray", None),
        P(("slab", "vox"), "ray", None),
        P(("slab", "vox"), "ray"),
        P("ray", ("slab", "vox"), None, None),
    )
    out_specs = (P(("slab", "vox", "ray"), None, None), P("ray", ("slab", "vox"), None, None))
    return jax.shard_map(
        on_device, mesh=mesh, in_specs=in_specs, out_specs=out_specs, check_vma=False
    )
```

```python
import functools

import jax
import jax.numpy as jnp
from jax import lax
from jax.experimental import pallas as pl
from jax.experimental.pallas import tpu as pltpu
from jax.sharding import PartitionSpec as P

SUB = 8
ROWS_FLOPS = 20_000_000_000
VMEM_BYTES = 16 << 20


def exchange(value, axis, mask):
    size = lax.axis_size(axis)
    return lax.ppermute(value, axis, [(i, i ^ mask) for i in range(size)])


def all_sum(value, axis):
    size = lax.axis_size(axis)
    stride = 1
    while stride < size:
        if 2 * stride < size:
            across = exchange(value, axis, stride)
            both = exchange(value, axis, 3 * stride)
            along = exchange(value, axis, 2 * stride)
            value = (value + across) + (along + both)
        else:
            value = value + exchange(value, axis, stride)
        stride *= 4
    return value


def rows_kernel(inst, picked):
    kind = lax.broadcasted_iota(jnp.int32, picked.shape, 0) % SUB
    picked[...] = (kind == inst).astype(jnp.float32)


def one_hot(key, blocks):
    return (lax.broadcasted_iota(jnp.int32, (blocks, key.shape[1]), 0) == key).astype(jnp.float32)


def places(cols, half):
    place = cols + lax.axis_index("ray") * half
    return jnp.where(place < 2 * half, place, place - 2 * half)


def slot_rows(which, table, picked):
    slots, width = which.shape[1], table[0].shape[1]
    rows = lax.dot_general(
        which.astype(jnp.bfloat16),
        jnp.concatenate(table, axis=1).astype(jnp.bfloat16),
        (((0,), (0,)), ((), ())),
        preferred_element_type=jnp.float32,
    )
    for c in range(len(table)):
        picked[pl.ds(c, slots, stride=SUB), :] = rows[:, c * width : (c + 1) * width]


def apply_tiles(picked, tiles, transposed, add, count, prods, kinds):
    slots, _, width = tiles.shape[2:]
    for n in range(0, slots, 2):
        pair = [tiles[0, 0, k] for k in (n, n + 1)]
        if transposed:
            pair = [tile.T for tile in pair]
        pair = jnp.concatenate(pair, axis=1)
        left = picked[n * SUB : (n + 2) * SUB, :].astype(jnp.bfloat16)
        both = jnp.dot(left, pair, preferred_element_type=jnp.float32)
        prods[pl.ds(n, SUB, stride=slots), :] = both[:SUB, :width]
        prods[pl.ds(n + 1, SUB, stride=slots), :] = both[SUB:, width:]
    left = jnp.concatenate([prods[c * slots : (c + 1) * slots, :] for c in range(kinds)], axis=1)
    used = lax.broadcasted_iota(jnp.int32, add.shape, 1) < count[0, 0]
    onehot = jnp.where(used, add, 0.0).astype(jnp.bfloat16)
    sums = None
    for _ in range(3):
        piece = left.astype(jnp.bfloat16)
        left = left - piece.astype(jnp.float32)
        term = jnp.dot(onehot, piece, preferred_element_type=jnp.float32)
        sums = term if sums is None else sums + term
    return [sums[:, c * width : (c + 1) * width] for c in range(kinds)]


def project_kernel(count, tiles, rows, cols, volume, other, measured, _, part, picked, prods):
    inst = measured.shape[2]
    blocks = part.shape[0] // (inst + 1)
    half = volume.shape[0] // inst
    strides = [pl.ds(c, half, stride=inst) for c in range(inst)]
    table = [jnp.concatenate([volume[row, :], other[row, :]], axis=0) for row in strides]
    slot_rows(one_hot(places(cols[0], half), 2 * half), table, picked)
    sums = apply_tiles(picked, tiles, True, one_hot(rows[0], blocks), count, prods, inst + 1)
    mine = lax.broadcasted_iota(jnp.int32, sums[0].shape, 0) == lax.axis_index("vox")
    for c in range(inst):
        row = jnp.broadcast_to(measured[0, 0, c : c + 1, :], sums[c].shape)
        part[c * blocks : (c + 1) * blocks, :] = jnp.where(mine, row, 0.0) - sums[c]
    part[inst * blocks : (inst + 1) * blocks, :] = sums[inst]


def backproject_kernel(count, tiles, rows, cols, total, _, own, send, residual, picked, prods):
    inst = residual.shape[0]
    blocks = total.shape[0] // (inst + 1)
    half = own.shape[0] // (inst + 1)
    kinds = [total[c * blocks : (c + 1) * blocks, :] for c in range(inst + 1)]
    weight = kinds[inst] + 1.0
    table = [(kind / weight).astype(jnp.bfloat16).astype(jnp.float32) for kind in kinds[:inst]]
    mine = lax.broadcasted_iota(jnp.int32, weight.shape, 0) == lax.axis_index("vox")
    for c in range(inst):
        residual[c : c + 1, :] = jnp.sum(jnp.where(mine, table[c], 0.0), axis=0, keepdims=True)
    slot_rows(one_hot(rows[0], blocks), table, picked)
    sums = apply_tiles(picked, tiles, False, one_hot(places(cols[0], half), 2 * half), count, prods, inst + 1)
    filler = [jnp.zeros((half, weight.shape[1]), jnp.float32)] * (SUB - inst - 1)
    own[...] = jnp.concatenate([x[:half] for x in sums], axis=0)
    send[...] = jnp.concatenate([x[half:] for x in sums] + filler, axis=0).astype(jnp.bfloat16)


def update_kernel(volume, own, there, residual, new_volume, own_residual):
    inst = residual.shape[0]
    half = volume.shape[0] // inst
    both = own[...] + there[...].astype(jnp.float32)[: own.shape[0]]
    weight = both[inst * half :] + 1.0
    for c in range(inst):
        row = pl.ds(c, half, stride=inst)
        new_volume[row, :] = jnp.maximum(volume[row, :] + both[c * half : (c + 1) * half] / weight, 0.0)
    own_residual[0, 0] = residual[...].astype(jnp.bfloat16)


def on_device(volume, tiles, tile_row, tile_col, tile_count, measured):
    half, inst, width = volume.shape
    slots = tiles.shape[2]
    blocks = lax.axis_size("vox") * measured.shape[1]
    f32, bf16 = jnp.float32, jnp.bfloat16
    vmem = pl.BlockSpec(memory_space=pltpu.VMEM)
    smem = pl.BlockSpec(memory_space=pltpu.SMEM)
    params = pltpu.CompilerParams(vmem_limit_bytes=VMEM_BYTES)

    def call(kernel, name, outs, scratch, args, scalars=0, cost=None, aliases={}):
        return pl.pallas_call(
            kernel,
            out_shape=[jax.ShapeDtypeStruct(shape, dtype) for shape, dtype in outs],
            in_specs=[smem] * scalars + [vmem] * (len(args) - scalars),
            out_specs=[vmem] * len(outs),
            scratch_shapes=scratch,
            input_output_aliases=aliases,
            compiler_params=params,
            cost_estimate=cost,
            name=name,
        )(*args)

    volume = volume.reshape(half * inst, width)
    other = exchange(volume, "ray", 1)
    slot_shape = ((slots * SUB, width), f32)
    prods = pltpu.VMEM(*slot_shape)
    (picked,) = call(
        functools.partial(rows_kernel, inst),
        "rows",
        [slot_shape],
        [],
        [],
        cost=pl.CostEstimate(flops=ROWS_FLOPS, bytes_accessed=0, transcendentals=0),
    )
    part, picked = call(
        project_kernel,
        "project",
        [(((inst + 1) * blocks, width), f32), slot_shape],
        [prods],
        [tile_count, tiles, tile_row, tile_col, volume, other, measured, picked],
        scalars=1,
        aliases={7: 1},
    )
    total = all_sum(part, "vox")
    own, send, residual, _ = call(
        backproject_kernel,
        "backproject",
        [(((inst + 1) * half, width), f32), ((SUB * half, width), bf16), ((inst, width), f32), slot_shape],
        [prods],
        [tile_count, tiles, tile_row, tile_col, total, picked],
        scalars=1,
        aliases={5: 3},
    )
    there = exchange(send, "ray", 1)
    new_volume, own_residual = call(
        update_kernel,
        "update",
        [(volume.shape, f32), ((1, 1, inst, width), bf16)],
        [],
        [volume, own, there, residual],
    )
    return new_volume.reshape(half, inst, width), own_residual


def solution(mesh):
    in_specs = (
        P(("slab", "vox", "ray"), None, None),
        P(("slab", "vox"), "ray", None, None, None),
        P(("slab", "vox"), "ray", None),
        P(("slab", "vox"), "ray", None),
        P(("slab", "vox"), "ray"),
        P("ray", ("slab", "vox"), None, None),
    )
    out_specs = (P(("slab", "vox", "ray"), None, None), P("ray", ("slab", "vox"), None, None))
    return jax.shard_map(
        on_device, mesh=mesh, in_specs=in_specs, out_specs=out_specs, check_vma=False
    )
```

```python
import functools

import jax
import jax.numpy as jnp
from jax import lax
from jax.experimental import pallas as pl
from jax.experimental.pallas import tpu as pltpu
from jax.sharding import PartitionSpec as P

SUB = 8
ROWS_FLOPS = 20_000_000_000
VMEM_BYTES = 16 << 20


def exchange(value, axis, mask):
    size = lax.axis_size(axis)
    return lax.ppermute(value, axis, [(i, i ^ mask) for i in range(size)])


def all_sum(value, axis):
    size = lax.axis_size(axis)
    stride = 1
    while stride < size:
        if 2 * stride < size:
            across = exchange(value, axis, stride)
            both = exchange(value, axis, 3 * stride)
            along = exchange(value, axis, 2 * stride)
            value = (value + across) + (along + both)
        else:
            value = value + exchange(value, axis, stride)
        stride *= 4
    return value


def rows_kernel(inst, picked):
    kind = lax.broadcasted_iota(jnp.int32, picked.shape, 0) % SUB
    picked[...] = (kind == inst).astype(jnp.float32)


def prepare_kernel(count, rows, cols, pick, pick_back, add, add_back):
    blocks, half = add.shape[0], add_back.shape[0] // 2
    used = lax.broadcasted_iota(jnp.int32, rows.shape[1:], 1) < count[0, 0]
    place = cols[0] + lax.axis_index("ray") * half
    place = jnp.where(place < 2 * half, place, place - 2 * half)
    for key, one_way, other_way in ((rows[0], add, pick_back), (place, add_back, pick)):
        hit = (lax.broadcasted_iota(jnp.int32, one_way.shape, 0) == key) & used
        hit = hit.astype(jnp.float32)
        one_way[...] = hit
        other_way[...] = hit.T


def slot_rows(pick, table, picked):
    slots, width = pick.shape[0], table[0].shape[1]
    rows = jnp.dot(
        pick[...].astype(jnp.bfloat16),
        jnp.concatenate(table, axis=1).astype(jnp.bfloat16),
        preferred_element_type=jnp.float32,
    )
    for c in range(len(table)):
        picked[pl.ds(c, slots, stride=SUB), :] = rows[:, c * width : (c + 1) * width]


def apply_tiles(picked, tiles, transposed, add, prods, kinds):
    slots, _, width = tiles.shape[2:]
    for n in range(0, slots, 2):
        pair = [tiles[0, 0, k] for k in (n, n + 1)]
        if transposed:
            pair = [tile.T for tile in pair]
        pair = jnp.concatenate(pair, axis=1)
        left = picked[n * SUB : (n + 2) * SUB, :].astype(jnp.bfloat16)
        both = jnp.dot(left, pair, preferred_element_type=jnp.float32)
        prods[pl.ds(n, SUB, stride=slots), :] = both[:SUB, :width]
        prods[pl.ds(n + 1, SUB, stride=slots), :] = both[SUB:, width:]
    left = jnp.concatenate([prods[c * slots : (c + 1) * slots, :] for c in range(kinds)], axis=1)
    onehot = add[...].astype(jnp.bfloat16)
    sums = None
    for _ in range(3):
        piece = left.astype(jnp.bfloat16)
        left = left - piece.astype(jnp.float32)
        term = jnp.dot(onehot, piece, preferred_element_type=jnp.float32)
        sums = term if sums is None else sums + term
    return [sums[:, c * width : (c + 1) * width] for c in range(kinds)]


def project_kernel(tiles, pick, add, volume, other, measured, _, part, picked, prods):
    inst = measured.shape[2]
    blocks = part.shape[0] // (inst + 1)
    half = volume.shape[0] // inst
    strides = [pl.ds(c, half, stride=inst) for c in range(inst)]
    table = [jnp.concatenate([volume[row, :], other[row, :]], axis=0) for row in strides]
    slot_rows(pick, table, picked)
    sums = apply_tiles(picked, tiles, True, add, prods, inst + 1)
    mine = lax.broadcasted_iota(jnp.int32, sums[0].shape, 0) == lax.axis_index("vox")
    for c in range(inst):
        row = jnp.broadcast_to(measured[0, 0, c : c + 1, :], sums[c].shape)
        part[c * blocks : (c + 1) * blocks, :] = jnp.where(mine, row, 0.0) - sums[c]
    part[inst * blocks : (inst + 1) * blocks, :] = sums[inst]


def backproject_kernel(tiles, pick, add, total, _, own, send, residual, picked, prods):
    inst = residual.shape[0]
    blocks = total.shape[0] // (inst + 1)
    half = own.shape[0] // (inst + 1)
    kinds = [total[c * blocks : (c + 1) * blocks, :] for c in range(inst + 1)]
    weight = kinds[inst] + 1.0
    table = [(kind / weight).astype(jnp.bfloat16).astype(jnp.float32) for kind in kinds[:inst]]
    mine = lax.broadcasted_iota(jnp.int32, weight.shape, 0) == lax.axis_index("vox")
    for c in range(inst):
        residual[c : c + 1, :] = jnp.sum(jnp.where(mine, table[c], 0.0), axis=0, keepdims=True)
    slot_rows(pick, table, picked)
    sums = apply_tiles(picked, tiles, False, add, prods, inst + 1)
    filler = [jnp.zeros((half, weight.shape[1]), jnp.float32)] * (SUB - inst - 1)
    own[...] = jnp.concatenate([x[:half] for x in sums], axis=0)
    send[...] = jnp.concatenate([x[half:] for x in sums] + filler, axis=0).astype(jnp.bfloat16)


def update_kernel(volume, own, there, residual, new_volume, own_residual):
    inst = residual.shape[0]
    half = volume.shape[0] // inst
    both = own[...] + there[...].astype(jnp.float32)[: own.shape[0]]
    weight = both[inst * half :] + 1.0
    for c in range(inst):
        row = pl.ds(c, half, stride=inst)
        new_volume[row, :] = jnp.maximum(volume[row, :] + both[c * half : (c + 1) * half] / weight, 0.0)
    own_residual[0, 0] = residual[...].astype(jnp.bfloat16)


def on_device(volume, tiles, tile_row, tile_col, tile_count, measured):
    half, inst, width = volume.shape
    slots = tiles.shape[2]
    blocks = lax.axis_size("vox") * measured.shape[1]
    f32, bf16 = jnp.float32, jnp.bfloat16
    vmem = pl.BlockSpec(memory_space=pltpu.VMEM)
    smem = pl.BlockSpec(memory_space=pltpu.SMEM)
    params = pltpu.CompilerParams(vmem_limit_bytes=VMEM_BYTES)

    def call(kernel, name, outs, scratch, args, scalars=0, cost=None, aliases={}):
        return pl.pallas_call(
            kernel,
            out_shape=[jax.ShapeDtypeStruct(shape, dtype) for shape, dtype in outs],
            in_specs=[smem] * scalars + [vmem] * (len(args) - scalars),
            out_specs=[vmem] * len(outs),
            scratch_shapes=scratch,
            input_output_aliases=aliases,
            compiler_params=params,
            cost_estimate=cost,
            name=name,
        )(*args)

    volume = volume.reshape(half * inst, width)
    other = exchange(volume, "ray", 1)
    slot_shape = ((slots * SUB, width), f32)
    prods = pltpu.VMEM(*slot_shape)
    (picked,) = call(
        functools.partial(rows_kernel, inst),
        "rows",
        [slot_shape],
        [],
        [],
        cost=pl.CostEstimate(flops=ROWS_FLOPS, bytes_accessed=0, transcendentals=0),
    )
    pick, pick_back, add, add_back = call(
        prepare_kernel,
        "prepare",
        [((slots, 2 * half), f32), ((slots, blocks), f32), ((blocks, slots), f32), ((2 * half, slots), f32)],
        [],
        [tile_count, tile_row, tile_col],
        scalars=1,
    )
    part, picked = call(
        project_kernel,
        "project",
        [(((inst + 1) * blocks, width), f32), slot_shape],
        [prods],
        [tiles, pick, add, volume, other, measured, picked],
        aliases={6: 1},
    )
    total = all_sum(part, "vox")
    own, send, residual, _ = call(
        backproject_kernel,
        "backproject",
        [(((inst + 1) * half, width), f32), ((SUB * half, width), bf16), ((inst, width), f32), slot_shape],
        [prods],
        [tiles, pick_back, add_back, total, picked],
        aliases={4: 3},
    )
    there = exchange(send, "ray", 1)
    new_volume, own_residual = call(
        update_kernel,
        "update",
        [(volume.shape, f32), ((1, 1, inst, width), bf16)],
        [],
        [volume, own, there, residual],
    )
    return new_volume.reshape(half, inst, width), own_residual


def solution(mesh):
    in_specs = (
        P(("slab", "vox", "ray"), None, None),
        P(("slab", "vox"), "ray", None, None, None),
        P(("slab", "vox"), "ray", None),
        P(("slab", "vox"), "ray", None),
        P(("slab", "vox"), "ray"),
        P("ray", ("slab", "vox"), None, None),
    )
    out_specs = (P(("slab", "vox", "ray"), None, None), P("ray", ("slab", "vox"), None, None))
    return jax.shard_map(
        on_device, mesh=mesh, in_specs=in_specs, out_specs=out_specs, check_vma=False
    )
```

```python
import functools

import jax
import jax.numpy as jnp
from jax import lax
from jax.experimental import pallas as pl
from jax.experimental.pallas import tpu as pltpu
from jax.sharding import PartitionSpec as P

SUB = 8
ROWS_FLOPS = 20_000_000_000
VMEM_BYTES = 16 << 20


def exchange(value, axis, mask):
    size = lax.axis_size(axis)
    return lax.ppermute(value, axis, [(i, i ^ mask) for i in range(size)])


def all_sum(value, axis):
    bits = (lax.axis_size(axis) - 1).bit_length()
    if bits % 2:
        bits -= 1
        value = value + exchange(value, axis, 1 << bits)
    while bits:
        bits -= 2
        stride = 1 << bits
        across = exchange(value, axis, stride)
        both = exchange(value, axis, 3 * stride)
        along = exchange(value, axis, 2 * stride)
        value = (value + across) + (along + both)
    return value


def rows_kernel(inst, picked):
    kind = lax.broadcasted_iota(jnp.int32, picked.shape, 0) % SUB
    picked[...] = (kind == inst).astype(jnp.float32)


def prepare_kernel(count, rows, cols, pick, pick_back, add, add_back):
    blocks, half = add.shape[0], add_back.shape[0] // 2
    used = lax.broadcasted_iota(jnp.int32, rows.shape[1:], 1) < count[0, 0]
    place = cols[0] + lax.axis_index("ray") * half
    place = jnp.where(place < 2 * half, place, place - 2 * half)
    for key, one_way, other_way in ((rows[0], add, pick_back), (place, add_back, pick)):
        hit = (lax.broadcasted_iota(jnp.int32, one_way.shape, 0) == key) & used
        hit = hit.astype(jnp.float32)
        one_way[...] = hit
        other_way[...] = hit.T


def slot_rows(pick, table, picked):
    slots, width = pick.shape[0], table[0].shape[1]
    rows = jnp.dot(
        pick[...].astype(jnp.bfloat16),
        jnp.concatenate(table, axis=1).astype(jnp.bfloat16),
        preferred_element_type=jnp.float32,
    )
    for c in range(len(table)):
        picked[pl.ds(c, slots, stride=SUB), :] = rows[:, c * width : (c + 1) * width]


def apply_tiles(picked, tiles, transposed, add, prods, kinds):
    slots, _, width = tiles.shape[2:]
    for n in range(0, slots, 2):
        pair = [tiles[0, 0, k] for k in (n, n + 1)]
        if transposed:
            pair = [tile.T for tile in pair]
        pair = jnp.concatenate(pair, axis=1)
        left = picked[n * SUB : (n + 2) * SUB, :].astype(jnp.bfloat16)
        both = jnp.dot(left, pair, preferred_element_type=jnp.float32)
        prods[pl.ds(n, SUB, stride=slots), :] = both[:SUB, :width]
        prods[pl.ds(n + 1, SUB, stride=slots), :] = both[SUB:, width:]
    left = jnp.concatenate([prods[c * slots : (c + 1) * slots, :] for c in range(kinds)], axis=1)
    onehot = add[...].astype(jnp.bfloat16)
    sums = None
    for _ in range(3):
        piece = left.astype(jnp.bfloat16)
        left = left - piece.astype(jnp.float32)
        term = jnp.dot(onehot, piece, preferred_element_type=jnp.float32)
        sums = term if sums is None else sums + term
    return [sums[:, c * width : (c + 1) * width] for c in range(kinds)]


def project_kernel(tiles, pick, add, volume, other, measured, _, part, picked, prods):
    inst = measured.shape[2]
    blocks = part.shape[0] // (inst + 1)
    half = volume.shape[0] // inst
    strides = [pl.ds(c, half, stride=inst) for c in range(inst)]
    table = [jnp.concatenate([volume[row, :], other[row, :]], axis=0) for row in strides]
    slot_rows(pick, table, picked)
    sums = apply_tiles(picked, tiles, True, add, prods, inst + 1)
    mine = lax.broadcasted_iota(jnp.int32, sums[0].shape, 0) == lax.axis_index("vox")
    for c in range(inst):
        row = jnp.broadcast_to(measured[0, 0, c : c + 1, :], sums[c].shape)
        part[c * blocks : (c + 1) * blocks, :] = jnp.where(mine, row, 0.0) - sums[c]
    part[inst * blocks : (inst + 1) * blocks, :] = sums[inst]


def backproject_kernel(tiles, pick, add, total, _, own, send, residual, picked, prods):
    inst = residual.shape[0]
    blocks = total.shape[0] // (inst + 1)
    half = own.shape[0] // (inst + 1)
    kinds = [total[c * blocks : (c + 1) * blocks, :] for c in range(inst + 1)]
    weight = kinds[inst] + 1.0
    table = [(kind / weight).astype(jnp.bfloat16).astype(jnp.float32) for kind in kinds[:inst]]
    mine = lax.broadcasted_iota(jnp.int32, weight.shape, 0) == lax.axis_index("vox")
    for c in range(inst):
        residual[c : c + 1, :] = jnp.sum(jnp.where(mine, table[c], 0.0), axis=0, keepdims=True)
    slot_rows(pick, table, picked)
    sums = apply_tiles(picked, tiles, False, add, prods, inst + 1)
    filler = [jnp.zeros((half, weight.shape[1]), jnp.float32)] * (SUB - inst - 1)
    own[...] = jnp.concatenate([x[:half] for x in sums], axis=0)
    send[...] = jnp.concatenate([x[half:] for x in sums] + filler, axis=0).astype(jnp.bfloat16)


def update_kernel(volume, own, there, residual, new_volume, own_residual):
    inst = residual.shape[0]
    half = volume.shape[0] // inst
    both = own[...] + there[...].astype(jnp.float32)[: own.shape[0]]
    weight = both[inst * half :] + 1.0
    for c in range(inst):
        row = pl.ds(c, half, stride=inst)
        new_volume[row, :] = jnp.maximum(volume[row, :] + both[c * half : (c + 1) * half] / weight, 0.0)
    own_residual[0, 0] = residual[...].astype(jnp.bfloat16)


def on_device(volume, tiles, tile_row, tile_col, tile_count, measured):
    half, inst, width = volume.shape
    slots = tiles.shape[2]
    blocks = lax.axis_size("vox") * measured.shape[1]
    f32, bf16 = jnp.float32, jnp.bfloat16
    vmem = pl.BlockSpec(memory_space=pltpu.VMEM)
    smem = pl.BlockSpec(memory_space=pltpu.SMEM)
    params = pltpu.CompilerParams(vmem_limit_bytes=VMEM_BYTES)

    def call(kernel, name, outs, scratch, args, scalars=0, cost=None, aliases={}):
        return pl.pallas_call(
            kernel,
            out_shape=[jax.ShapeDtypeStruct(shape, dtype) for shape, dtype in outs],
            in_specs=[smem] * scalars + [vmem] * (len(args) - scalars),
            out_specs=[vmem] * len(outs),
            scratch_shapes=scratch,
            input_output_aliases=aliases,
            compiler_params=params,
            cost_estimate=cost,
            name=name,
        )(*args)

    volume = volume.reshape(half * inst, width)
    other = exchange(volume, "ray", 1)
    slot_shape = ((slots * SUB, width), f32)
    prods = pltpu.VMEM(*slot_shape)
    (picked,) = call(
        functools.partial(rows_kernel, inst),
        "rows",
        [slot_shape],
        [],
        [],
        cost=pl.CostEstimate(flops=ROWS_FLOPS, bytes_accessed=0, transcendentals=0),
    )
    pick, pick_back, add, add_back = call(
        prepare_kernel,
        "prepare",
        [((slots, 2 * half), f32), ((slots, blocks), f32), ((blocks, slots), f32), ((2 * half, slots), f32)],
        [],
        [tile_count, tile_row, tile_col],
        scalars=1,
    )
    part, picked = call(
        project_kernel,
        "project",
        [(((inst + 1) * blocks, width), f32), slot_shape],
        [prods],
        [tiles, pick, add, volume, other, measured, picked],
        aliases={6: 1},
    )
    total = all_sum(part, "vox")
    own, send, residual, _ = call(
        backproject_kernel,
        "backproject",
        [(((inst + 1) * half, width), f32), ((SUB * half, width), bf16), ((inst, width), f32), slot_shape],
        [prods],
        [tiles, pick_back, add_back, total, picked],
        aliases={4: 3},
    )
    there = exchange(send, "ray", 1)
    new_volume, own_residual = call(
        update_kernel,
        "update",
        [(volume.shape, f32), ((1, 1, inst, width), bf16)],
        [],
        [volume, own, there, residual],
    )
    return new_volume.reshape(half, inst, width), own_residual


def solution(mesh):
    in_specs = (
        P(("slab", "vox", "ray"), None, None),
        P(("slab", "vox"), "ray", None, None, None),
        P(("slab", "vox"), "ray", None),
        P(("slab", "vox"), "ray", None),
        P(("slab", "vox"), "ray"),
        P("ray", ("slab", "vox"), None, None),
    )
    out_specs = (P(("slab", "vox", "ray"), None, None), P("ray", ("slab", "vox"), None, None))
    return jax.shard_map(
        on_device, mesh=mesh, in_specs=in_specs, out_specs=out_specs, check_vma=False
    )
```

```python
import functools

import jax
import jax.numpy as jnp
from jax import lax
from jax.experimental import pallas as pl
from jax.experimental.pallas import tpu as pltpu
from jax.sharding import PartitionSpec as P

SUB = 8
ROWS_FLOPS = 20_000_000_000
PARTS = 3
VMEM_BYTES = 16 << 20


def exchange(value, axis, mask):
    size = lax.axis_size(axis)
    return lax.ppermute(value, axis, [(i, i ^ mask) for i in range(size)])


def all_sum(value, axis):
    bits = (lax.axis_size(axis) - 1).bit_length()
    if bits % 2:
        bits -= 1
        value = value + exchange(value, axis, 1 << bits)
    while bits:
        bits -= 2
        stride = 1 << bits
        across = exchange(value, axis, stride)
        both = exchange(value, axis, 3 * stride)
        along = exchange(value, axis, 2 * stride)
        value = (value + across) + (along + both)
    return value


def rows_kernel(inst, picked):
    kind = lax.broadcasted_iota(jnp.int32, picked.shape, 0) % SUB
    picked[...] = (kind == inst).astype(jnp.float32)


def prepare_kernel(count, rows, cols, pick, pick_back, add, add_back):
    blocks, half = add.shape[0], add_back.shape[0] // 2
    used = lax.broadcasted_iota(jnp.int32, rows.shape[1:], 1) < count[0, 0]
    place = cols[0] + lax.axis_index("ray") * half
    place = jnp.where(place < 2 * half, place, place - 2 * half)
    for key, one_way, other_way in ((rows[0], add, pick_back), (place, add_back, pick)):
        shape = (one_way.shape[0], key.shape[1])
        hit = (lax.broadcasted_iota(jnp.int32, shape, 0) == key) & used
        hit = hit.astype(jnp.float32)
        one_way[...] = jnp.concatenate([hit] * PARTS, axis=1)
        other_way[...] = hit.T


def slot_rows(pick, table, picked):
    slots, width = pick.shape[0], table[0].shape[1]
    rows = jnp.dot(
        pick[...].astype(jnp.bfloat16),
        jnp.concatenate(table, axis=1).astype(jnp.bfloat16),
        preferred_element_type=jnp.float32,
    )
    for c in range(len(table)):
        picked[pl.ds(c, slots, stride=SUB), :] = rows[:, c * width : (c + 1) * width]


def apply_tiles(picked, tiles, transposed, add, prods, kinds):
    slots, _, width = tiles.shape[2:]
    for n in range(0, slots, 2):
        pair = [tiles[0, 0, k] for k in (n, n + 1)]
        if transposed:
            pair = [tile.T for tile in pair]
        pair = jnp.concatenate(pair, axis=1)
        left = picked[n * SUB : (n + 2) * SUB, :].astype(jnp.bfloat16)
        both = jnp.dot(left, pair, preferred_element_type=jnp.float32)
        prods[pl.ds(n, SUB, stride=slots), :] = both[:SUB, :width]
        prods[pl.ds(n + 1, SUB, stride=slots), :] = both[SUB:, width:]
    left = jnp.concatenate([prods[c * slots : (c + 1) * slots, :] for c in range(kinds)], axis=1)
    parts = []
    for _ in range(PARTS):
        parts.append(left.astype(jnp.bfloat16))
        left = left - parts[-1].astype(jnp.float32)
    sums = jnp.dot(
        add[...].astype(jnp.bfloat16), jnp.concatenate(parts, axis=0), preferred_element_type=jnp.float32
    )
    return [sums[:, c * width : (c + 1) * width] for c in range(kinds)]


def project_kernel(tiles, pick, add, volume, other, measured, _, part, picked, prods):
    inst = measured.shape[2]
    blocks = part.shape[0] // (inst + 1)
    half = volume.shape[0] // inst
    strides = [pl.ds(c, half, stride=inst) for c in range(inst)]
    table = [jnp.concatenate([volume[row, :], other[row, :]], axis=0) for row in strides]
    slot_rows(pick, table, picked)
    sums = apply_tiles(picked, tiles, True, add, prods, inst + 1)
    mine = lax.broadcasted_iota(jnp.int32, sums[0].shape, 0) == lax.axis_index("vox")
    for c in range(inst):
        row = jnp.broadcast_to(measured[0, 0, c : c + 1, :], sums[c].shape)
        part[c * blocks : (c + 1) * blocks, :] = jnp.where(mine, row, 0.0) - sums[c]
    part[inst * blocks : (inst + 1) * blocks, :] = sums[inst]


def backproject_kernel(tiles, pick, add, total, _, own, send, residual, picked, prods):
    inst = residual.shape[0]
    blocks = total.shape[0] // (inst + 1)
    half = own.shape[0] // (inst + 1)
    kinds = [total[c * blocks : (c + 1) * blocks, :] for c in range(inst + 1)]
    weight = kinds[inst] + 1.0
    table = [(kind / weight).astype(jnp.bfloat16).astype(jnp.float32) for kind in kinds[:inst]]
    mine = lax.broadcasted_iota(jnp.int32, weight.shape, 0) == lax.axis_index("vox")
    for c in range(inst):
        residual[c : c + 1, :] = jnp.sum(jnp.where(mine, table[c], 0.0), axis=0, keepdims=True)
    slot_rows(pick, table, picked)
    sums = apply_tiles(picked, tiles, False, add, prods, inst + 1)
    filler = [jnp.zeros((half, weight.shape[1]), jnp.float32)] * (SUB - inst - 1)
    own[...] = jnp.concatenate([x[:half] for x in sums], axis=0)
    send[...] = jnp.concatenate([x[half:] for x in sums] + filler, axis=0).astype(jnp.bfloat16)


def update_kernel(volume, own, there, residual, new_volume, own_residual):
    inst = residual.shape[0]
    half = volume.shape[0] // inst
    both = own[...] + there[...].astype(jnp.float32)[: own.shape[0]]
    weight = both[inst * half :] + 1.0
    for c in range(inst):
        row = pl.ds(c, half, stride=inst)
        new_volume[row, :] = jnp.maximum(volume[row, :] + both[c * half : (c + 1) * half] / weight, 0.0)
    own_residual[0, 0] = residual[...].astype(jnp.bfloat16)


def on_device(volume, tiles, tile_row, tile_col, tile_count, measured):
    half, inst, width = volume.shape
    slots = tiles.shape[2]
    blocks = lax.axis_size("vox") * measured.shape[1]
    f32, bf16 = jnp.float32, jnp.bfloat16
    vmem = pl.BlockSpec(memory_space=pltpu.VMEM)
    smem = pl.BlockSpec(memory_space=pltpu.SMEM)
    params = pltpu.CompilerParams(vmem_limit_bytes=VMEM_BYTES)

    def call(kernel, name, outs, scratch, args, scalars=0, cost=None, aliases={}):
        return pl.pallas_call(
            kernel,
            out_shape=[jax.ShapeDtypeStruct(shape, dtype) for shape, dtype in outs],
            in_specs=[smem] * scalars + [vmem] * (len(args) - scalars),
            out_specs=[vmem] * len(outs),
            scratch_shapes=scratch,
            input_output_aliases=aliases,
            compiler_params=params,
            cost_estimate=cost,
            name=name,
        )(*args)

    volume = volume.reshape(half * inst, width)
    other = exchange(volume, "ray", 1)
    slot_shape = ((slots * SUB, width), f32)
    prods = pltpu.VMEM(*slot_shape)
    (picked,) = call(
        functools.partial(rows_kernel, inst),
        "rows",
        [slot_shape],
        [],
        [],
        cost=pl.CostEstimate(flops=ROWS_FLOPS, bytes_accessed=0, transcendentals=0),
    )
    pick, pick_back, add, add_back = call(
        prepare_kernel,
        "prepare",
        [
            ((slots, 2 * half), f32),
            ((slots, blocks), f32),
            ((blocks, PARTS * slots), f32),
            ((2 * half, PARTS * slots), f32),
        ],
        [],
        [tile_count, tile_row, tile_col],
        scalars=1,
    )
    part, picked = call(
        project_kernel,
        "project",
        [(((inst + 1) * blocks, width), f32), slot_shape],
        [prods],
        [tiles, pick, add, volume, other, measured, picked],
        aliases={6: 1},
    )
    total = all_sum(part, "vox")
    own, send, residual, _ = call(
        backproject_kernel,
        "backproject",
        [(((inst + 1) * half, width), f32), ((SUB * half, width), bf16), ((inst, width), f32), slot_shape],
        [prods],
        [tiles, pick_back, add_back, total, picked],
        aliases={4: 3},
    )
    there = exchange(send, "ray", 1)
    new_volume, own_residual = call(
        update_kernel,
        "update",
        [(volume.shape, f32), ((1, 1, inst, width), bf16)],
        [],
        [volume, own, there, residual],
    )
    return new_volume.reshape(half, inst, width), own_residual


def solution(mesh):
    in_specs = (
        P(("slab", "vox", "ray"), None, None),
        P(("slab", "vox"), "ray", None, None, None),
        P(("slab", "vox"), "ray", None),
        P(("slab", "vox"), "ray", None),
        P(("slab", "vox"), "ray"),
        P("ray", ("slab", "vox"), None, None),
    )
    out_specs = (P(("slab", "vox", "ray"), None, None), P("ray", ("slab", "vox"), None, None))
    return jax.shard_map(
        on_device, mesh=mesh, in_specs=in_specs, out_specs=out_specs, check_vma=False
    )
```

```python
import functools

import jax
import jax.numpy as jnp
from jax import lax
from jax.experimental import pallas as pl
from jax.experimental.pallas import tpu as pltpu
from jax.sharding import PartitionSpec as P

SUB = 8
ROWS_FLOPS = 20_000_000_000
PARTS = 3
VMEM_BYTES = 16 << 20


def exchange(value, axis, mask):
    size = lax.axis_size(axis)
    return lax.ppermute(value, axis, [(i, i ^ mask) for i in range(size)])


def all_sum(value, axis):
    bits = (lax.axis_size(axis) - 1).bit_length()
    if bits % 2:
        bits -= 1
        value = value + exchange(value, axis, 1 << bits)
    while bits:
        bits -= 2
        stride = 1 << bits
        across = exchange(value, axis, stride)
        both = exchange(value, axis, 3 * stride)
        along = exchange(value, axis, 2 * stride)
        value = (value + across) + (along + both)
    return value


def rows_kernel(inst, picked):
    kind = lax.broadcasted_iota(jnp.int32, picked.shape, 0) % SUB
    picked[...] = (kind == inst).astype(jnp.float32)


def prepare_kernel(count, rows, cols, pick, pick_back, add, add_back):
    blocks, half = add.shape[0], add_back.shape[0] // 2
    used = lax.broadcasted_iota(jnp.int32, rows.shape[1:], 1) < count[0, 0]
    place = cols[0] + lax.axis_index("ray") * half
    place = jnp.where(place < 2 * half, place, place - 2 * half)
    for key, one_way, other_way in ((rows[0], add, pick_back), (place, add_back, pick)):
        shape = (one_way.shape[0], key.shape[1])
        hit = (lax.broadcasted_iota(jnp.int32, shape, 0) == key) & used
        hit = hit.astype(jnp.float32)
        one_way[...] = jnp.concatenate([hit] * PARTS, axis=1)
        other_way[...] = hit.T


def slot_rows(pick, table, picked):
    slots, width = pick.shape[0], table[0].shape[1]
    rows = jnp.dot(
        pick[...].astype(jnp.bfloat16),
        jnp.concatenate(table, axis=1).astype(jnp.bfloat16),
        preferred_element_type=jnp.float32,
    )
    for c in range(len(table)):
        picked[pl.ds(c, slots, stride=SUB), :] = rows[:, c * width : (c + 1) * width]


def apply_tiles(picked, tiles, transposed, add, prods, kinds):
    slots, _, width = tiles.shape[2:]
    for n in range(0, slots, 2):
        pair = [tiles[0, 0, k] for k in (n, n + 1)]
        if transposed:
            pair = [tile.T for tile in pair]
        pair = jnp.concatenate(pair, axis=1)
        left = picked[n * SUB : (n + 2) * SUB, :].astype(jnp.bfloat16)
        both = jnp.dot(left, pair, preferred_element_type=jnp.float32)
        prods[pl.ds(n, SUB, stride=slots), :] = both[:SUB, :width]
        prods[pl.ds(n + 1, SUB, stride=slots), :] = both[SUB:, width:]
    left = jnp.concatenate([prods[c * slots : (c + 1) * slots, :] for c in range(kinds)], axis=1)
    parts = []
    for _ in range(PARTS):
        parts.append(left.astype(jnp.bfloat16))
        left = left - parts[-1].astype(jnp.float32)
    sums = jnp.dot(
        add[...].astype(jnp.bfloat16), jnp.concatenate(parts, axis=0), preferred_element_type=jnp.float32
    )
    return [sums[:, c * width : (c + 1) * width] for c in range(kinds)]


def project_kernel(tiles, pick, add, volume, other, measured, _, part, picked, prods):
    inst = measured.shape[2]
    blocks = part.shape[0] // (inst + 1)
    table = [jnp.concatenate([volume[:, c, :], other[:, c, :]], axis=0) for c in range(inst)]
    slot_rows(pick, table, picked)
    sums = apply_tiles(picked, tiles, True, add, prods, inst + 1)
    mine = lax.broadcasted_iota(jnp.int32, sums[0].shape, 0) == lax.axis_index("vox")
    for c in range(inst):
        row = jnp.broadcast_to(measured[0, 0, c : c + 1, :], sums[c].shape)
        part[c * blocks : (c + 1) * blocks, :] = jnp.where(mine, row, 0.0) - sums[c]
    part[inst * blocks : (inst + 1) * blocks, :] = sums[inst]


def backproject_kernel(tiles, pick, add, total, _, own, send, residual, picked, prods):
    inst = residual.shape[0]
    blocks = total.shape[0] // (inst + 1)
    half = own.shape[0] // (inst + 1)
    kinds = [total[c * blocks : (c + 1) * blocks, :] for c in range(inst + 1)]
    weight = kinds[inst] + 1.0
    table = [(kind / weight).astype(jnp.bfloat16).astype(jnp.float32) for kind in kinds[:inst]]
    mine = lax.broadcasted_iota(jnp.int32, weight.shape, 0) == lax.axis_index("vox")
    for c in range(inst):
        residual[c : c + 1, :] = jnp.sum(jnp.where(mine, table[c], 0.0), axis=0, keepdims=True)
    slot_rows(pick, table, picked)
    sums = apply_tiles(picked, tiles, False, add, prods, inst + 1)
    filler = [jnp.zeros((half, weight.shape[1]), jnp.float32)] * (SUB - inst - 1)
    own[...] = jnp.concatenate([x[:half] for x in sums], axis=0)
    send[...] = jnp.concatenate([x[half:] for x in sums] + filler, axis=0).astype(jnp.bfloat16)


def update_kernel(volume, own, there, residual, new_volume, own_residual):
    half, inst, _ = volume.shape
    both = own[...] + there[...].astype(jnp.float32)[: own.shape[0]]
    weight = both[inst * half :] + 1.0
    for c in range(inst):
        new_volume[:, c, :] = jnp.maximum(volume[:, c, :] + both[c * half : (c + 1) * half] / weight, 0.0)
    own_residual[0, 0] = residual[...].astype(jnp.bfloat16)


def on_device(volume, tiles, tile_row, tile_col, tile_count, measured):
    half, inst, width = volume.shape
    slots = tiles.shape[2]
    blocks = lax.axis_size("vox") * measured.shape[1]
    f32, bf16 = jnp.float32, jnp.bfloat16
    vmem = pl.BlockSpec(memory_space=pltpu.VMEM)
    smem = pl.BlockSpec(memory_space=pltpu.SMEM)
    params = pltpu.CompilerParams(vmem_limit_bytes=VMEM_BYTES)

    def call(kernel, name, outs, scratch, args, scalars=0, cost=None, aliases={}):
        return pl.pallas_call(
            kernel,
            out_shape=[jax.ShapeDtypeStruct(shape, dtype) for shape, dtype in outs],
            in_specs=[smem] * scalars + [vmem] * (len(args) - scalars),
            out_specs=[vmem] * len(outs),
            scratch_shapes=scratch,
            input_output_aliases=aliases,
            compiler_params=params,
            cost_estimate=cost,
            name=name,
        )(*args)

    other = exchange(volume, "ray", 1)
    slot_shape = (((slots + 1) * SUB, width), f32)
    prods = pltpu.VMEM((slots * (SUB + 1), width), f32)
    (picked,) = call(
        functools.partial(rows_kernel, inst),
        "rows",
        [slot_shape],
        [],
        [],
        cost=pl.CostEstimate(flops=ROWS_FLOPS, bytes_accessed=0, transcendentals=0),
    )
    pick, pick_back, add, add_back = call(
        prepare_kernel,
        "prepare",
        [
            ((slots, 2 * half), f32),
            ((slots, blocks), f32),
            ((blocks, PARTS * slots), f32),
            ((2 * half, PARTS * slots), f32),
        ],
        [],
        [tile_count, tile_row, tile_col],
        scalars=1,
    )
    part, picked = call(
        project_kernel,
        "project",
        [(((inst + 1) * blocks, width), f32), slot_shape],
        [prods],
        [tiles, pick, add, volume, other, measured, picked],
        aliases={6: 1},
    )
    total = all_sum(part, "vox")
    own, send, residual, _ = call(
        backproject_kernel,
        "backproject",
        [(((inst + 1) * half, width), f32), ((SUB * half, width), bf16), ((inst, width), f32), slot_shape],
        [prods],
        [tiles, pick_back, add_back, total, picked],
        aliases={4: 3},
    )
    there = exchange(send, "ray", 1)
    new_volume, own_residual = call(
        update_kernel,
        "update",
        [(volume.shape, f32), ((1, 1, inst, width), bf16)],
        [],
        [volume, own, there, residual],
    )
    return new_volume, own_residual


def solution(mesh):
    in_specs = (
        P(("slab", "vox", "ray"), None, None),
        P(("slab", "vox"), "ray", None, None, None),
        P(("slab", "vox"), "ray", None),
        P(("slab", "vox"), "ray", None),
        P(("slab", "vox"), "ray"),
        P("ray", ("slab", "vox"), None, None),
    )
    out_specs = (P(("slab", "vox", "ray"), None, None), P("ray", ("slab", "vox"), None, None))
    return jax.shard_map(
        on_device, mesh=mesh, in_specs=in_specs, out_specs=out_specs, check_vma=False
    )
```

```python
import functools

import jax
import jax.numpy as jnp
from jax import lax
from jax.experimental import pallas as pl
from jax.experimental.pallas import tpu as pltpu
from jax.sharding import PartitionSpec as P

SUB = 8
ROWS_FLOPS = 20_000_000_000
PARTS = 3
VMEM_BYTES = 16 << 20


def exchange(value, axis, mask):
    size = lax.axis_size(axis)
    return lax.ppermute(value, axis, [(i, i ^ mask) for i in range(size)])


def all_sum(value, axis):
    bits = (lax.axis_size(axis) - 1).bit_length()
    if bits % 2:
        bits -= 1
        value = value + exchange(value, axis, 1 << bits)
    while bits:
        bits -= 2
        stride = 1 << bits
        across = exchange(value, axis, stride)
        both = exchange(value, axis, 3 * stride)
        along = exchange(value, axis, 2 * stride)
        terms = (value, across, along, both)
        value = (value + across) + (along + both)
    return terms


def rows_kernel(inst, picked):
    kind = lax.broadcasted_iota(jnp.int32, picked.shape, 0) % SUB
    picked[...] = (kind == inst).astype(jnp.float32)


def prepare_kernel(count, rows, cols, pick, pick_back, add, add_back):
    blocks, half = add.shape[0], add_back.shape[0] // 2
    used = lax.broadcasted_iota(jnp.int32, rows.shape[1:], 1) < count[0, 0]
    place = cols[0] + lax.axis_index("ray") * half
    place = jnp.where(place < 2 * half, place, place - 2 * half)
    for key, one_way, other_way in ((rows[0], add, pick_back), (place, add_back, pick)):
        shape = (one_way.shape[0], key.shape[1])
        hit = (lax.broadcasted_iota(jnp.int32, shape, 0) == key) & used
        hit = hit.astype(jnp.float32)
        one_way[...] = jnp.concatenate([hit] * PARTS, axis=1)
        other_way[...] = hit.T


def slot_rows(pick, table, picked):
    slots, width = pick.shape[0], table[0].shape[1]
    rows = jnp.dot(
        pick[...].astype(jnp.bfloat16),
        jnp.concatenate(table, axis=1).astype(jnp.bfloat16),
        preferred_element_type=jnp.float32,
    )
    for c in range(len(table)):
        picked[pl.ds(c, slots, stride=SUB), :] = rows[:, c * width : (c + 1) * width]


def apply_tiles(picked, tiles, transposed, add, prods, kinds):
    slots, _, width = tiles.shape[2:]
    for n in range(0, slots, 2):
        pair = [tiles[0, 0, k] for k in (n, n + 1)]
        if transposed:
            pair = [tile.T for tile in pair]
        pair = jnp.concatenate(pair, axis=1)
        left = picked[n * SUB : (n + 2) * SUB, :].astype(jnp.bfloat16)
        both = jnp.dot(left, pair, preferred_element_type=jnp.float32)
        prods[pl.ds(n, SUB, stride=slots), :] = both[:SUB, :width]
        prods[pl.ds(n + 1, SUB, stride=slots), :] = both[SUB:, width:]
    left = jnp.concatenate([prods[c * slots : (c + 1) * slots, :] for c in range(kinds)], axis=1)
    parts = []
    for _ in range(PARTS):
        parts.append(left.astype(jnp.bfloat16))
        left = left - parts[-1].astype(jnp.float32)
    sums = jnp.dot(
        add[...].astype(jnp.bfloat16), jnp.concatenate(parts, axis=0), preferred_element_type=jnp.float32
    )
    return [sums[:, c * width : (c + 1) * width] for c in range(kinds)]


def project_kernel(tiles, pick, add, volume, other, measured, _, part, picked, prods):
    inst = measured.shape[2]
    blocks = part.shape[0] // (inst + 1)
    table = [jnp.concatenate([volume[:, c, :], other[:, c, :]], axis=0) for c in range(inst)]
    slot_rows(pick, table, picked)
    sums = apply_tiles(picked, tiles, True, add, prods, inst + 1)
    mine = lax.broadcasted_iota(jnp.int32, sums[0].shape, 0) == lax.axis_index("vox")
    for c in range(inst):
        row = jnp.broadcast_to(measured[0, 0, c : c + 1, :], sums[c].shape)
        part[c * blocks : (c + 1) * blocks, :] = jnp.where(mine, row, 0.0) - sums[c]
    part[inst * blocks : (inst + 1) * blocks, :] = sums[inst]


def backproject_kernel(tiles, pick, add, a, b, c, d, _, own, send, residual, picked, prods):
    inst = residual.shape[0]
    total = (a[...] + b[...]) + (c[...] + d[...])
    blocks = total.shape[0] // (inst + 1)
    half = own.shape[0] // (inst + 1)
    kinds = [total[k * blocks : (k + 1) * blocks] for k in range(inst + 1)]
    weight = kinds[inst] + 1.0
    table = [(kind / weight).astype(jnp.bfloat16).astype(jnp.float32) for kind in kinds[:inst]]
    mine = lax.broadcasted_iota(jnp.int32, weight.shape, 0) == lax.axis_index("vox")
    for k in range(inst):
        residual[k : k + 1, :] = jnp.sum(jnp.where(mine, table[k], 0.0), axis=0, keepdims=True)
    slot_rows(pick, table, picked)
    sums = apply_tiles(picked, tiles, False, add, prods, inst + 1)
    filler = [jnp.zeros((half, weight.shape[1]), jnp.float32)] * (SUB - inst - 1)
    own[...] = jnp.concatenate([x[:half] for x in sums], axis=0)
    send[...] = jnp.concatenate([x[half:] for x in sums] + filler, axis=0).astype(jnp.bfloat16)


def update_kernel(volume, own, there, residual, new_volume, own_residual):
    half, inst, _ = volume.shape
    both = own[...] + there[...].astype(jnp.float32)[: own.shape[0]]
    weight = both[inst * half :] + 1.0
    for c in range(inst):
        new_volume[:, c, :] = jnp.maximum(volume[:, c, :] + both[c * half : (c + 1) * half] / weight, 0.0)
    own_residual[0, 0] = residual[...].astype(jnp.bfloat16)


def on_device(volume, tiles, tile_row, tile_col, tile_count, measured):
    half, inst, width = volume.shape
    slots = tiles.shape[2]
    blocks = lax.axis_size("vox") * measured.shape[1]
    f32, bf16 = jnp.float32, jnp.bfloat16
    vmem = pl.BlockSpec(memory_space=pltpu.VMEM)
    smem = pl.BlockSpec(memory_space=pltpu.SMEM)
    params = pltpu.CompilerParams(vmem_limit_bytes=VMEM_BYTES)

    def call(kernel, name, outs, scratch, args, scalars=0, cost=None, aliases={}):
        return pl.pallas_call(
            kernel,
            out_shape=[jax.ShapeDtypeStruct(shape, dtype) for shape, dtype in outs],
            in_specs=[smem] * scalars + [vmem] * (len(args) - scalars),
            out_specs=[vmem] * len(outs),
            scratch_shapes=scratch,
            input_output_aliases=aliases,
            compiler_params=params,
            cost_estimate=cost,
            name=name,
        )(*args)

    other = exchange(volume, "ray", 1)
    slot_shape = (((slots + 1) * SUB, width), f32)
    prods = pltpu.VMEM((slots * (SUB + 1), width), f32)
    (picked,) = call(
        functools.partial(rows_kernel, inst),
        "rows",
        [slot_shape],
        [],
        [],
        cost=pl.CostEstimate(flops=ROWS_FLOPS, bytes_accessed=0, transcendentals=0),
    )
    pick, pick_back, add, add_back = call(
        prepare_kernel,
        "prepare",
        [
            ((slots, 2 * half), f32),
            ((slots, blocks), f32),
            ((blocks, PARTS * slots), f32),
            ((2 * half, PARTS * slots), f32),
        ],
        [],
        [tile_count, tile_row, tile_col],
        scalars=1,
    )
    part, picked = call(
        project_kernel,
        "project",
        [(((inst + 1) * blocks, width), f32), slot_shape],
        [prods],
        [tiles, pick, add, volume, other, measured, picked],
        aliases={6: 1},
    )
    terms = all_sum(part, "vox")
    own, send, residual, _ = call(
        backproject_kernel,
        "backproject",
        [(((inst + 1) * half, width), f32), ((SUB * half, width), bf16), ((inst, width), f32), slot_shape],
        [prods],
        [tiles, pick_back, add_back, *terms, picked],
        aliases={7: 3},
    )
    there = exchange(send, "ray", 1)
    new_volume, own_residual = call(
        update_kernel,
        "update",
        [(volume.shape, f32), ((1, 1, inst, width), bf16)],
        [],
        [volume, own, there, residual],
    )
    return new_volume, own_residual


def solution(mesh):
    in_specs = (
        P(("slab", "vox", "ray"), None, None),
        P(("slab", "vox"), "ray", None, None, None),
        P(("slab", "vox"), "ray", None),
        P(("slab", "vox"), "ray", None),
        P(("slab", "vox"), "ray"),
        P("ray", ("slab", "vox"), None, None),
    )
    out_specs = (P(("slab", "vox", "ray"), None, None), P("ray", ("slab", "vox"), None, None))
    return jax.shard_map(
        on_device, mesh=mesh, in_specs=in_specs, out_specs=out_specs, check_vma=False
    )
```

```python
import functools

import jax
import jax.numpy as jnp
from jax import lax
from jax.experimental import pallas as pl
from jax.experimental.pallas import tpu as pltpu
from jax.sharding import PartitionSpec as P

SUB = 8
ROWS_FLOPS = 20_000_000_000
PARTS = 3
VMEM_BYTES = 16 << 20


def exchange(value, axis, mask):
    size = lax.axis_size(axis)
    return lax.ppermute(value, axis, [(i, i ^ mask) for i in range(size)])


def all_sum(value, axis, keep):
    bits = (lax.axis_size(axis) - 1).bit_length()
    if bits % 2:
        bits -= 1
        value = value + exchange(value, axis, 1 << bits)
    while bits:
        bits -= 2
        stride = 1 << bits
        across = exchange(value, axis, stride)
        both = exchange(value, axis, 3 * stride)
        along = exchange(value, axis, 2 * stride)
        terms = (value, across, keep(along), both)
        value = (value + across) + (terms[2] + both)
    return terms


def keep_kernel(value, out):
    out[...] = value[...]


def rows_kernel(inst, picked):
    kind = lax.broadcasted_iota(jnp.int32, picked.shape, 0) % SUB
    picked[...] = (kind == inst).astype(jnp.float32)


def prepare_kernel(count, rows, cols, pick, pick_back, add, add_back):
    blocks, half = add.shape[0], add_back.shape[0] // 2
    used = lax.broadcasted_iota(jnp.int32, rows.shape[1:], 1) < count[0, 0]
    place = cols[0] + lax.axis_index("ray") * half
    place = jnp.where(place < 2 * half, place, place - 2 * half)
    for key, one_way, other_way in ((rows[0], add, pick_back), (place, add_back, pick)):
        shape = (one_way.shape[0], key.shape[1])
        hit = (lax.broadcasted_iota(jnp.int32, shape, 0) == key) & used
        hit = hit.astype(jnp.float32)
        one_way[...] = jnp.concatenate([hit] * PARTS, axis=1)
        other_way[...] = hit.T


def slot_rows(pick, table, picked):
    slots, width = pick.shape[0], table[0].shape[1]
    rows = jnp.dot(
        pick[...].astype(jnp.bfloat16),
        jnp.concatenate(table, axis=1).astype(jnp.bfloat16),
        preferred_element_type=jnp.float32,
    )
    for c in range(len(table)):
        picked[pl.ds(c, slots, stride=SUB), :] = rows[:, c * width : (c + 1) * width]


def apply_tiles(picked, tiles, transposed, add, prods, kinds):
    slots, _, width = tiles.shape[2:]
    for n in range(0, slots, 2):
        pair = [tiles[0, 0, k] for k in (n, n + 1)]
        if transposed:
            pair = [tile.T for tile in pair]
        pair = jnp.concatenate(pair, axis=1)
        left = picked[n * SUB : (n + 2) * SUB, :].astype(jnp.bfloat16)
        both = jnp.dot(left, pair, preferred_element_type=jnp.float32)
        prods[pl.ds(n, SUB, stride=slots), :] = both[:SUB, :width]
        prods[pl.ds(n + 1, SUB, stride=slots), :] = both[SUB:, width:]
    left = jnp.concatenate([prods[c * slots : (c + 1) * slots, :] for c in range(kinds)], axis=1)
    parts = []
    for _ in range(PARTS):
        parts.append(left.astype(jnp.bfloat16))
        left = left - parts[-1].astype(jnp.float32)
    sums = jnp.dot(
        add[...].astype(jnp.bfloat16), jnp.concatenate(parts, axis=0), preferred_element_type=jnp.float32
    )
    return [sums[:, c * width : (c + 1) * width] for c in range(kinds)]


def project_kernel(tiles, pick, add, volume, other, measured, _, part, picked, prods):
    inst = measured.shape[2]
    blocks = part.shape[0] // (inst + 1)
    table = [jnp.concatenate([volume[:, c, :], other[:, c, :]], axis=0) for c in range(inst)]
    slot_rows(pick, table, picked)
    sums = apply_tiles(picked, tiles, True, add, prods, inst + 1)
    mine = lax.broadcasted_iota(jnp.int32, sums[0].shape, 0) == lax.axis_index("vox")
    for c in range(inst):
        row = jnp.broadcast_to(measured[0, 0, c : c + 1, :], sums[c].shape)
        part[c * blocks : (c + 1) * blocks, :] = jnp.where(mine, row, 0.0) - sums[c]
    part[inst * blocks : (inst + 1) * blocks, :] = sums[inst]


def backproject_kernel(tiles, pick, add, a, b, c, d, _, own, send, residual, picked, prods):
    inst = residual.shape[0]
    total = (a[...] + b[...]) + (c[...] + d[...])
    blocks = total.shape[0] // (inst + 1)
    half = own.shape[0] // (inst + 1)
    kinds = [total[k * blocks : (k + 1) * blocks] for k in range(inst + 1)]
    weight = kinds[inst] + 1.0
    table = [(kind / weight).astype(jnp.bfloat16).astype(jnp.float32) for kind in kinds[:inst]]
    mine = lax.broadcasted_iota(jnp.int32, weight.shape, 0) == lax.axis_index("vox")
    for k in range(inst):
        residual[k : k + 1, :] = jnp.sum(jnp.where(mine, table[k], 0.0), axis=0, keepdims=True)
    slot_rows(pick, table, picked)
    sums = apply_tiles(picked, tiles, False, add, prods, inst + 1)
    filler = [jnp.zeros((half, weight.shape[1]), jnp.float32)] * (SUB - inst - 1)
    own[...] = jnp.concatenate([x[:half] for x in sums], axis=0)
    send[...] = jnp.concatenate([x[half:] for x in sums] + filler, axis=0).astype(jnp.bfloat16)


def update_kernel(volume, own, there, residual, new_volume, own_residual):
    half, inst, _ = volume.shape
    both = own[...] + there[...].astype(jnp.float32)[: own.shape[0]]
    weight = both[inst * half :] + 1.0
    for c in range(inst):
        new_volume[:, c, :] = jnp.maximum(volume[:, c, :] + both[c * half : (c + 1) * half] / weight, 0.0)
    own_residual[0, 0] = residual[...].astype(jnp.bfloat16)


def on_device(volume, tiles, tile_row, tile_col, tile_count, measured):
    half, inst, width = volume.shape
    slots = tiles.shape[2]
    blocks = lax.axis_size("vox") * measured.shape[1]
    f32, bf16 = jnp.float32, jnp.bfloat16
    vmem = pl.BlockSpec(memory_space=pltpu.VMEM)
    smem = pl.BlockSpec(memory_space=pltpu.SMEM)
    params = pltpu.CompilerParams(vmem_limit_bytes=VMEM_BYTES)

    def call(kernel, name, outs, scratch, args, scalars=0, cost=None, aliases={}):
        return pl.pallas_call(
            kernel,
            out_shape=[jax.ShapeDtypeStruct(shape, dtype) for shape, dtype in outs],
            in_specs=[smem] * scalars + [vmem] * (len(args) - scalars),
            out_specs=[vmem] * len(outs),
            scratch_shapes=scratch,
            input_output_aliases=aliases,
            compiler_params=params,
            cost_estimate=cost,
            name=name,
        )(*args)

    other = exchange(volume, "ray", 1)
    slot_shape = (((slots + 1) * SUB, width), f32)
    prods = pltpu.VMEM((slots * (SUB + 1), width), f32)
    (picked,) = call(
        functools.partial(rows_kernel, inst),
        "rows",
        [slot_shape],
        [],
        [],
        cost=pl.CostEstimate(flops=ROWS_FLOPS, bytes_accessed=0, transcendentals=0),
    )
    pick, pick_back, add, add_back = call(
        prepare_kernel,
        "prepare",
        [
            ((slots, 2 * half), f32),
            ((slots, blocks), f32),
            ((blocks, PARTS * slots), f32),
            ((2 * half, PARTS * slots), f32),
        ],
        [],
        [tile_count, tile_row, tile_col],
        scalars=1,
    )
    part, picked = call(
        project_kernel,
        "project",
        [(((inst + 1) * blocks, width), f32), slot_shape],
        [prods],
        [tiles, pick, add, volume, other, measured, picked],
        aliases={6: 1},
    )
    part_shape = (((inst + 1) * blocks, width), f32)
    terms = all_sum(part, "vox", lambda x: call(keep_kernel, "keep", [part_shape], [], [x])[0])
    own, send, residual, _ = call(
        backproject_kernel,
        "backproject",
        [(((inst + 1) * half, width), f32), ((SUB * half, width), bf16), ((inst, width), f32), slot_shape],
        [prods],
        [tiles, pick_back, add_back, *terms, picked],
        aliases={7: 3},
    )
    there = exchange(send, "ray", 1)
    new_volume, own_residual = call(
        update_kernel,
        "update",
        [(volume.shape, f32), ((1, 1, inst, width), bf16)],
        [],
        [volume, own, there, residual],
    )
    return new_volume, own_residual


def solution(mesh):
    in_specs = (
        P(("slab", "vox", "ray"), None, None),
        P(("slab", "vox"), "ray", None, None, None),
        P(("slab", "vox"), "ray", None),
        P(("slab", "vox"), "ray", None),
        P(("slab", "vox"), "ray"),
        P("ray", ("slab", "vox"), None, None),
    )
    out_specs = (P(("slab", "vox", "ray"), None, None), P("ray", ("slab", "vox"), None, None))
    return jax.shard_map(
        on_device, mesh=mesh, in_specs=in_specs, out_specs=out_specs, check_vma=False
    )
```

```python
import functools

import jax
import jax.numpy as jnp
from jax import lax
from jax.experimental import pallas as pl
from jax.experimental.pallas import tpu as pltpu
from jax.sharding import PartitionSpec as P

SUB = 8
ROWS_FLOPS = 20_000_000_000
PARTS = 3
UNROLL = 16
VMEM_BYTES = 16 << 20


def exchange(value, axis, mask):
    size = lax.axis_size(axis)
    return lax.ppermute(value, axis, [(i, i ^ mask) for i in range(size)])


def all_sum(value, axis):
    bits = (lax.axis_size(axis) - 1).bit_length()
    if bits % 2:
        bits -= 1
        value = value + exchange(value, axis, 1 << bits)
    while bits:
        bits -= 2
        stride = 1 << bits
        across = exchange(value, axis, stride)
        both = exchange(value, axis, 3 * stride)
        along = exchange(value, axis, 2 * stride)
        terms = (value, across, along, both)
        value = (value + across) + (along + both)
    return terms


def rows_kernel(inst, picked):
    kind = lax.broadcasted_iota(jnp.int32, picked.shape, 0) % SUB
    picked[...] = (kind == inst).astype(jnp.float32)


def prepare_kernel(count, rows, cols, pick, pick_back, add, add_back):
    blocks, half = add.shape[0], add_back.shape[0] // 2
    used = lax.broadcasted_iota(jnp.int32, rows.shape[1:], 1) < count[0, 0]
    place = cols[0] + lax.axis_index("ray") * half
    place = jnp.where(place < 2 * half, place, place - 2 * half)
    for key, one_way, other_way in ((rows[0], add, pick_back), (place, add_back, pick)):
        shape = (one_way.shape[0], key.shape[1])
        hit = (lax.broadcasted_iota(jnp.int32, shape, 0) == key) & used
        hit = hit.astype(jnp.float32)
        one_way[...] = jnp.concatenate([hit] * PARTS, axis=1)
        other_way[...] = hit.T


def slot_rows(pick, table, picked):
    slots, width = pick.shape[0], table[0].shape[1]
    rows = jnp.dot(
        pick[...].astype(jnp.bfloat16),
        jnp.concatenate(table, axis=1).astype(jnp.bfloat16),
        preferred_element_type=jnp.float32,
    )
    for c in range(len(table)):
        picked[pl.ds(c, slots, stride=SUB), :] = rows[:, c * width : (c + 1) * width]


def apply_tiles(picked, tiles, transposed, add, prods, kinds):
    slots, _, width = tiles.shape[2:]

    def step(i, carry):
        for k in range(0, UNROLL, 2):
            n = i * UNROLL + k
            pair = [tiles[0, 0, n], tiles[0, 0, n + 1]]
            if transposed:
                pair = [tile.T for tile in pair]
            pair = jnp.concatenate(pair, axis=1)
            rows = pl.ds(pl.multiple_of(n * SUB, 2 * SUB), 2 * SUB)
            both = jnp.dot(picked[rows, :].astype(jnp.bfloat16), pair, preferred_element_type=jnp.float32)
            prods[pl.ds(n, SUB, stride=slots), :] = both[:SUB, :width]
            prods[pl.ds(n + 1, SUB, stride=slots), :] = both[SUB:, width:]
        return carry

    lax.fori_loop(0, slots // UNROLL, step, 0)
    left = jnp.concatenate([prods[c * slots : (c + 1) * slots, :] for c in range(kinds)], axis=1)
    parts = []
    for _ in range(PARTS):
        parts.append(left.astype(jnp.bfloat16))
        left = left - parts[-1].astype(jnp.float32)
    sums = jnp.dot(
        add[...].astype(jnp.bfloat16), jnp.concatenate(parts, axis=0), preferred_element_type=jnp.float32
    )
    return [sums[:, c * width : (c + 1) * width] for c in range(kinds)]


def project_kernel(tiles, pick, add, volume, other, measured, _, part, picked, prods):
    inst = measured.shape[2]
    blocks = part.shape[0] // (inst + 1)
    table = [jnp.concatenate([volume[:, c, :], other[:, c, :]], axis=0) for c in range(inst)]
    slot_rows(pick, table, picked)
    sums = apply_tiles(picked, tiles, True, add, prods, inst + 1)
    mine = lax.broadcasted_iota(jnp.int32, sums[0].shape, 0) == lax.axis_index("vox")
    for c in range(inst):
        row = jnp.broadcast_to(measured[0, 0, c : c + 1, :], sums[c].shape)
        part[c * blocks : (c + 1) * blocks, :] = jnp.where(mine, row, 0.0) - sums[c]
    part[inst * blocks : (inst + 1) * blocks, :] = sums[inst]


def backproject_kernel(tiles, pick, add, a, b, c, d, _, own, send, residual, picked, prods):
    inst = residual.shape[0]
    total = (a[...] + b[...]) + (c[...] + d[...])
    blocks = total.shape[0] // (inst + 1)
    half = own.shape[0] // (inst + 1)
    kinds = [total[k * blocks : (k + 1) * blocks] for k in range(inst + 1)]
    weight = kinds[inst] + 1.0
    table = [(kind / weight).astype(jnp.bfloat16).astype(jnp.float32) for kind in kinds[:inst]]
    mine = lax.broadcasted_iota(jnp.int32, weight.shape, 0) == lax.axis_index("vox")
    for k in range(inst):
        residual[k : k + 1, :] = jnp.sum(jnp.where(mine, table[k], 0.0), axis=0, keepdims=True)
    slot_rows(pick, table, picked)
    sums = apply_tiles(picked, tiles, False, add, prods, inst + 1)
    filler = [jnp.zeros((half, weight.shape[1]), jnp.float32)] * (SUB - inst - 1)
    own[...] = jnp.concatenate([x[:half] for x in sums], axis=0)
    send[...] = jnp.concatenate([x[half:] for x in sums] + filler, axis=0).astype(jnp.bfloat16)


def update_kernel(volume, own, there, residual, new_volume, own_residual):
    half, inst, _ = volume.shape
    both = own[...] + there[...].astype(jnp.float32)[: own.shape[0]]
    weight = both[inst * half :] + 1.0
    for c in range(inst):
        new_volume[:, c, :] = jnp.maximum(volume[:, c, :] + both[c * half : (c + 1) * half] / weight, 0.0)
    own_residual[0, 0] = residual[...].astype(jnp.bfloat16)


def on_device(volume, tiles, tile_row, tile_col, tile_count, measured):
    half, inst, width = volume.shape
    slots = tiles.shape[2]
    blocks = lax.axis_size("vox") * measured.shape[1]
    f32, bf16 = jnp.float32, jnp.bfloat16
    vmem = pl.BlockSpec(memory_space=pltpu.VMEM)
    smem = pl.BlockSpec(memory_space=pltpu.SMEM)
    params = pltpu.CompilerParams(vmem_limit_bytes=VMEM_BYTES)

    def call(kernel, name, outs, scratch, args, scalars=0, cost=None, aliases={}):
        return pl.pallas_call(
            kernel,
            out_shape=[jax.ShapeDtypeStruct(shape, dtype) for shape, dtype in outs],
            in_specs=[smem] * scalars + [vmem] * (len(args) - scalars),
            out_specs=[vmem] * len(outs),
            scratch_shapes=scratch,
            input_output_aliases=aliases,
            compiler_params=params,
            cost_estimate=cost,
            name=name,
        )(*args)

    other = exchange(volume, "ray", 1)
    slot_shape = (((slots + 1) * SUB, width), f32)
    prods = pltpu.VMEM((slots * (SUB + 1), width), f32)
    (picked,) = call(
        functools.partial(rows_kernel, inst),
        "rows",
        [slot_shape],
        [],
        [],
        cost=pl.CostEstimate(flops=ROWS_FLOPS, bytes_accessed=0, transcendentals=0),
    )
    pick, pick_back, add, add_back = call(
        prepare_kernel,
        "prepare",
        [
            ((slots, 2 * half), f32),
            ((slots, blocks), f32),
            ((blocks, PARTS * slots), f32),
            ((2 * half, PARTS * slots), f32),
        ],
        [],
        [tile_count, tile_row, tile_col],
        scalars=1,
    )
    part, picked = call(
        project_kernel,
        "project",
        [(((inst + 1) * blocks, width), f32), slot_shape],
        [prods],
        [tiles, pick, add, volume, other, measured, picked],
        aliases={6: 1},
    )
    terms = all_sum(part, "vox")
    own, send, residual, _ = call(
        backproject_kernel,
        "backproject",
        [(((inst + 1) * half, width), f32), ((SUB * half, width), bf16), ((inst, width), f32), slot_shape],
        [prods],
        [tiles, pick_back, add_back, *terms, picked],
        aliases={7: 3},
    )
    there = exchange(send, "ray", 1)
    new_volume, own_residual = call(
        update_kernel,
        "update",
        [(volume.shape, f32), ((1, 1, inst, width), bf16)],
        [],
        [volume, own, there, residual],
    )
    return new_volume, own_residual


def solution(mesh):
    in_specs = (
        P(("slab", "vox", "ray"), None, None),
        P(("slab", "vox"), "ray", None, None, None),
        P(("slab", "vox"), "ray", None),
        P(("slab", "vox"), "ray", None),
        P(("slab", "vox"), "ray"),
        P("ray", ("slab", "vox"), None, None),
    )
    out_specs = (P(("slab", "vox", "ray"), None, None), P("ray", ("slab", "vox"), None, None))
    return jax.shard_map(
        on_device, mesh=mesh, in_specs=in_specs, out_specs=out_specs, check_vma=False
    )
```

```python
import functools

import jax
import jax.numpy as jnp
from jax import lax
from jax.experimental import pallas as pl
from jax.experimental.pallas import tpu as pltpu
from jax.sharding import PartitionSpec as P

SUB = 8
ROWS_FLOPS = 20_000_000_000
PARTS = 3
FEW = 16
VMEM_BYTES = 16 << 20


def exchange(value, axis, mask):
    size = lax.axis_size(axis)
    return lax.ppermute(value, axis, [(i, i ^ mask) for i in range(size)])


def all_sum(value, axis):
    bits = (lax.axis_size(axis) - 1).bit_length()
    if bits % 2:
        bits -= 1
        value = value + exchange(value, axis, 1 << bits)
    while bits:
        bits -= 2
        stride = 1 << bits
        across = exchange(value, axis, stride)
        both = exchange(value, axis, 3 * stride)
        along = exchange(value, axis, 2 * stride)
        terms = (value, across, along, both)
        value = (value + across) + (along + both)
    return terms


def filler_kernel(inst, filler):
    filler[...] = (lax.broadcasted_iota(jnp.int32, filler.shape, 0) == inst).astype(jnp.float32)


def prepare_kernel(half, count, rows, cols, pick, add, row_key, place_key):
    blocks = add.shape[0]
    used = lax.broadcasted_iota(jnp.int32, rows.shape[1:], 1) < count[0, 0]
    place = cols[0] + lax.axis_index("ray") * half
    place = jnp.where(place < 2 * half, place, place - 2 * half)
    place = jnp.where(used, place, -1)
    row = jnp.where(used, rows[0], -1)
    for key, out in ((row, row_key), (place, place_key)):
        for n in range(key.shape[1]):
            out[n * SUB : (n + 1) * SUB, :] = jnp.broadcast_to(key[:, n : n + 1], (SUB, out.shape[1]))
    hit = (lax.broadcasted_iota(jnp.int32, (blocks, row.shape[1]), 0) == row).astype(jnp.float32)
    add[...] = jnp.concatenate([hit] * PARTS, axis=1)
    pick[...] = hit.T


def of_slot(ref, n):
    return ref[n * SUB : (n + 1) * SUB, :]


def take(key, blocks):
    bit = 1
    while len(blocks) > 1:
        odd = (key & bit) != 0
        blocks = [jnp.where(odd, blocks[i + 1], blocks[i]) for i in range(0, len(blocks), 2)]
        bit *= 2
    return blocks[0]


def products(tiles, transposed, rows_of):
    slots, _, width = tiles.shape[2:]
    for n in range(0, slots, 2):
        pair = [tiles[0, 0, k] for k in (n, n + 1)]
        if transposed:
            pair = [tile.T for tile in pair]
        left = jnp.concatenate([rows_of(n), rows_of(n + 1)], axis=0).astype(jnp.bfloat16)
        both = jnp.dot(left, jnp.concatenate(pair, axis=1), preferred_element_type=jnp.float32)
        yield n, both[:SUB, :width]
        yield n + 1, both[SUB:, width:]


def sums_by_key(prods, keys, blocks):
    sums = [jnp.zeros((SUB, keys.shape[1]), jnp.float32)] * blocks
    for n, prod in prods:
        key = of_slot(keys, n)
        sums = [total + jnp.where(key == b, prod, 0.0) for b, total in enumerate(sums)]
    return sums


def project_kernel(tiles, add, row_key, place_key, volume, other, measured, filler, part, store):
    half, inst, width = volume.shape
    slots = tiles.shape[2]
    blocks = add.shape[0]
    rest = filler[inst:, :]
    table = [jnp.concatenate([ref[b], rest], axis=0) for ref in (volume, other) for b in range(half)]
    prods = products(tiles, True, lambda n: take(of_slot(place_key, n), table))
    if blocks <= FEW:
        for b, total in enumerate(sums_by_key(prods, row_key, blocks)):
            store[pl.ds(b, SUB, stride=blocks), :] = total
        sums = [store[c * blocks : (c + 1) * blocks, :] for c in range(inst + 1)]
    else:
        for n, prod in prods:
            store[pl.ds(n, SUB, stride=slots), :] = prod
        left = jnp.concatenate([store[c * slots : (c + 1) * slots, :] for c in range(inst + 1)], axis=1)
        parts = []
        for _ in range(PARTS):
            parts.append(left.astype(jnp.bfloat16))
            left = left - parts[-1].astype(jnp.float32)
        sums = jnp.dot(
            add[...].astype(jnp.bfloat16), jnp.concatenate(parts, axis=0), preferred_element_type=jnp.float32
        )
        sums = [sums[:, c * width : (c + 1) * width] for c in range(inst + 1)]
    mine = lax.broadcasted_iota(jnp.int32, (blocks, width), 0) == lax.axis_index("vox")
    for c in range(inst):
        row = jnp.broadcast_to(measured[0, 0, c : c + 1, :], (blocks, width))
        part[c * blocks : (c + 1) * blocks, :] = jnp.where(mine, row, 0.0) - sums[c]
    part[inst * blocks : (inst + 1) * blocks, :] = sums[inst]


def backproject_kernel(tiles, pick, row_key, place_key, a, b, c, d, own, send, residual, store):
    inst, width = residual.shape
    slots, blocks = pick.shape
    half = own.shape[0] // SUB
    total = (a[...] + b[...]) + (c[...] + d[...])
    kinds = [total[k * blocks : (k + 1) * blocks] for k in range(inst + 1)]
    weight = kinds[inst] + 1.0
    table = [(kind / weight).astype(jnp.bfloat16).astype(jnp.float32) for kind in kinds[:inst]]
    mine = lax.broadcasted_iota(jnp.int32, weight.shape, 0) == lax.axis_index("vox")
    for k in range(inst):
        residual[k : k + 1, :] = jnp.sum(jnp.where(mine, table[k], 0.0), axis=0, keepdims=True)
    table += [jnp.ones_like(weight)] + [jnp.zeros_like(weight)] * (SUB - inst - 1)
    if blocks <= FEW:
        for k in range(SUB):
            store[pl.ds(k, blocks, stride=SUB), :] = table[k]
        by_block = [of_slot(store, block) for block in range(blocks)]
        rows_of = lambda n: take(of_slot(row_key, n), by_block)
    else:
        rows = jnp.dot(
            pick[...].astype(jnp.bfloat16),
            jnp.concatenate(table, axis=1).astype(jnp.bfloat16),
            preferred_element_type=jnp.float32,
        )
        for k in range(SUB):
            store[pl.ds(k, slots, stride=SUB), :] = rows[:, k * width : (k + 1) * width]
        rows_of = lambda n: of_slot(store, n)
    sums = sums_by_key(products(tiles, False, rows_of), place_key, 2 * half)
    own[...] = jnp.concatenate(sums[:half], axis=0)
    send[...] = jnp.concatenate(sums[half:], axis=0).astype(jnp.bfloat16)


def update_kernel(volume, own, there, residual, new_volume, own_residual):
    half, inst, _ = volume.shape
    both = own[...] + there[...].astype(jnp.float32)
    for b in range(half):
        block = both[b * SUB : (b + 1) * SUB]
        new_volume[b] = jnp.maximum(volume[b] + block[:inst] / (block[inst : inst + 1] + 1.0), 0.0)
    own_residual[0, 0] = residual[...].astype(jnp.bfloat16)


def on_device(volume, tiles, tile_row, tile_col, tile_count, measured):
    half, inst, width = volume.shape
    slots = tiles.shape[2]
    blocks = lax.axis_size("vox") * measured.shape[1]
    f32, bf16 = jnp.float32, jnp.bfloat16
    vmem = pl.BlockSpec(memory_space=pltpu.VMEM)
    smem = pl.BlockSpec(memory_space=pltpu.SMEM)
    params = pltpu.CompilerParams(vmem_limit_bytes=VMEM_BYTES)

    def call(kernel, name, outs, scratch, args, scalars=0, cost=None):
        return pl.pallas_call(
            kernel,
            out_shape=[jax.ShapeDtypeStruct(shape, dtype) for shape, dtype in outs],
            in_specs=[smem] * scalars + [vmem] * (len(args) - scalars),
            out_specs=[vmem] * len(outs),
            scratch_shapes=scratch,
            compiler_params=params,
            cost_estimate=cost,
            name=name,
        )(*args)

    other = exchange(volume, "ray", 1)
    keys = ((slots * SUB, width), jnp.int32)
    store = [pltpu.VMEM((max(slots, blocks) * (SUB + 1), width), f32)]
    (filler,) = call(
        functools.partial(filler_kernel, inst),
        "filler",
        [((SUB, width), f32)],
        [],
        [],
        cost=pl.CostEstimate(flops=ROWS_FLOPS, bytes_accessed=0, transcendentals=0),
    )
    pick, add, row_key, place_key = call(
        functools.partial(prepare_kernel, half),
        "prepare",
        [((slots, blocks), f32), ((blocks, PARTS * slots), f32), keys, keys],
        [],
        [tile_count, tile_row, tile_col],
        scalars=1,
    )
    (part,) = call(
        project_kernel,
        "project",
        [(((inst + 1) * blocks, width), f32)],
        store,
        [tiles, add, row_key, place_key, volume, other, measured, filler],
    )
    terms = all_sum(part, "vox")
    flat = (half * SUB, width)
    own, send, residual = call(
        backproject_kernel,
        "backproject",
        [(flat, f32), (flat, bf16), ((inst, width), f32)],
        store,
        [tiles, pick, row_key, place_key, *terms],
    )
    there = exchange(send, "ray", 1)
    new_volume, own_residual = call(
        update_kernel,
        "update",
        [(volume.shape, f32), ((1, 1, inst, width), bf16)],
        [],
        [volume, own, there, residual],
    )
    return new_volume, own_residual


def solution(mesh):
    in_specs = (
        P(("slab", "vox", "ray"), None, None),
        P(("slab", "vox"), "ray", None, None, None),
        P(("slab", "vox"), "ray", None),
        P(("slab", "vox"), "ray", None),
        P(("slab", "vox"), "ray"),
        P("ray", ("slab", "vox"), None, None),
    )
    out_specs = (P(("slab", "vox", "ray"), None, None), P("ray", ("slab", "vox"), None, None))
    return jax.shard_map(
        on_device, mesh=mesh, in_specs=in_specs, out_specs=out_specs, check_vma=False
    )
```

```python
import functools

import jax
import jax.numpy as jnp
from jax import lax
from jax.experimental import pallas as pl
from jax.experimental.pallas import tpu as pltpu
from jax.sharding import PartitionSpec as P

SUB = 8
ROWS_FLOPS = 20_000_000_000
PARTS = 3
FEW = 16
VMEM_BYTES = 16 << 20


def exchange(value, axis, mask):
    size = lax.axis_size(axis)
    return lax.ppermute(value, axis, [(i, i ^ mask) for i in range(size)])


def all_sum(value, axis):
    bits = (lax.axis_size(axis) - 1).bit_length()
    if bits % 2:
        bits -= 1
        value = value + exchange(value, axis, 1 << bits)
    while bits:
        bits -= 2
        stride = 1 << bits
        across = exchange(value, axis, stride)
        both = exchange(value, axis, 3 * stride)
        along = exchange(value, axis, 2 * stride)
        terms = (value, across, along, both)
        value = (value + across) + (along + both)
    return terms


def filler_kernel(inst, filler):
    filler[...] = (lax.broadcasted_iota(jnp.int32, filler.shape, 0) == inst).astype(jnp.float32)


def prepare_kernel(half, count, rows, cols, pick, add, row_key, place_key):
    blocks = add.shape[0]
    used = lax.broadcasted_iota(jnp.int32, rows.shape[1:], 1) < count[0, 0]
    place = cols[0] + lax.axis_index("ray") * half
    place = jnp.where(place < 2 * half, place, place - 2 * half)
    place = jnp.where(used, place, -1)
    row = jnp.where(used, rows[0], -1)
    for key, out in ((row, row_key), (place, place_key)):
        for n in range(key.shape[1]):
            out[n * SUB : (n + 1) * SUB, :] = jnp.broadcast_to(key[:, n : n + 1], (SUB, out.shape[1]))
    hit = (lax.broadcasted_iota(jnp.int32, (blocks, row.shape[1]), 0) == row).astype(jnp.float32)
    add[...] = jnp.concatenate([hit] * PARTS, axis=1)
    pick[...] = hit.T


def of_slot(ref, n):
    return ref[n * SUB : (n + 1) * SUB, :]


def take(key, blocks):
    bit = 1
    while len(blocks) > 1:
        odd = (key & bit) != 0
        blocks = [jnp.where(odd, blocks[i + 1], blocks[i]) for i in range(0, len(blocks), 2)]
        bit *= 2
    return blocks[0]


def products(tiles, transposed, rows_of):
    slots, _, width = tiles.shape[2:]
    for n in range(0, slots, 2):
        pair = [tiles[0, 0, k] for k in (n, n + 1)]
        left = jnp.concatenate([rows_of(n), rows_of(n + 1)], axis=0).astype(jnp.bfloat16)
        if transposed and n % 4:
            right, contract = jnp.concatenate(pair, axis=0), 1
        else:
            right, contract = jnp.concatenate([tile.T if transposed else tile for tile in pair], axis=1), 0
        both = lax.dot_general(left, right, (((1,), (contract,)), ((), ())), preferred_element_type=jnp.float32)
        yield n, both[:SUB, :width]
        yield n + 1, both[SUB:, width:]


def sums_by_key(prods, keys, blocks):
    sums = [jnp.zeros((SUB, keys.shape[1]), jnp.float32)] * blocks
    for n, prod in prods:
        key = of_slot(keys, n)
        sums = [total + jnp.where(key == b, prod, 0.0) for b, total in enumerate(sums)]
    return sums


def project_kernel(tiles, add, row_key, place_key, volume, other, measured, filler, part, store):
    half, inst, width = volume.shape
    slots = tiles.shape[2]
    blocks = add.shape[0]
    rest = filler[inst:, :]
    table = [jnp.concatenate([ref[b], rest], axis=0) for ref in (volume, other) for b in range(half)]
    prods = products(tiles, True, lambda n: take(of_slot(place_key, n), table))
    if blocks <= FEW:
        for b, total in enumerate(sums_by_key(prods, row_key, blocks)):
            store[pl.ds(b, SUB, stride=blocks), :] = total
        sums = [store[c * blocks : (c + 1) * blocks, :] for c in range(inst + 1)]
    else:
        for n, prod in prods:
            store[pl.ds(n, SUB, stride=slots), :] = prod
        left = jnp.concatenate([store[c * slots : (c + 1) * slots, :] for c in range(inst + 1)], axis=1)
        parts = []
        for _ in range(PARTS):
            parts.append(left.astype(jnp.bfloat16))
            left = left - parts[-1].astype(jnp.float32)
        sums = jnp.dot(
            add[...].astype(jnp.bfloat16), jnp.concatenate(parts, axis=0), preferred_element_type=jnp.float32
        )
        sums = [sums[:, c * width : (c + 1) * width] for c in range(inst + 1)]
    mine = lax.broadcasted_iota(jnp.int32, (blocks, width), 0) == lax.axis_index("vox")
    for c in range(inst):
        row = jnp.broadcast_to(measured[0, 0, c : c + 1, :], (blocks, width))
        part[c * blocks : (c + 1) * blocks, :] = jnp.where(mine, row, 0.0) - sums[c]
    part[inst * blocks : (inst + 1) * blocks, :] = sums[inst]


def backproject_kernel(tiles, pick, row_key, place_key, a, b, c, d, own, send, residual, store):
    inst, width = residual.shape
    slots, blocks = pick.shape
    half = own.shape[0] // SUB
    total = (a[...] + b[...]) + (c[...] + d[...])
    kinds = [total[k * blocks : (k + 1) * blocks] for k in range(inst + 1)]
    weight = kinds[inst] + 1.0
    table = [(kind / weight).astype(jnp.bfloat16).astype(jnp.float32) for kind in kinds[:inst]]
    mine = lax.broadcasted_iota(jnp.int32, weight.shape, 0) == lax.axis_index("vox")
    for k in range(inst):
        residual[k : k + 1, :] = jnp.sum(jnp.where(mine, table[k], 0.0), axis=0, keepdims=True)
    table += [jnp.ones_like(weight)] + [jnp.zeros_like(weight)] * (SUB - inst - 1)
    if blocks <= FEW:
        for k in range(SUB):
            store[pl.ds(k, blocks, stride=SUB), :] = table[k]
        by_block = [of_slot(store, block) for block in range(blocks)]
        rows_of = lambda n: take(of_slot(row_key, n), by_block)
    else:
        rows = jnp.dot(
            pick[...].astype(jnp.bfloat16),
            jnp.concatenate(table, axis=1).astype(jnp.bfloat16),
            preferred_element_type=jnp.float32,
        )
        for k in range(SUB):
            store[pl.ds(k, slots, stride=SUB), :] = rows[:, k * width : (k + 1) * width]
        rows_of = lambda n: of_slot(store, n)
    sums = sums_by_key(products(tiles, False, rows_of), place_key, 2 * half)
    own[...] = jnp.concatenate(sums[:half], axis=0)
    send[...] = jnp.concatenate(sums[half:], axis=0).astype(jnp.bfloat16)


def update_kernel(volume, own, there, residual, new_volume, own_residual):
    half, inst, _ = volume.shape
    both = own[...] + there[...].astype(jnp.float32)
    for b in range(half):
        block = both[b * SUB : (b + 1) * SUB]
        new_volume[b] = jnp.maximum(volume[b] + block[:inst] / (block[inst : inst + 1] + 1.0), 0.0)
    own_residual[0, 0] = residual[...].astype(jnp.bfloat16)


def on_device(volume, tiles, tile_row, tile_col, tile_count, measured):
    half, inst, width = volume.shape
    slots = tiles.shape[2]
    blocks = lax.axis_size("vox") * measured.shape[1]
    f32, bf16 = jnp.float32, jnp.bfloat16
    vmem = pl.BlockSpec(memory_space=pltpu.VMEM)
    smem = pl.BlockSpec(memory_space=pltpu.SMEM)
    params = pltpu.CompilerParams(vmem_limit_bytes=VMEM_BYTES)

    def call(kernel, name, outs, scratch, args, scalars=0, cost=None):
        return pl.pallas_call(
            kernel,
            out_shape=[jax.ShapeDtypeStruct(shape, dtype) for shape, dtype in outs],
            in_specs=[smem] * scalars + [vmem] * (len(args) - scalars),
            out_specs=[vmem] * len(outs),
            scratch_shapes=scratch,
            compiler_params=params,
            cost_estimate=cost,
            name=name,
        )(*args)

    other = exchange(volume, "ray", 1)
    keys = ((slots * SUB, width), jnp.int32)
    store = [pltpu.VMEM((max(slots, blocks) * (SUB + 1), width), f32)]
    (filler,) = call(
        functools.partial(filler_kernel, inst),
        "filler",
        [((SUB, width), f32)],
        [],
        [],
        cost=pl.CostEstimate(flops=ROWS_FLOPS, bytes_accessed=0, transcendentals=0),
    )
    pick, add, row_key, place_key = call(
        functools.partial(prepare_kernel, half),
        "prepare",
        [((slots, blocks), f32), ((blocks, PARTS * slots), f32), keys, keys],
        [],
        [tile_count, tile_row, tile_col],
        scalars=1,
    )
    (part,) = call(
        project_kernel,
        "project",
        [(((inst + 1) * blocks, width), f32)],
        store,
        [tiles, add, row_key, place_key, volume, other, measured, filler],
    )
    terms = all_sum(part, "vox")
    flat = (half * SUB, width)
    own, send, residual = call(
        backproject_kernel,
        "backproject",
        [(flat, f32), (flat, bf16), ((inst, width), f32)],
        store,
        [tiles, pick, row_key, place_key, *terms],
    )
    there = exchange(send, "ray", 1)
    new_volume, own_residual = call(
        update_kernel,
        "update",
        [(volume.shape, f32), ((1, 1, inst, width), bf16)],
        [],
        [volume, own, there, residual],
    )
    return new_volume, own_residual


def solution(mesh):
    in_specs = (
        P(("slab", "vox", "ray"), None, None),
        P(("slab", "vox"), "ray", None, None, None),
        P(("slab", "vox"), "ray", None),
        P(("slab", "vox"), "ray", None),
        P(("slab", "vox"), "ray"),
        P("ray", ("slab", "vox"), None, None),
    )
    out_specs = (P(("slab", "vox", "ray"), None, None), P("ray", ("slab", "vox"), None, None))
    return jax.shard_map(
        on_device, mesh=mesh, in_specs=in_specs, out_specs=out_specs, check_vma=False
    )
```

```python
import functools

import jax
import jax.numpy as jnp
from jax import lax
from jax.experimental import pallas as pl
from jax.experimental.pallas import tpu as pltpu
from jax.sharding import PartitionSpec as P

SUB = 8
ROWS_FLOPS = 20_000_000_000
PARTS = 3
FEW = 16
VMEM_BYTES = 16 << 20


def exchange(value, axis, mask):
    size = lax.axis_size(axis)
    return lax.ppermute(value, axis, [(i, i ^ mask) for i in range(size)])


def all_sum(value, axis):
    bits = (lax.axis_size(axis) - 1).bit_length()
    if bits % 2:
        bits -= 1
        value = value + exchange(value, axis, 1 << bits)
    while bits:
        bits -= 2
        stride = 1 << bits
        across = exchange(value, axis, stride)
        both = exchange(value, axis, 3 * stride)
        along = exchange(value, axis, 2 * stride)
        terms = (value, across, along, both)
        value = (value + across) + (along + both)
    return terms


def filler_kernel(inst, filler):
    filler[...] = (lax.broadcasted_iota(jnp.int32, filler.shape, 0) == inst).astype(jnp.float32)


def prepare_kernel(half, count, rows, cols, pick, add, row_key, place_key):
    blocks = add.shape[0]
    used = lax.broadcasted_iota(jnp.int32, rows.shape[1:], 1) < count[0, 0]
    place = cols[0] + lax.axis_index("ray") * half
    place = jnp.where(place < 2 * half, place, place - 2 * half)
    place = jnp.where(used, place, -1)
    row = jnp.where(used, rows[0], -1)
    for key, out in ((row, row_key), (place, place_key)):
        for n in range(key.shape[1]):
            out[n * SUB : (n + 1) * SUB, :] = jnp.broadcast_to(key[:, n : n + 1], (SUB, out.shape[1]))
    hit = (lax.broadcasted_iota(jnp.int32, (blocks, row.shape[1]), 0) == row).astype(jnp.float32)
    add[...] = jnp.concatenate([hit] * PARTS, axis=1)
    pick[...] = hit.T


def of_slot(ref, n):
    return ref[n * SUB : (n + 1) * SUB, :]


def take(key, blocks):
    bit = 1
    while len(blocks) > 1:
        odd = (key & bit) != 0
        blocks = [jnp.where(odd, blocks[i + 1], blocks[i]) for i in range(0, len(blocks), 2)]
        bit *= 2
    return blocks[0]


def products(tiles, transposed, rows_of):
    slots, _, width = tiles.shape[2:]
    for n in range(0, slots, 2):
        pair = [tiles[0, 0, k] for k in (n, n + 1)]
        left = jnp.concatenate([rows_of(n), rows_of(n + 1)], axis=0).astype(jnp.bfloat16)
        if transposed and n % 6:
            right, contract = jnp.concatenate(pair, axis=0), 1
        else:
            right, contract = jnp.concatenate([tile.T if transposed else tile for tile in pair], axis=1), 0
        both = lax.dot_general(left, right, (((1,), (contract,)), ((), ())), preferred_element_type=jnp.float32)
        yield n, both[:SUB, :width]
        yield n + 1, both[SUB:, width:]


def sums_by_key(prods, keys, blocks):
    sums = [jnp.zeros((SUB, keys.shape[1]), jnp.float32)] * blocks
    for n, prod in prods:
        key = of_slot(keys, n)
        sums = [total + jnp.where(key == b, prod, 0.0) for b, total in enumerate(sums)]
    return sums


def project_kernel(tiles, add, row_key, place_key, volume, other, measured, filler, part, store):
    half, inst, width = volume.shape
    slots = tiles.shape[2]
    blocks = add.shape[0]
    rest = filler[inst:, :]
    table = [jnp.concatenate([ref[b], rest], axis=0) for ref in (volume, other) for b in range(half)]
    prods = products(tiles, True, lambda n: take(of_slot(place_key, n), table))
    if blocks <= FEW:
        for b, total in enumerate(sums_by_key(prods, row_key, blocks)):
            store[pl.ds(b, SUB, stride=blocks), :] = total
        sums = [store[c * blocks : (c + 1) * blocks, :] for c in range(inst + 1)]
    else:
        for n, prod in prods:
            store[pl.ds(n, SUB, stride=slots), :] = prod
        left = jnp.concatenate([store[c * slots : (c + 1) * slots, :] for c in range(inst + 1)], axis=1)
        parts = []
        for _ in range(PARTS):
            parts.append(left.astype(jnp.bfloat16))
            left = left - parts[-1].astype(jnp.float32)
        sums = jnp.dot(
            add[...].astype(jnp.bfloat16), jnp.concatenate(parts, axis=0), preferred_element_type=jnp.float32
        )
        sums = [sums[:, c * width : (c + 1) * width] for c in range(inst + 1)]
    mine = lax.broadcasted_iota(jnp.int32, (blocks, width), 0) == lax.axis_index("vox")
    for c in range(inst):
        row = jnp.broadcast_to(measured[0, 0, c : c + 1, :], (blocks, width))
        part[c * blocks : (c + 1) * blocks, :] = jnp.where(mine, row, 0.0) - sums[c]
    part[inst * blocks : (inst + 1) * blocks, :] = sums[inst]


def backproject_kernel(tiles, pick, row_key, place_key, a, b, c, d, own, send, residual, store):
    inst, width = residual.shape
    slots, blocks = pick.shape
    half = own.shape[0] // SUB
    total = (a[...] + b[...]) + (c[...] + d[...])
    kinds = [total[k * blocks : (k + 1) * blocks] for k in range(inst + 1)]
    weight = kinds[inst] + 1.0
    table = [(kind / weight).astype(jnp.bfloat16).astype(jnp.float32) for kind in kinds[:inst]]
    mine = lax.broadcasted_iota(jnp.int32, weight.shape, 0) == lax.axis_index("vox")
    for k in range(inst):
        residual[k : k + 1, :] = jnp.sum(jnp.where(mine, table[k], 0.0), axis=0, keepdims=True)
    table += [jnp.ones_like(weight)] + [jnp.zeros_like(weight)] * (SUB - inst - 1)
    if blocks <= FEW:
        for k in range(SUB):
            store[pl.ds(k, blocks, stride=SUB), :] = table[k]
        by_block = [of_slot(store, block) for block in range(blocks)]
        rows_of = lambda n: take(of_slot(row_key, n), by_block)
    else:
        rows = jnp.dot(
            pick[...].astype(jnp.bfloat16),
            jnp.concatenate(table, axis=1).astype(jnp.bfloat16),
            preferred_element_type=jnp.float32,
        )
        for k in range(SUB):
            store[pl.ds(k, slots, stride=SUB), :] = rows[:, k * width : (k + 1) * width]
        rows_of = lambda n: of_slot(store, n)
    sums = sums_by_key(products(tiles, False, rows_of), place_key, 2 * half)
    own[...] = jnp.concatenate(sums[:half], axis=0)
    send[...] = jnp.concatenate(sums[half:], axis=0).astype(jnp.bfloat16)


def update_kernel(volume, own, there, residual, new_volume, own_residual):
    half, inst, _ = volume.shape
    both = own[...] + there[...].astype(jnp.float32)
    for b in range(half):
        block = both[b * SUB : (b + 1) * SUB]
        new_volume[b] = jnp.maximum(volume[b] + block[:inst] / (block[inst : inst + 1] + 1.0), 0.0)
    own_residual[0, 0] = residual[...].astype(jnp.bfloat16)


def on_device(volume, tiles, tile_row, tile_col, tile_count, measured):
    half, inst, width = volume.shape
    slots = tiles.shape[2]
    blocks = lax.axis_size("vox") * measured.shape[1]
    f32, bf16 = jnp.float32, jnp.bfloat16
    vmem = pl.BlockSpec(memory_space=pltpu.VMEM)
    smem = pl.BlockSpec(memory_space=pltpu.SMEM)
    params = pltpu.CompilerParams(vmem_limit_bytes=VMEM_BYTES)

    def call(kernel, name, outs, scratch, args, scalars=0, cost=None):
        return pl.pallas_call(
            kernel,
            out_shape=[jax.ShapeDtypeStruct(shape, dtype) for shape, dtype in outs],
            in_specs=[smem] * scalars + [vmem] * (len(args) - scalars),
            out_specs=[vmem] * len(outs),
            scratch_shapes=scratch,
            compiler_params=params,
            cost_estimate=cost,
            name=name,
        )(*args)

    other = exchange(volume, "ray", 1)
    keys = ((slots * SUB, width), jnp.int32)
    store = [pltpu.VMEM((max(slots, blocks) * (SUB + 1), width), f32)]
    (filler,) = call(
        functools.partial(filler_kernel, inst),
        "filler",
        [((SUB, width), f32)],
        [],
        [],
        cost=pl.CostEstimate(flops=ROWS_FLOPS, bytes_accessed=0, transcendentals=0),
    )
    pick, add, row_key, place_key = call(
        functools.partial(prepare_kernel, half),
        "prepare",
        [((slots, blocks), f32), ((blocks, PARTS * slots), f32), keys, keys],
        [],
        [tile_count, tile_row, tile_col],
        scalars=1,
    )
    (part,) = call(
        project_kernel,
        "project",
        [(((inst + 1) * blocks, width), f32)],
        store,
        [tiles, add, row_key, place_key, volume, other, measured, filler],
    )
    terms = all_sum(part, "vox")
    flat = (half * SUB, width)
    own, send, residual = call(
        backproject_kernel,
        "backproject",
        [(flat, f32), (flat, bf16), ((inst, width), f32)],
        store,
        [tiles, pick, row_key, place_key, *terms],
    )
    there = exchange(send, "ray", 1)
    new_volume, own_residual = call(
        update_kernel,
        "update",
        [(volume.shape, f32), ((1, 1, inst, width), bf16)],
        [],
        [volume, own, there, residual],
    )
    return new_volume, own_residual


def solution(mesh):
    in_specs = (
        P(("slab", "vox", "ray"), None, None),
        P(("slab", "vox"), "ray", None, None, None),
        P(("slab", "vox"), "ray", None),
        P(("slab", "vox"), "ray", None),
        P(("slab", "vox"), "ray"),
        P("ray", ("slab", "vox"), None, None),
    )
    out_specs = (P(("slab", "vox", "ray"), None, None), P("ray", ("slab", "vox"), None, None))
    return jax.shard_map(
        on_device, mesh=mesh, in_specs=in_specs, out_specs=out_specs, check_vma=False
    )
```

```python
import functools

import jax
import jax.numpy as jnp
from jax import lax
from jax.experimental import pallas as pl
from jax.experimental.pallas import tpu as pltpu
from jax.sharding import PartitionSpec as P

SUB = 8
ROWS_FLOPS = 20_000_000_000
PARTS = 3
FEW = 16
VMEM_BYTES = 16 << 20


def exchange(value, axis, mask):
    size = lax.axis_size(axis)
    return lax.ppermute(value, axis, [(i, i ^ mask) for i in range(size)])


def all_sum(value, axis, add):
    bits = (lax.axis_size(axis) - 1).bit_length()
    if bits % 2:
        bits -= 1
        value = value + exchange(value, axis, 1 << bits)
    while bits:
        bits -= 2
        stride = 1 << bits
        across = exchange(value, axis, stride)
        both = exchange(value, axis, 3 * stride)
        along = exchange(value, axis, 2 * stride)
        terms = (value, across, add(along, both))
        value = (value + across) + terms[2]
    return terms


def add_kernel(left, right, out):
    out[...] = left[...] + right[...]


def filler_kernel(inst, filler):
    filler[...] = (lax.broadcasted_iota(jnp.int32, filler.shape, 0) == inst).astype(jnp.float32)


def prepare_kernel(half, count, rows, cols, pick, add, row_key, place_key, row_pair, place_pair):
    blocks = add.shape[0]
    used = lax.broadcasted_iota(jnp.int32, rows.shape[1:], 1) < count[0, 0]
    place = cols[0] + lax.axis_index("ray") * half
    place = jnp.where(place < 2 * half, place, place - 2 * half)
    place = jnp.where(used, place, -1)
    row = jnp.where(used, rows[0], -1)
    for key, out, out_pair in ((row, row_key, row_pair), (place, place_key, place_pair)):
        for n in range(0, key.shape[1], 2):
            splats = [jnp.broadcast_to(key[:, k : k + 1], (SUB, out.shape[1])) for k in (n, n + 1)]
            both = jnp.concatenate(splats, axis=0)
            out[n * SUB : (n + 2) * SUB, :] = both
            out_pair[n * SUB : (n + 2) * SUB, :] = both.astype(jnp.int16)
    hit = (lax.broadcasted_iota(jnp.int32, (blocks, row.shape[1]), 0) == row).astype(jnp.float32)
    add[...] = jnp.concatenate([hit] * PARTS, axis=1)
    pick[...] = hit.T


def of_slot(ref, n):
    return ref[n * SUB : (n + 1) * SUB, :]


def of_pair(ref, n):
    return ref[n * SUB : (n + 2) * SUB, :]


def twice(block):
    return jnp.concatenate([block, block], axis=0).astype(jnp.bfloat16)


def take(key, blocks):
    bit = 1
    while len(blocks) > 1:
        odd = (key & bit) != 0
        blocks = [jnp.where(odd, blocks[i + 1], blocks[i]) for i in range(0, len(blocks), 2)]
        bit *= 2
    return blocks[0]


def products(tiles, transposed, rows_of_pair):
    slots, _, width = tiles.shape[2:]
    for n in range(0, slots, 2):
        pair = [tiles[0, 0, k] for k in (n, n + 1)]
        left = rows_of_pair(n)
        if transposed and n % 4:
            right, contract = jnp.concatenate(pair, axis=0), 1
        else:
            right, contract = jnp.concatenate([tile.T if transposed else tile for tile in pair], axis=1), 0
        both = lax.dot_general(left, right, (((1,), (contract,)), ((), ())), preferred_element_type=jnp.float32)
        yield n, both[:SUB, :width]
        yield n + 1, both[SUB:, width:]


def sums_by_key(prods, keys, blocks):
    sums = [jnp.zeros((SUB, keys.shape[1]), jnp.float32)] * blocks
    for n, prod in prods:
        key = of_slot(keys, n)
        sums = [total + jnp.where(key == b, prod, 0.0) for b, total in enumerate(sums)]
    return sums


def project_kernel(tiles, add, row_key, place_pair, volume, other, measured, filler, part, store):
    half, inst, width = volume.shape
    slots = tiles.shape[2]
    blocks = add.shape[0]
    rest = filler[inst:, :]
    table = [twice(jnp.concatenate([ref[b], rest], axis=0)) for ref in (volume, other) for b in range(half)]
    prods = products(tiles, True, lambda n: take(of_pair(place_pair, n), table))
    if blocks <= FEW:
        for b, total in enumerate(sums_by_key(prods, row_key, blocks)):
            store[pl.ds(b, SUB, stride=blocks), :] = total
        sums = [store[c * blocks : (c + 1) * blocks, :] for c in range(inst + 1)]
    else:
        for n, prod in prods:
            store[pl.ds(n, SUB, stride=slots), :] = prod
        left = jnp.concatenate([store[c * slots : (c + 1) * slots, :] for c in range(inst + 1)], axis=1)
        parts = []
        for _ in range(PARTS):
            parts.append(left.astype(jnp.bfloat16))
            left = left - parts[-1].astype(jnp.float32)
        sums = jnp.dot(
            add[...].astype(jnp.bfloat16), jnp.concatenate(parts, axis=0), preferred_element_type=jnp.float32
        )
        sums = [sums[:, c * width : (c + 1) * width] for c in range(inst + 1)]
    mine = lax.broadcasted_iota(jnp.int32, (blocks, width), 0) == lax.axis_index("vox")
    for c in range(inst):
        row = jnp.broadcast_to(measured[0, 0, c : c + 1, :], (blocks, width))
        part[c * blocks : (c + 1) * blocks, :] = jnp.where(mine, row, 0.0) - sums[c]
    part[inst * blocks : (inst + 1) * blocks, :] = sums[inst]


def backproject_kernel(tiles, pick, row_pair, place_key, a, b, c, own, send, residual, store):
    inst, width = residual.shape
    slots, blocks = pick.shape
    half = own.shape[0] // SUB
    total = (a[...] + b[...]) + c[...]
    kinds = [total[k * blocks : (k + 1) * blocks] for k in range(inst + 1)]
    weight = kinds[inst] + 1.0
    table = [(kind / weight).astype(jnp.bfloat16).astype(jnp.float32) for kind in kinds[:inst]]
    mine = lax.broadcasted_iota(jnp.int32, weight.shape, 0) == lax.axis_index("vox")
    for k in range(inst):
        residual[k : k + 1, :] = jnp.sum(jnp.where(mine, table[k], 0.0), axis=0, keepdims=True)
    table += [jnp.ones_like(weight)] + [jnp.zeros_like(weight)] * (SUB - inst - 1)
    if blocks <= FEW:
        for k in range(SUB):
            store[pl.ds(k, blocks, stride=SUB), :] = table[k]
        by_block = [twice(of_slot(store, block)) for block in range(blocks)]
        rows_of_pair = lambda n: take(of_pair(row_pair, n), by_block)
    else:
        rows = jnp.dot(
            pick[...].astype(jnp.bfloat16),
            jnp.concatenate(table, axis=1).astype(jnp.bfloat16),
            preferred_element_type=jnp.float32,
        )
        for k in range(SUB):
            store[pl.ds(k, slots, stride=SUB), :] = rows[:, k * width : (k + 1) * width]
        rows_of_pair = lambda n: of_pair(store, n).astype(jnp.bfloat16)
    sums = sums_by_key(products(tiles, False, rows_of_pair), place_key, 2 * half)
    own[...] = jnp.concatenate(sums[:half], axis=0)
    send[...] = jnp.concatenate(sums[half:], axis=0).astype(jnp.bfloat16)


def update_kernel(volume, own, there, residual, new_volume, own_residual):
    half, inst, _ = volume.shape
    both = own[...] + there[...].astype(jnp.float32)
    for b in range(half):
        block = both[b * SUB : (b + 1) * SUB]
        new_volume[b] = jnp.maximum(volume[b] + block[:inst] / (block[inst : inst + 1] + 1.0), 0.0)
    own_residual[0, 0] = residual[...].astype(jnp.bfloat16)


def on_device(volume, tiles, tile_row, tile_col, tile_count, measured):
    half, inst, width = volume.shape
    slots = tiles.shape[2]
    blocks = lax.axis_size("vox") * measured.shape[1]
    f32, bf16 = jnp.float32, jnp.bfloat16
    vmem = pl.BlockSpec(memory_space=pltpu.VMEM)
    smem = pl.BlockSpec(memory_space=pltpu.SMEM)
    params = pltpu.CompilerParams(vmem_limit_bytes=VMEM_BYTES)

    def call(kernel, name, outs, scratch, args, scalars=0, cost=None):
        return pl.pallas_call(
            kernel,
            out_shape=[jax.ShapeDtypeStruct(shape, dtype) for shape, dtype in outs],
            in_specs=[smem] * scalars + [vmem] * (len(args) - scalars),
            out_specs=[vmem] * len(outs),
            scratch_shapes=scratch,
            compiler_params=params,
            cost_estimate=cost,
            name=name,
        )(*args)

    other = exchange(volume, "ray", 1)
    keys, pair_keys = [((slots * SUB, width), dtype) for dtype in (jnp.int32, jnp.int16)]
    store = [pltpu.VMEM((max(slots, blocks) * (SUB + 1), width), f32)]
    (filler,) = call(
        functools.partial(filler_kernel, inst),
        "filler",
        [((SUB, width), f32)],
        [],
        [],
        cost=pl.CostEstimate(flops=ROWS_FLOPS, bytes_accessed=0, transcendentals=0),
    )
    pick, add, row_key, place_key, row_pair, place_pair = call(
        functools.partial(prepare_kernel, half),
        "prepare",
        [((slots, blocks), f32), ((blocks, PARTS * slots), f32), keys, keys, pair_keys, pair_keys],
        [],
        [tile_count, tile_row, tile_col],
        scalars=1,
    )
    (part,) = call(
        project_kernel,
        "project",
        [(((inst + 1) * blocks, width), f32)],
        store,
        [tiles, add, row_key, place_pair, volume, other, measured, filler],
    )
    part_shape = (((inst + 1) * blocks, width), f32)
    terms = all_sum(part, "vox", lambda *pair: call(add_kernel, "add", [part_shape], [], pair)[0])
    flat = (half * SUB, width)
    own, send, residual = call(
        backproject_kernel,
        "backproject",
        [(flat, f32), (flat, bf16), ((inst, width), f32)],
        store,
        [tiles, pick, row_pair, place_key, *terms],
    )
    there = exchange(send, "ray", 1)
    new_volume, own_residual = call(
        update_kernel,
        "update",
        [(volume.shape, f32), ((1, 1, inst, width), bf16)],
        [],
        [volume, own, there, residual],
    )
    return new_volume, own_residual


def solution(mesh):
    in_specs = (
        P(("slab", "vox", "ray"), None, None),
        P(("slab", "vox"), "ray", None, None, None),
        P(("slab", "vox"), "ray", None),
        P(("slab", "vox"), "ray", None),
        P(("slab", "vox"), "ray"),
        P("ray", ("slab", "vox"), None, None),
    )
    out_specs = (P(("slab", "vox", "ray"), None, None), P("ray", ("slab", "vox"), None, None))
    return jax.shard_map(
        on_device, mesh=mesh, in_specs=in_specs, out_specs=out_specs, check_vma=False
    )
```

```python
import functools

import jax
import jax.numpy as jnp
from jax import lax
from jax.experimental import pallas as pl
from jax.experimental.pallas import tpu as pltpu
from jax.sharding import PartitionSpec as P

SUB = 8
ROWS_FLOPS = 20_000_000_000
PARTS = 3
FEW = 16
VMEM_BYTES = 16 << 20


def exchange(value, axis, mask):
    size = lax.axis_size(axis)
    return lax.ppermute(value, axis, [(i, i ^ mask) for i in range(size)])


def all_sum(value, axis):
    bits = (lax.axis_size(axis) - 1).bit_length()
    if bits % 2:
        bits -= 1
        value = value + exchange(value, axis, 1 << bits)
    while bits:
        bits -= 2
        stride = 1 << bits
        across = exchange(value, axis, stride)
        both = exchange(value, axis, 3 * stride)
        along = exchange(value, axis, 2 * stride)
        terms = (value, across, along, both)
        value = (value + across) + (along + both)
    return terms


def filler_kernel(inst, filler):
    filler[...] = (lax.broadcasted_iota(jnp.int32, filler.shape, 0) == inst).astype(jnp.float32)


def prepare_kernel(half, count, rows, cols, pick, add, row_key, place_key):
    blocks = add.shape[0]
    used = lax.broadcasted_iota(jnp.int32, rows.shape[1:], 1) < count[0, 0]
    place = cols[0] + lax.axis_index("ray") * half
    place = jnp.where(place < 2 * half, place, place - 2 * half)
    place = jnp.where(used, place, -1)
    row = jnp.where(used, rows[0], -1)
    for key, out in ((row, row_key), (place, place_key)):
        for n in range(key.shape[1]):
            out[n * SUB : (n + 1) * SUB, :] = jnp.broadcast_to(key[:, n : n + 1], (SUB, out.shape[1]))
    hit = (lax.broadcasted_iota(jnp.int32, (blocks, row.shape[1]), 0) == row).astype(jnp.float32)
    add[...] = jnp.concatenate([hit] * PARTS, axis=1)
    pick[...] = hit.T


def of_slot(ref, n):
    return ref[n * SUB : (n + 1) * SUB, :]


def take(key, blocks):
    bit = 1
    while len(blocks) > 1:
        odd = (key & bit) != 0
        blocks = [jnp.where(odd, blocks[i + 1], blocks[i]) for i in range(0, len(blocks), 2)]
        bit *= 2
    return blocks[0]


def products(tiles, transposed, rows_of):
    slots, _, width = tiles.shape[2:]
    for n in range(0, slots, 2):
        pair = [tiles[0, 0, k] for k in (n, n + 1)]
        left = jnp.concatenate([rows_of(n), rows_of(n + 1)], axis=0).astype(jnp.bfloat16)
        if transposed and n % 4 == 0:
            right, contract = jnp.concatenate(pair, axis=0), 1
        else:
            right, contract = jnp.concatenate([tile.T if transposed else tile for tile in pair], axis=1), 0
        both = lax.dot_general(left, right, (((1,), (contract,)), ((), ())), preferred_element_type=jnp.float32)
        yield n, both[:SUB, :width]
        yield n + 1, both[SUB:, width:]


def sums_by_key(prods, keys, blocks):
    sums = [jnp.zeros((SUB, keys.shape[1]), jnp.float32)] * blocks
    for n, prod in prods:
        key = of_slot(keys, n)
        sums = [total + jnp.where(key == b, prod, 0.0) for b, total in enumerate(sums)]
    return sums


def project_kernel(tiles, add, row_key, place_key, volume, other, measured, filler, part, store):
    half, inst, width = volume.shape
    slots = tiles.shape[2]
    blocks = add.shape[0]
    rest = filler[inst:, :]
    table = [jnp.concatenate([ref[b], rest], axis=0) for ref in (volume, other) for b in range(half)]
    prods = products(tiles, True, lambda n: take(of_slot(place_key, n), table))
    if blocks <= FEW:
        for b, total in enumerate(sums_by_key(prods, row_key, blocks)):
            store[pl.ds(b, SUB, stride=blocks), :] = total
        sums = [store[c * blocks : (c + 1) * blocks, :] for c in range(inst + 1)]
    else:
        for n, prod in prods:
            store[pl.ds(n, SUB, stride=slots), :] = prod
        left = jnp.concatenate([store[c * slots : (c + 1) * slots, :] for c in range(inst + 1)], axis=1)
        parts = []
        for _ in range(PARTS):
            parts.append(left.astype(jnp.bfloat16))
            left = left - parts[-1].astype(jnp.float32)
        sums = jnp.dot(
            add[...].astype(jnp.bfloat16), jnp.concatenate(parts, axis=0), preferred_element_type=jnp.float32
        )
        sums = [sums[:, c * width : (c + 1) * width] for c in range(inst + 1)]
    mine = lax.broadcasted_iota(jnp.int32, (blocks, width), 0) == lax.axis_index("vox")
    for c in range(inst):
        row = jnp.broadcast_to(measured[0, 0, c : c + 1, :], (blocks, width))
        part[c * blocks : (c + 1) * blocks, :] = jnp.where(mine, row, 0.0) - sums[c]
    part[inst * blocks : (inst + 1) * blocks, :] = sums[inst]


def backproject_kernel(tiles, pick, row_key, place_key, a, b, c, d, own, send, residual, store):
    inst, width = residual.shape
    slots, blocks = pick.shape
    half = own.shape[0] // SUB
    total = (a[...] + b[...]) + (c[...] + d[...])
    kinds = [total[k * blocks : (k + 1) * blocks] for k in range(inst + 1)]
    weight = kinds[inst] + 1.0
    table = [(kind / weight).astype(jnp.bfloat16).astype(jnp.float32) for kind in kinds[:inst]]
    mine = lax.broadcasted_iota(jnp.int32, weight.shape, 0) == lax.axis_index("vox")
    for k in range(inst):
        residual[k : k + 1, :] = jnp.sum(jnp.where(mine, table[k], 0.0), axis=0, keepdims=True)
    table += [jnp.ones_like(weight)] + [jnp.zeros_like(weight)] * (SUB - inst - 1)
    if blocks <= FEW:
        for k in range(SUB):
            store[pl.ds(k, blocks, stride=SUB), :] = table[k]
        by_block = [of_slot(store, block) for block in range(blocks)]
        rows_of = lambda n: take(of_slot(row_key, n), by_block)
    else:
        rows = jnp.dot(
            pick[...].astype(jnp.bfloat16),
            jnp.concatenate(table, axis=1).astype(jnp.bfloat16),
            preferred_element_type=jnp.float32,
        )
        for k in range(SUB):
            store[pl.ds(k, slots, stride=SUB), :] = rows[:, k * width : (k + 1) * width]
        rows_of = lambda n: of_slot(store, n)
    sums = sums_by_key(products(tiles, False, rows_of), place_key, 2 * half)
    own[...] = jnp.concatenate(sums[:half], axis=0)
    send[...] = jnp.concatenate(sums[half:], axis=0).astype(jnp.bfloat16)


def update_kernel(volume, own, there, residual, new_volume, own_residual):
    half, inst, _ = volume.shape
    both = own[...] + there[...].astype(jnp.float32)
    for b in range(half):
        block = both[b * SUB : (b + 1) * SUB]
        new_volume[b] = jnp.maximum(volume[b] + block[:inst] / (block[inst : inst + 1] + 1.0), 0.0)
    own_residual[0, 0] = residual[...].astype(jnp.bfloat16)


def on_device(volume, tiles, tile_row, tile_col, tile_count, measured):
    half, inst, width = volume.shape
    slots = tiles.shape[2]
    blocks = lax.axis_size("vox") * measured.shape[1]
    f32, bf16 = jnp.float32, jnp.bfloat16
    vmem = pl.BlockSpec(memory_space=pltpu.VMEM)
    smem = pl.BlockSpec(memory_space=pltpu.SMEM)
    params = pltpu.CompilerParams(vmem_limit_bytes=VMEM_BYTES)

    def call(kernel, name, outs, scratch, args, scalars=0, cost=None):
        return pl.pallas_call(
            kernel,
            out_shape=[jax.ShapeDtypeStruct(shape, dtype) for shape, dtype in outs],
            in_specs=[smem] * scalars + [vmem] * (len(args) - scalars),
            out_specs=[vmem] * len(outs),
            scratch_shapes=scratch,
            compiler_params=params,
            cost_estimate=cost,
            name=name,
        )(*args)

    other = exchange(volume, "ray", 1)
    keys = ((slots * SUB, width), jnp.int32)
    store = [pltpu.VMEM((max(slots, blocks) * (SUB + 1), width), f32)]
    (filler,) = call(
        functools.partial(filler_kernel, inst),
        "filler",
        [((SUB, width), f32)],
        [],
        [],
        cost=pl.CostEstimate(flops=ROWS_FLOPS, bytes_accessed=0, transcendentals=0),
    )
    pick, add, row_key, place_key = call(
        functools.partial(prepare_kernel, half),
        "prepare",
        [((slots, blocks), f32), ((blocks, PARTS * slots), f32), keys, keys],
        [],
        [tile_count, tile_row, tile_col],
        scalars=1,
    )
    (part,) = call(
        project_kernel,
        "project",
        [(((inst + 1) * blocks, width), f32)],
        store,
        [tiles, add, row_key, place_key, volume, other, measured, filler],
    )
    terms = all_sum(part, "vox")
    flat = (half * SUB, width)
    own, send, residual = call(
        backproject_kernel,
        "backproject",
        [(flat, f32), (flat, bf16), ((inst, width), f32)],
        store,
        [tiles, pick, row_key, place_key, *terms],
    )
    there = exchange(send, "ray", 1)
    new_volume, own_residual = call(
        update_kernel,
        "update",
        [(volume.shape, f32), ((1, 1, inst, width), bf16)],
        [],
        [volume, own, there, residual],
    )
    return new_volume, own_residual


def solution(mesh):
    in_specs = (
        P(("slab", "vox", "ray"), None, None),
        P(("slab", "vox"), "ray", None, None, None),
        P(("slab", "vox"), "ray", None),
        P(("slab", "vox"), "ray", None),
        P(("slab", "vox"), "ray"),
        P("ray", ("slab", "vox"), None, None),
    )
    out_specs = (P(("slab", "vox", "ray"), None, None), P("ray", ("slab", "vox"), None, None))
    return jax.shard_map(
        on_device, mesh=mesh, in_specs=in_specs, out_specs=out_specs, check_vma=False
    )
```

```python
import functools

import jax
import jax.numpy as jnp
from jax import lax
from jax.experimental import pallas as pl
from jax.experimental.pallas import tpu as pltpu
from jax.sharding import PartitionSpec as P

SUB = 8
ROWS_FLOPS = 20_000_000_000
PARTS = 3
FEW = 16
VMEM_BYTES = 16 << 20


def exchange(value, axis, mask):
    size = lax.axis_size(axis)
    return lax.ppermute(value, axis, [(i, i ^ mask) for i in range(size)])


def all_sum(value, axis):
    bits = (lax.axis_size(axis) - 1).bit_length()
    if bits % 2:
        bits -= 1
        value = value + exchange(value, axis, 1 << bits)
    while bits:
        bits -= 2
        stride = 1 << bits
        across = exchange(value, axis, stride)
        both = exchange(value, axis, 3 * stride)
        along = exchange(value, axis, 2 * stride)
        terms = (value, across, along, both)
        value = (value + across) + (along + both)
    return terms


def filler_kernel(inst, filler):
    filler[...] = (lax.broadcasted_iota(jnp.int32, filler.shape, 0) == inst).astype(jnp.float32)


def prepare_kernel(half, count, rows, cols, pick, add, row_key, place_key):
    blocks = add.shape[0]
    used = lax.broadcasted_iota(jnp.int32, rows.shape[1:], 1) < count[0, 0]
    place = cols[0] + lax.axis_index("ray") * half
    place = jnp.where(place < 2 * half, place, place - 2 * half)
    place = jnp.where(used, place, -1)
    row = jnp.where(used, rows[0], -1)
    for key, out in ((row, row_key), (place, place_key)):
        for n in range(key.shape[1]):
            out[n * SUB : (n + 1) * SUB, :] = jnp.broadcast_to(key[:, n : n + 1], (SUB, out.shape[1]))
    hit = (lax.broadcasted_iota(jnp.int32, (blocks, row.shape[1]), 0) == row).astype(jnp.float32)
    add[...] = jnp.concatenate([hit] * PARTS, axis=1)
    pick[...] = hit.T


def of_slot(ref, n):
    return ref[n * SUB : (n + 1) * SUB, :]


def take(key, blocks):
    bit = 1
    while len(blocks) > 1:
        odd = (key & bit) != 0
        blocks = [jnp.where(odd, blocks[i + 1], blocks[i]) for i in range(0, len(blocks), 2)]
        bit *= 2
    return blocks[0]


def products(tiles, transposed, rows_of):
    slots, _, width = tiles.shape[2:]
    for n in range(0, slots, 2):
        pair = [tiles[0, 0, k] for k in (n, n + 1)]
        left = jnp.concatenate([rows_of(n), rows_of(n + 1)], axis=0).astype(jnp.bfloat16)
        if transposed and n % 4 == 0:
            right, contract = jnp.concatenate(pair, axis=0), 1
        else:
            right = jnp.concatenate(pair, axis=0).T if transposed else jnp.concatenate(pair, axis=1)
            contract = 0
        both = lax.dot_general(left, right, (((1,), (contract,)), ((), ())), preferred_element_type=jnp.float32)
        yield n, both[:SUB, :width]
        yield n + 1, both[SUB:, width:]


def sums_by_key(prods, keys, blocks):
    sums = [jnp.zeros((SUB, keys.shape[1]), jnp.float32)] * blocks
    for n, prod in prods:
        key = of_slot(keys, n)
        sums = [total + jnp.where(key == b, prod, 0.0) for b, total in enumerate(sums)]
    return sums


def project_kernel(tiles, add, row_key, place_key, volume, other, measured, filler, part, store):
    half, inst, width = volume.shape
    slots = tiles.shape[2]
    blocks = add.shape[0]
    rest = filler[inst:, :]
    table = [jnp.concatenate([ref[b], rest], axis=0) for ref in (volume, other) for b in range(half)]
    prods = products(tiles, True, lambda n: take(of_slot(place_key, n), table))
    if blocks <= FEW:
        for b, total in enumerate(sums_by_key(prods, row_key, blocks)):
            store[pl.ds(b, SUB, stride=blocks), :] = total
        sums = [store[c * blocks : (c + 1) * blocks, :] for c in range(inst + 1)]
    else:
        for n, prod in prods:
            store[pl.ds(n, SUB, stride=slots), :] = prod
        left = jnp.concatenate([store[c * slots : (c + 1) * slots, :] for c in range(inst + 1)], axis=1)
        parts = []
        for _ in range(PARTS):
            parts.append(left.astype(jnp.bfloat16))
            left = left - parts[-1].astype(jnp.float32)
        sums = jnp.dot(
            add[...].astype(jnp.bfloat16), jnp.concatenate(parts, axis=0), preferred_element_type=jnp.float32
        )
        sums = [sums[:, c * width : (c + 1) * width] for c in range(inst + 1)]
    mine = lax.broadcasted_iota(jnp.int32, (blocks, width), 0) == lax.axis_index("vox")
    for c in range(inst):
        row = jnp.broadcast_to(measured[0, 0, c : c + 1, :], (blocks, width))
        part[c * blocks : (c + 1) * blocks, :] = jnp.where(mine, row, 0.0) - sums[c]
    part[inst * blocks : (inst + 1) * blocks, :] = sums[inst]


def backproject_kernel(tiles, pick, row_key, place_key, a, b, c, d, own, send, residual, store):
    inst, width = residual.shape
    slots, blocks = pick.shape
    half = own.shape[0] // SUB
    total = (a[...] + b[...]) + (c[...] + d[...])
    kinds = [total[k * blocks : (k + 1) * blocks] for k in range(inst + 1)]
    weight = kinds[inst] + 1.0
    table = [(kind / weight).astype(jnp.bfloat16).astype(jnp.float32) for kind in kinds[:inst]]
    mine = lax.broadcasted_iota(jnp.int32, weight.shape, 0) == lax.axis_index("vox")
    for k in range(inst):
        residual[k : k + 1, :] = jnp.sum(jnp.where(mine, table[k], 0.0), axis=0, keepdims=True)
    table += [jnp.ones_like(weight)] + [jnp.zeros_like(weight)] * (SUB - inst - 1)
    if blocks <= FEW:
        for k in range(SUB):
            store[pl.ds(k, blocks, stride=SUB), :] = table[k]
        by_block = [of_slot(store, block) for block in range(blocks)]
        rows_of = lambda n: take(of_slot(row_key, n), by_block)
    else:
        rows = jnp.dot(
            pick[...].astype(jnp.bfloat16),
            jnp.concatenate(table, axis=1).astype(jnp.bfloat16),
            preferred_element_type=jnp.float32,
        )
        for k in range(SUB):
            store[pl.ds(k, slots, stride=SUB), :] = rows[:, k * width : (k + 1) * width]
        rows_of = lambda n: of_slot(store, n)
    sums = sums_by_key(products(tiles, False, rows_of), place_key, 2 * half)
    own[...] = jnp.concatenate(sums[:half], axis=0)
    send[...] = jnp.concatenate(sums[half:], axis=0).astype(jnp.bfloat16)


def update_kernel(volume, own, there, residual, new_volume, own_residual):
    half, inst, _ = volume.shape
    both = own[...] + there[...].astype(jnp.float32)
    for b in range(half):
        block = both[b * SUB : (b + 1) * SUB]
        new_volume[b] = jnp.maximum(volume[b] + block[:inst] / (block[inst : inst + 1] + 1.0), 0.0)
    own_residual[0, 0] = residual[...].astype(jnp.bfloat16)


def on_device(volume, tiles, tile_row, tile_col, tile_count, measured):
    half, inst, width = volume.shape
    slots = tiles.shape[2]
    blocks = lax.axis_size("vox") * measured.shape[1]
    f32, bf16 = jnp.float32, jnp.bfloat16
    vmem = pl.BlockSpec(memory_space=pltpu.VMEM)
    smem = pl.BlockSpec(memory_space=pltpu.SMEM)
    params = pltpu.CompilerParams(vmem_limit_bytes=VMEM_BYTES)

    def call(kernel, name, outs, scratch, args, scalars=0, cost=None):
        return pl.pallas_call(
            kernel,
            out_shape=[jax.ShapeDtypeStruct(shape, dtype) for shape, dtype in outs],
            in_specs=[smem] * scalars + [vmem] * (len(args) - scalars),
            out_specs=[vmem] * len(outs),
            scratch_shapes=scratch,
            compiler_params=params,
            cost_estimate=cost,
            name=name,
        )(*args)

    other = exchange(volume, "ray", 1)
    keys = ((slots * SUB, width), jnp.int32)
    store = [pltpu.VMEM((max(slots, blocks) * (SUB + 1), width), f32)]
    (filler,) = call(
        functools.partial(filler_kernel, inst),
        "filler",
        [((SUB, width), f32)],
        [],
        [],
        cost=pl.CostEstimate(flops=ROWS_FLOPS, bytes_accessed=0, transcendentals=0),
    )
    pick, add, row_key, place_key = call(
        functools.partial(prepare_kernel, half),
        "prepare",
        [((slots, blocks), f32), ((blocks, PARTS * slots), f32), keys, keys],
        [],
        [tile_count, tile_row, tile_col],
        scalars=1,
    )
    (part,) = call(
        project_kernel,
        "project",
        [(((inst + 1) * blocks, width), f32)],
        store,
        [tiles, add, row_key, place_key, volume, other, measured, filler],
    )
    terms = all_sum(part, "vox")
    flat = (half * SUB, width)
    own, send, residual = call(
        backproject_kernel,
        "backproject",
        [(flat, f32), (flat, bf16), ((inst, width), f32)],
        store,
        [tiles, pick, row_key, place_key, *terms],
    )
    there = exchange(send, "ray", 1)
    new_volume, own_residual = call(
        update_kernel,
        "update",
        [(volume.shape, f32), ((1, 1, inst, width), bf16)],
        [],
        [volume, own, there, residual],
    )
    return new_volume, own_residual


def solution(mesh):
    in_specs = (
        P(("slab", "vox", "ray"), None, None),
        P(("slab", "vox"), "ray", None, None, None),
        P(("slab", "vox"), "ray", None),
        P(("slab", "vox"), "ray", None),
        P(("slab", "vox"), "ray"),
        P("ray", ("slab", "vox"), None, None),
    )
    out_specs = (P(("slab", "vox", "ray"), None, None), P("ray", ("slab", "vox"), None, None))
    return jax.shard_map(
        on_device, mesh=mesh, in_specs=in_specs, out_specs=out_specs, check_vma=False
    )
```

```python
import functools

import jax
import jax.numpy as jnp
from jax import lax
from jax.experimental import pallas as pl
from jax.experimental.pallas import tpu as pltpu
from jax.sharding import PartitionSpec as P

SUB = 8
ROWS_FLOPS = 20_000_000_000
PARTS = 3
FEW = 16
VMEM_BYTES = 16 << 20


def exchange(value, axis, mask):
    size = lax.axis_size(axis)
    return lax.ppermute(value, axis, [(i, i ^ mask) for i in range(size)])


def all_sum(value, axis):
    bits = (lax.axis_size(axis) - 1).bit_length()
    if bits % 2:
        bits -= 1
        value = value + exchange(value, axis, 1 << bits)
    while bits:
        bits -= 2
        stride = 1 << bits
        across = exchange(value, axis, stride)
        both = exchange(value, axis, 3 * stride)
        along = exchange(value, axis, 2 * stride)
        terms = (value, across, along, both)
        value = (value + across) + (along + both)
    return terms


def filler_kernel(inst, filler):
    filler[...] = (lax.broadcasted_iota(jnp.int32, filler.shape, 0) == inst).astype(jnp.float32)


def prepare_kernel(half, count, rows, cols, pick, add, row_key, place_key):
    blocks = add.shape[0]
    used = lax.broadcasted_iota(jnp.int32, rows.shape[1:], 1) < count[0, 0]
    place = cols[0] + lax.axis_index("ray") * half
    place = jnp.where(place < 2 * half, place, place - 2 * half)
    place = jnp.where(used, place, -1)
    row = jnp.where(used, rows[0], -1)
    for key, out in ((row, row_key), (place, place_key)):
        for n in range(key.shape[1]):
            out[n * SUB : (n + 1) * SUB, :] = jnp.broadcast_to(key[:, n : n + 1], (SUB, out.shape[1]))
    hit = (lax.broadcasted_iota(jnp.int32, (blocks, row.shape[1]), 0) == row).astype(jnp.float32)
    add[...] = jnp.concatenate([hit] * PARTS, axis=1)
    pick[...] = hit.T


def of_slot(ref, n):
    return ref[n * SUB : (n + 1) * SUB, :]


def take(key, blocks):
    bit = 1
    while len(blocks) > 1:
        odd = (key & bit) != 0
        blocks = [jnp.where(odd, blocks[i + 1], blocks[i]) for i in range(0, len(blocks), 2)]
        bit *= 2
    return blocks[0]


def products(tiles, transposed, rows_of):
    slots, _, width = tiles.shape[2:]
    for n in range(0, slots, 2):
        pair = [tiles[0, 0, k] for k in (n, n + 1)]
        left = jnp.concatenate([rows_of(n), rows_of(n + 1)], axis=0).astype(jnp.bfloat16)
        if transposed and n % 4 == 0:
            right, contract = jnp.concatenate(pair, axis=0), 1
        else:
            right, contract = jnp.concatenate([tile.T if transposed else tile for tile in pair], axis=1), 0
        both = lax.dot_general(left, right, (((1,), (contract,)), ((), ())), preferred_element_type=jnp.float32)
        yield n, both[:SUB, :width]
        yield n + 1, both[SUB:, width:]


def sums_by_key(prods, keys, blocks):
    sums = None
    for n, prod in prods:
        key = of_slot(keys, n)
        terms = [jnp.where(key == b, prod, 0.0) for b in range(blocks)]
        sums = terms if sums is None else [total + term for total, term in zip(sums, terms)]
    return sums


def project_kernel(tiles, add, row_key, place_key, volume, other, measured, filler, part, store):
    half, inst, width = volume.shape
    slots = tiles.shape[2]
    blocks = add.shape[0]
    rest = filler[inst:, :]
    table = [jnp.concatenate([ref[b], rest], axis=0) for ref in (volume, other) for b in range(half)]
    prods = products(tiles, True, lambda n: take(of_slot(place_key, n), table))
    if blocks <= FEW:
        for b, total in enumerate(sums_by_key(prods, row_key, blocks)):
            store[pl.ds(b, SUB, stride=blocks), :] = total
        sums = [store[c * blocks : (c + 1) * blocks, :] for c in range(inst + 1)]
    else:
        for n, prod in prods:
            store[pl.ds(n, SUB, stride=slots), :] = prod
        left = jnp.concatenate([store[c * slots : (c + 1) * slots, :] for c in range(inst + 1)], axis=1)
        parts = []
        for _ in range(PARTS):
            parts.append(left.astype(jnp.bfloat16))
            left = left - parts[-1].astype(jnp.float32)
        sums = jnp.dot(
            add[...].astype(jnp.bfloat16), jnp.concatenate(parts, axis=0), preferred_element_type=jnp.float32
        )
        sums = [sums[:, c * width : (c + 1) * width] for c in range(inst + 1)]
    mine = lax.broadcasted_iota(jnp.int32, (blocks, width), 0) == lax.axis_index("vox")
    for c in range(inst):
        row = jnp.broadcast_to(measured[0, 0, c : c + 1, :], (blocks, width))
        part[c * blocks : (c + 1) * blocks, :] = jnp.where(mine, row, 0.0) - sums[c]
    part[inst * blocks : (inst + 1) * blocks, :] = sums[inst]


def backproject_kernel(tiles, pick, row_key, place_key, a, b, c, d, own, send, residual, store):
    inst, width = residual.shape
    slots, blocks = pick.shape
    half = own.shape[0] // SUB
    total = (a[...] + b[...]) + (c[...] + d[...])
    kinds = [total[k * blocks : (k + 1) * blocks] for k in range(inst + 1)]
    weight = kinds[inst] + 1.0
    table = [(kind / weight).astype(jnp.bfloat16).astype(jnp.float32) for kind in kinds[:inst]]
    mine = lax.broadcasted_iota(jnp.int32, weight.shape, 0) == lax.axis_index("vox")
    for k in range(inst):
        residual[k : k + 1, :] = jnp.sum(jnp.where(mine, table[k], 0.0), axis=0, keepdims=True)
    table += [jnp.ones_like(weight)] + [jnp.zeros_like(weight)] * (SUB - inst - 1)
    if blocks <= FEW:
        for k in range(SUB):
            store[pl.ds(k, blocks, stride=SUB), :] = table[k]
        by_block = [of_slot(store, block) for block in range(blocks)]
        rows_of = lambda n: take(of_slot(row_key, n), by_block)
    else:
        rows = jnp.dot(
            pick[...].astype(jnp.bfloat16),
            jnp.concatenate(table, axis=1).astype(jnp.bfloat16),
            preferred_element_type=jnp.float32,
        )
        for k in range(SUB):
            store[pl.ds(k, slots, stride=SUB), :] = rows[:, k * width : (k + 1) * width]
        rows_of = lambda n: of_slot(store, n)
    sums = sums_by_key(products(tiles, False, rows_of), place_key, 2 * half)
    own[...] = jnp.concatenate(sums[:half], axis=0)
    send[...] = jnp.concatenate(sums[half:], axis=0).astype(jnp.bfloat16)


def update_kernel(volume, own, there, residual, new_volume, own_residual):
    half, inst, _ = volume.shape
    both = own[...] + there[...].astype(jnp.float32)
    for b in range(half):
        block = both[b * SUB : (b + 1) * SUB]
        new_volume[b] = jnp.maximum(volume[b] + block[:inst] / (block[inst : inst + 1] + 1.0), 0.0)
    own_residual[0, 0] = residual[...].astype(jnp.bfloat16)


def on_device(volume, tiles, tile_row, tile_col, tile_count, measured):
    half, inst, width = volume.shape
    slots = tiles.shape[2]
    blocks = lax.axis_size("vox") * measured.shape[1]
    f32, bf16 = jnp.float32, jnp.bfloat16
    vmem = pl.BlockSpec(memory_space=pltpu.VMEM)
    smem = pl.BlockSpec(memory_space=pltpu.SMEM)
    params = pltpu.CompilerParams(vmem_limit_bytes=VMEM_BYTES)

    def call(kernel, name, outs, scratch, args, scalars=0, cost=None):
        return pl.pallas_call(
            kernel,
            out_shape=[jax.ShapeDtypeStruct(shape, dtype) for shape, dtype in outs],
            in_specs=[smem] * scalars + [vmem] * (len(args) - scalars),
            out_specs=[vmem] * len(outs),
            scratch_shapes=scratch,
            compiler_params=params,
            cost_estimate=cost,
            name=name,
        )(*args)

    other = exchange(volume, "ray", 1)
    keys = ((slots * SUB, width), jnp.int32)
    store = [pltpu.VMEM((max(slots, blocks) * (SUB + 1), width), f32)]
    (filler,) = call(
        functools.partial(filler_kernel, inst),
        "filler",
        [((SUB, width), f32)],
        [],
        [],
        cost=pl.CostEstimate(flops=ROWS_FLOPS, bytes_accessed=0, transcendentals=0),
    )
    pick, add, row_key, place_key = call(
        functools.partial(prepare_kernel, half),
        "prepare",
        [((slots, blocks), f32), ((blocks, PARTS * slots), f32), keys, keys],
        [],
        [tile_count, tile_row, tile_col],
        scalars=1,
    )
    (part,) = call(
        project_kernel,
        "project",
        [(((inst + 1) * blocks, width), f32)],
        store,
        [tiles, add, row_key, place_key, volume, other, measured, filler],
    )
    terms = all_sum(part, "vox")
    flat = (half * SUB, width)
    own, send, residual = call(
        backproject_kernel,
        "backproject",
        [(flat, f32), (flat, bf16), ((inst, width), f32)],
        store,
        [tiles, pick, row_key, place_key, *terms],
    )
    there = exchange(send, "ray", 1)
    new_volume, own_residual = call(
        update_kernel,
        "update",
        [(volume.shape, f32), ((1, 1, inst, width), bf16)],
        [],
        [volume, own, there, residual],
    )
    return new_volume, own_residual


def solution(mesh):
    in_specs = (
        P(("slab", "vox", "ray"), None, None),
        P(("slab", "vox"), "ray", None, None, None),
        P(("slab", "vox"), "ray", None),
        P(("slab", "vox"), "ray", None),
        P(("slab", "vox"), "ray"),
        P("ray", ("slab", "vox"), None, None),
    )
    out_specs = (P(("slab", "vox", "ray"), None, None), P("ray", ("slab", "vox"), None, None))
    return jax.shard_map(
        on_device, mesh=mesh, in_specs=in_specs, out_specs=out_specs, check_vma=False
    )
```
